128 devices in a mesh: region: 4 (over y_hi, core), tile: 32 (over x, z, y_lo).
Axes of the slice: x: 4, y: 4 (y_hi: 2, y_lo: 2; y = y_hi * 2 + y_lo), z: 4, core: 2. Of those that a mesh axis runs over, the one named last changes fastest.
Arguments:
- fields: float32 [9, 32, 64, 4096], P(None, None, 'region', 'tile'), may hold values from -6 to 6
- buoyancy: float32 [32, 64, 4096], P(None, 'region', 'tile'), may hold values from 0.5 to 1.5
- lame_first: float32 [32, 64, 4096], P(None, 'region', 'tile'), may hold values from 0.5 to 2
- shear_modulus: float32 [32, 64, 4096], P(None, 'region', 'tile'), may hold values from 0.3 to 1.5
- observed: float32 [3, 4096], P(None, ('region', 'tile')), may hold values from -6 to 6
- station_weight: float32 [4096], P(('region', 'tile')), may hold values from 0.2 to 2
- depth_profile: float32 [3, 32], replicated, may hold values from 0.1 to 1
- station_cell: int32 [4096], P(('region', 'tile')), may hold values from 0 to 2047
- station_count: int32 [128], P(('region', 'tile')), may hold values from 1 to 32, as said below
- influence: int32 [128, 64], P(('region', 'tile')), may hold values from 0 to 4095, as said below
- influence_count: int32 [128], P(('region', 'tile')), may hold values from 1 to 64, as said below
Outputs:
- analysis: float32 [9, 32, 64, 4096], P(None, None, 'region', 'tile')
The draws below stay inside these ranges and needn't reach their ends.
Inputs may be any that keep to these rules, and one draw needn't show every extreme that they name: Slots k < station_count[g] of tile g are live; the others are empty and ignored. `influence`: row g holds 64 distinct slot numbers; the tile s // 32 of each lies at a region index and a tile index that each differ from those of tile g by at most one, without wrapping. Only the first influence_count[g] entries of row g of influence are used.
All inputs are finite; a program needn't handle non-finite values.
Results may differ from the reference program's by a relative error of at most 0.0003.
Values sent between devices are 32-bit elements; how exact they have to be, the bound alone decides.
No kernel may reach another device: no remote copies, remote signals or barrier semaphores. Data moves between devices by JAX's collectives and lax.ppermute only.
A program may use at most 128 MiB of HBM per device.

```python
import math
import jax
import jax.numpy as jnp
from jax import lax

CX = 16
CY = 128
NZ = 32
ITERS = 4
S = 32
LIST = 64
NX = 64
NY = 4096
TILES = 128
SLOTS = 4096
N_REGION = 4
N_TILE = 32


def draw_station_count(key, part):
    key = jax.random.fold_in(key, 11)
    key_base, key_pick, key_load = jax.random.split(key, 3)
    base_load = jax.random.randint(key_base, (TILES,), max(1, S // 4), S // 2 + 1, dtype=jnp.int32)
    crowded = jax.random.permutation(key_pick, TILES)[:3]
    heavy_load = jax.random.randint(key_load, (3,), S // 2, S + 1, dtype=jnp.int32)
    heavy_load = heavy_load.at[0].set(S)
    return base_load.at[crowded].set(heavy_load)


def draw_influence(key, part):
    key = jax.random.fold_in(key, 12)
    span_count = 9 * S
    candidate = jnp.arange(span_count, dtype=jnp.int32)
    neighbour = candidate // S
    within = candidate % S
    tile_all = jnp.arange(TILES, dtype=jnp.int32)
    row_of = tile_all // N_TILE
    col_of = tile_all % N_TILE
    near_row = row_of[:, None] + neighbour[None] // 3 - 1
    near_col = col_of[:, None] + neighbour[None] % 3 - 1
    inside = (near_row >= 0) & (near_row < N_REGION) & (near_col >= 0) & (near_col < N_TILE)
    slot_id = (near_row * N_TILE + near_col) * S + within[None]
    scores = jax.random.randint(key, (TILES, span_count), 0, 1 << 20, dtype=jnp.int32) * span_count + candidate[None]
    scores = jnp.where(inside, scores, -1 - candidate[None])
    top_scores, chosen = lax.top_k(scores, LIST)
    return jnp.take_along_axis(slot_id, chosen, axis=1)


def draw_influence_count(key, part):
    key = jax.random.fold_in(key, 13)
    key_base, key_pick = jax.random.split(key)
    counts = jax.random.randint(key_base, (TILES,), 1, LIST + 1, dtype=jnp.int32)
    fullest = jax.random.randint(key_pick, (), 0, TILES, dtype=jnp.int32)
    return counts.at[fullest].set(LIST)


def plant(result, key, least, high):
    place = [jax.random.randint(jax.random.fold_in(key, axis), (), 0, length) for axis, length in enumerate(result.shape)]
    longest = result.shape.index(max(result.shape))
    beside = place[:longest] + [(place[longest] + 1) % result.shape[longest]] + place[longest + 1:]
    return result.at[tuple(place)].set(least).at[tuple(beside)].set(high)


def steps_of(key, shape, shards, least, top_value):
    factor_of, own = 1.0, jax.random.fold_in(key, 6)
    for axis_at, blocks in shards:
        heights = jnp.exp(jax.random.uniform(jax.random.fold_in(own, axis_at), (blocks,), jnp.float32, least / len(shards), top_value / len(shards)))
        factor_of = factor_of * jnp.repeat(heights, shape[axis_at] // blocks).reshape([-1 if axis == axis_at else 1 for axis in range(len(shape))])
    return factor_of


def centred(rng, dims, deviation, bound, shards=(), held_as=jnp.bfloat16):
    drawn = jax.random.normal(rng, dims, jnp.float32) * deviation
    if len(shards) > 0:
        drawn = steps_of(rng, dims, shards, -0.22, 0.18) * drawn
    return jnp.clip(drawn, min=-bound, max=bound).astype(held_as)


def setup_inputs(seed: int = 0) -> dict:
    key_list = jax.random.split(jax.random.key(seed), 12)
    return {
        "fields": centred(key_list[0], (9, NZ, NX, NY), 1.0, 6.0, ((2, 4), (3, 32)), jnp.float32),
        "buoyancy": jnp.clip(jnp.exp(math.log(1.5) - 1.0986123 * jax.random.uniform(key_list[1], (NZ, NX, NY), jnp.float32) ** steps_of(key_list[1], (NZ, NX, NY), ((1, 4), (2, 32)), -0.2, 0.2)), 0.5, 1.5),
        "lame_first": jnp.clip(jnp.exp(math.log(2.0) - 1.3862944 * jax.random.uniform(key_list[2], (NZ, NX, NY), jnp.float32) ** steps_of(key_list[2], (NZ, NX, NY), ((1, 4), (2, 32)), -0.2, 0.2)), 0.5, 2.0),
        "shear_modulus": jnp.clip(jnp.exp(math.log(1.5) - 1.60943787 * jax.random.uniform(key_list[3], (NZ, NX, NY), jnp.float32) ** steps_of(key_list[3], (NZ, NX, NY), ((1, 4), (2, 32)), -0.2, 0.2)), 0.3, 1.5),
        "observed": centred(key_list[4], (3, SLOTS), 1.0, 6.0, ((1, 128),), jnp.float32),
        "station_weight": jnp.clip(jnp.exp(math.log(2.0) - 2.3025851 * jax.random.uniform(key_list[5], (SLOTS,), jnp.float32) ** steps_of(key_list[5], (SLOTS,), ((0, 128),), -0.2, 0.2)), 0.2, 2.0),
        "depth_profile": jnp.clip(jnp.exp(jax.random.uniform(key_list[6], (3, NZ), jnp.float32, math.log(0.1), math.log(1.0))), 0.1, 1.0),
        "station_cell": plant(jax.random.randint(key_list[7], (SLOTS,), 0, CX * CY), jax.random.fold_in(key_list[7], 1), 0, (CX * CY) - 1).astype(jnp.int32),
        "station_count": draw_station_count(jax.random.fold_in(key_list[11], 71), 0),
        "influence": draw_influence(jax.random.fold_in(key_list[11], 71), 0),
        "influence_count": draw_influence_count(jax.random.fold_in(key_list[11], 71), 0),
    }


near_coef = 1.125
far_coef = -1.0 / 24.0
time_step = 0.15


def shifted(field, along, offset, length):
    return lax.slice_in_dim(field, offset, offset + length, axis=along)


def differ(field, along, forward):
    for other_axis in range(3):
        if other_axis != along:
            field = shifted(field, other_axis, 2, field.shape[other_axis] - 4)
    length = field.shape[along] - 4
    if forward:
        near_term = shifted(field, along, 3, length) - shifted(field, along, 2, length)
        far_term = shifted(field, along, 4, length) - shifted(field, along, 1, length)
    else:
        near_term = shifted(field, along, 2, length) - shifted(field, along, 1, length)
        far_term = shifted(field, along, 3, length) - shifted(field, along, 0, length)
    return near_coef * near_term + far_coef * far_term


def move_velocity(velocity, stress, buoyancy):
    force_x = differ(stress[0], 1, True) + differ(stress[3], 2, False) + differ(stress[4], 0, False)
    force_y = differ(stress[3], 1, False) + differ(stress[1], 2, True) + differ(stress[5], 0, False)
    force_z = differ(stress[4], 1, False) + differ(stress[5], 2, False) + differ(stress[2], 0, True)
    factor = time_step * buoyancy
    return velocity + factor[None] * jnp.stack([force_x, force_y, force_z])


def move_stress(stress, velocity, lame_first, shear_modulus):
    grad_x = differ(velocity[0], 1, False)
    grad_y = differ(velocity[1], 2, False)
    grad_z = differ(velocity[2], 0, False)
    modulus = lame_first + 2.0 * shear_modulus
    rates = jnp.stack([
        modulus * grad_x + lame_first * (grad_y + grad_z),
        modulus * grad_y + lame_first * (grad_x + grad_z),
        modulus * grad_z + lame_first * (grad_x + grad_y),
        shear_modulus * (differ(velocity[0], 2, True) + differ(velocity[1], 1, True)),
        shear_modulus * (differ(velocity[0], 0, True) + differ(velocity[2], 1, True)),
        shear_modulus * (differ(velocity[1], 0, True) + differ(velocity[2], 2, True)),
    ])
    return stress + time_step * rates


def pad_all(field):
    return jnp.pad(field, ((0, 0), (2, 2), (2, 2), (2, 2)))


def reference(fields, buoyancy, lame_first, shear_modulus, observed, station_weight, depth_profile, station_cell, station_count, influence, influence_count):
    velocity = fields[:3]
    stress = fields[3:]
    for iteration in range(ITERS):
        velocity = move_velocity(velocity, pad_all(stress), buoyancy)
        stress = move_stress(stress, pad_all(velocity), lame_first, shear_modulus)
    slot_all = jnp.arange(SLOTS, dtype=jnp.int32)
    owner_tile = slot_all // S
    live_slot = (slot_all % S) < station_count[owner_tile]
    station_x = (owner_tile // N_TILE) * CX + station_cell // CY
    station_y = (owner_tile % N_TILE) * CY + station_cell % CY
    sample = velocity[:, 0][:, station_x, station_y]
    weight = jnp.where(live_slot[None], station_weight[None] * (observed - sample), 0.0)
    width_x = 2.0 * (0.5 * CX) ** 2
    width_y = 2.0 * (0.25 * CY) ** 2

    def one_tile(tile_number):
        listed = influence[tile_number]
        used_entry = jnp.arange(LIST, dtype=jnp.int32) < influence_count[tile_number]
        cell_x = (tile_number // N_TILE) * CX + jnp.arange(CX, dtype=jnp.int32)
        cell_y = (tile_number % N_TILE) * CY + jnp.arange(CY, dtype=jnp.int32)
        dist_x = (cell_x[:, None] - station_x[listed][None]).astype(jnp.float32)
        dist_y = (cell_y[:, None] - station_y[listed][None]).astype(jnp.float32)
        along_x = jnp.exp(-(dist_x * dist_x) / width_x)
        along_y = jnp.exp(-(dist_y * dist_y) / width_y)
        scaled = jnp.where(used_entry[None, None], weight[:, listed][:, None, :] * along_x[None], 0.0)
        return jnp.einsum("cxl,yl->cxy", scaled, along_y, precision=lax.Precision.HIGHEST)

    blocks = lax.map(one_tile, jnp.arange(TILES, dtype=jnp.int32))
    increment = blocks.reshape(N_REGION, N_TILE, 3, CX, CY).transpose(2, 0, 3, 1, 4).reshape(3, NX, NY)
    velocity = velocity + depth_profile[:, :, None, None] * increment[:, None]
    return jnp.concatenate([velocity, stress], axis=0)
```

```python
import jax
import jax.numpy as jnp
from jax import lax
from jax.experimental import pallas as pl
from jax.experimental.pallas import tpu as pltpu
from jax.sharding import PartitionSpec as P

ITERS = 4
NEAR = 1.125
FAR = -1.0 / 24.0
DT = 0.15

CX, CY, NZ = 16, 128, 32
S, LIST = 32, 64
GROUPS = 4
WIDE = 16
PACK = NZ // GROUPS
DEPTH = NZ + PACK
LOW = 4
PLANES = LOW + CX + 4
ZROWS = 72

VX, VY, VZ, SXX, SYY, SZZ, SXY, SXZ, SYZ = range(9)
BELOW = [(f, r) for f in (SXX, SXY, SXZ) for r in (-3, -2, -1)] + [
    (SYY, -1), (SYZ, -1), (SZZ, -1), (VX, -2), (VX, -1), (VY, -1), (VZ, -1)]
ABOVE = [(f, r) for f in (SXX, SXY, SXZ) for r in (16, 17, 18)] + [
    (f, r) for f in (SYY, SYZ, SZZ) for r in (16, 17)] + [
    (VX, 16), (VY, 16), (VY, 17), (VZ, 16), (VZ, 17)]
BUOY_ROWS = 2

VMEM_BYTES = 40 * 1024 * 1024


def lanes(rows):
    return lax.broadcasted_iota(jnp.int32, (rows, 128), 1)


def edge_pack(main):
    lane = lanes(PACK)
    out = pltpu.roll(main[0:8], WIDE, 1)
    for g in range(1, GROUPS):
        rolled = pltpu.roll(main[8 * g:8 * g + 8], (WIDE + 32 * g) % 128, 1)
        out = jnp.where(lane >= 32 * g, rolled, out)
    return out


def y_shifts(a, offsets):
    main, halo = a[:NZ], a[NZ:]
    near = [pltpu.roll(halo, (128 - WIDE - 32 * g) % 128, 1) for g in range(GROUPS)]
    other = jnp.concatenate(near + [edge_pack(main)], axis=0)
    lane = lanes(DEPTH)
    is_main = lax.broadcasted_iota(jnp.int32, (DEPTH, 128), 0) < NZ
    spot = jnp.where(is_main, lane, (lane + WIDE) % 32)
    last = jnp.where(is_main, 128, 32)
    out = []
    for o in offsets:
        if o > 0:
            mixed = jnp.where(spot < o, other, a)
        else:
            mixed = jnp.where(spot >= last + o, other, a)
        out.append(pltpu.roll(mixed, (-o) % 128, 1))
    return out


def combine(m1, c0, p1, p2):
    return NEAR * (p1 - c0) + FAR * (p2 - m1)


def load(ref, f, x, dz=0):
    return jnp.concatenate(
        [ref[f, x, 8 + dz:8 + NZ + dz, :], ref[f, x, 56 + dz:64 + dz, :]], axis=0)


def store(ref, f, x, value, z_pads):
    ref[f, x, 8:8 + NZ, :] = value[:NZ]
    halo = value[NZ:]
    ref[f, x, 56:64, :] = halo
    if z_pads:
        lane = lanes(PACK)
        ref[f, x, 48:56, :] = jnp.where(lane < 32, 0.0, pltpu.roll(halo, 32, 1))
        ref[f, x, 64:72, :] = jnp.where(lane >= 96, 0.0, pltpu.roll(halo, 96, 1))


def diff_x(ref, f, x, forward):
    first = -1 if forward else -2
    return combine(*[load(ref, f, x + first + k) for k in range(4)])


def diff_z(ref, f, x, forward):
    first = -1 if forward else -2
    return combine(*[load(ref, f, x, first + k) for k in range(4)])


def diff_y(ref, f, x, forward):
    here = load(ref, f, x)
    if forward:
        m1, p1, p2 = y_shifts(here, (-1, 1, 2))
        return combine(m1, here, p1, p2)
    m2, m1, p1 = y_shifts(here, (-2, -1, 1))
    return combine(m2, m1, here, p1)


Z_PADDED = (VX, VY, VZ, SZZ, SXZ, SYZ)


def fill(x_ref, main_ref, halo_ref, below_ref, above_ref):
    zero = jnp.zeros((8, 128), jnp.float32)

    def zero_pads(x, _):
        for f in Z_PADDED:
            x_ref[f, x, 0:8, :] = zero
            x_ref[f, x, 40:48, :] = zero
        return 0

    lax.fori_loop(0, PLANES, zero_pads, 0)

    def copy_in(x, _):
        for f in range(9):
            value = jnp.concatenate([main_ref[f, x], halo_ref[f, x]], axis=0)
            store(x_ref, f, x + LOW, value, f in Z_PADDED)
        return 0

    lax.fori_loop(0, CX, copy_in, 0)
    for n, (f, r) in enumerate(BELOW):
        store(x_ref, f, r + LOW, below_ref[n], f in Z_PADDED)
    for n, (f, r) in enumerate(ABOVE):
        store(x_ref, f, r + LOW, above_ref[n], f in Z_PADDED)


def param(main_ref, halo_ref, f, x):
    return jnp.concatenate([main_ref[9 + f, x], halo_ref[9 + f, x]], axis=0)


def fill_buoyancy(b_ref, par_main, par_halo, below_first, above_first):
    def copy_in(x, _):
        b_ref[x + BUOY_ROWS] = DT * param(par_main, par_halo, 0, x)
        return 0

    lax.fori_loop(0, CX, copy_in, 0)
    for k in range(BUOY_ROWS):
        b_ref[k] = DT * below_first[len(BELOW) + k]
        b_ref[CX + BUOY_ROWS + k] = DT * above_first[len(ABOVE) + k]


def velocity_pass(x_ref, b_ref):
    def body(j, _):
        x = j - 2 + LOW
        force = (diff_x(x_ref, SXX, x, True) + diff_y(x_ref, SXY, x, False)
                 + diff_z(x_ref, SXZ, x, False))
        store(x_ref, VX, x, load(x_ref, VX, x) + b_ref[j] * force, True)
        x = x + 1
        b = b_ref[j + 1]
        force = (diff_x(x_ref, SXY, x, False) + diff_y(x_ref, SYY, x, True)
                 + diff_z(x_ref, SYZ, x, False))
        store(x_ref, VY, x, load(x_ref, VY, x) + b * force, True)
        force = (diff_x(x_ref, SXZ, x, False) + diff_y(x_ref, SYZ, x, False)
                 + diff_z(x_ref, SZZ, x, True))
        store(x_ref, VZ, x, load(x_ref, VZ, x) + b * force, True)
        return 0

    lax.fori_loop(0, CX + 3, body, 0)


def stress_rates(x_ref, x, lame, mu):
    grad_x = diff_x(x_ref, VX, x, False)
    grad_y = diff_y(x_ref, VY, x, False)
    grad_z = diff_z(x_ref, VZ, x, False)
    modulus = lame + 2.0 * mu
    return {
        SXX: modulus * grad_x + lame * (grad_y + grad_z),
        SYY: modulus * grad_y + lame * (grad_x + grad_z),
        SZZ: modulus * grad_z + lame * (grad_x + grad_y),
        SXY: mu * (diff_y(x_ref, VX, x, True) + diff_x(x_ref, VY, x, True)),
        SXZ: mu * (diff_z(x_ref, VX, x, True) + diff_x(x_ref, VZ, x, True)),
        SYZ: mu * (diff_z(x_ref, VY, x, True) + diff_y(x_ref, VZ, x, True)),
    }


def step_kernel(main_ref, halo_ref, par_main, par_halo, below_ref, above_ref, below_first,
                above_first, new_main, new_halo, send_down, send_up, x_ref, b_ref):
    fill(x_ref, main_ref, halo_ref, below_ref, above_ref)
    fill_buoyancy(b_ref, par_main, par_halo, below_first, above_first)
    velocity_pass(x_ref, b_ref)

    def body(r, _):
        x = r + LOW
        lame, mu = param(par_main, par_halo, 1, r), param(par_main, par_halo, 2, r)
        for f, rate in stress_rates(x_ref, x, lame, mu).items():
            value = load(x_ref, f, x) + DT * rate
            new_main[f, r] = value[:NZ]
            new_halo[f, r] = value[NZ:]
        for f in (VX, VY, VZ):
            value = load(x_ref, f, x)
            new_main[f, r] = value[:NZ]
            new_halo[f, r] = value[NZ:]
        return 0

    lax.fori_loop(0, CX, body, 0)
    write_sends(new_main, new_halo, send_down, send_up)


def write_sends(main_ref, halo_ref, send_down, send_up):
    for n, (f, r) in enumerate(ABOVE):
        send_down[n, 0:NZ] = main_ref[f, r - CX]
        send_down[n, NZ:DEPTH] = halo_ref[f, r - CX]
    for n, (f, r) in enumerate(BELOW):
        send_up[n, 0:NZ] = main_ref[f, r + CX]
        send_up[n, NZ:DEPTH] = halo_ref[f, r + CX]


def pack_kernel(fields_ref, buoy_ref, lame_ref, mu_ref, main_ref, right_ref, left_ref):
    lane = lanes(PACK)
    low = lane % 32 < WIDE

    def pair(read, a, p):
        edges = []
        for k in range(2):
            x = 2 * p + k
            value = read(x)
            main_ref[a, x] = value
            edges.append(edge_pack(value))
        right_ref[a, p] = jnp.where(low, edges[0], pltpu.roll(edges[1], WIDE, 1))
        left_ref[a, p] = jnp.where(low, pltpu.roll(edges[1], 128 - WIDE, 1), edges[0])

    def body(p, _):
        for a in range(9):
            pair(lambda x: fields_ref[pl.ds(a * NZ * CX + x, NZ, stride=CX), :], a, p)
        for a, ref in ((9, buoy_ref), (10, lame_ref), (11, mu_ref)):
            pair(lambda x: ref[pl.ds(x, NZ, stride=CX), :], a, p)
        return 0

    lax.fori_loop(0, CX // 2, body, 0)


def halo_kernel(main_ref, from_left, from_right, halo_ref, send_down, send_up):
    lane = lanes(PACK)
    low = lane % 32 < WIDE

    def body(p, _):
        for a in range(12):
            one, two = from_left[a, p], from_right[a, p]
            halo_ref[a, 2 * p] = jnp.where(low, one, two)
            halo_ref[a, 2 * p + 1] = jnp.where(
                low, pltpu.roll(one, 128 - WIDE, 1), pltpu.roll(two, WIDE, 1))
        return 0

    lax.fori_loop(0, CX // 2, body, 0)
    write_sends(main_ref, halo_ref, send_down, send_up)
    for k in range(BUOY_ROWS):
        for ref, n, r in ((send_down, len(ABOVE) + k, k), (send_up, len(BELOW) + k, CX - BUOY_ROWS + k)):
            ref[n, 0:NZ] = main_ref[9, r]
            ref[n, NZ:DEPTH] = halo_ref[9, r]


def last_velocity_kernel(place_ref, count_ref, main_ref, halo_ref, par_main, par_halo, below_ref,
                         above_ref, below_first, above_first, observed_ref, gain_ref, cell_ref,
                         v_ref, packet_ref, x_ref, b_ref, slot_ref):
    fill(x_ref, main_ref, halo_ref, below_ref, above_ref)
    fill_buoyancy(b_ref, par_main, par_halo, below_first, above_first)
    velocity_pass(x_ref, b_ref)

    def copy_out(x, _):
        v_ref[0, x] = x_ref[0, x]
        v_ref[1, x] = x_ref[1, x]
        v_ref[2, x] = x_ref[2, x]
        return 0

    lax.fori_loop(0, PLANES, copy_out, 0)
    slot_ref[...] = jnp.zeros((16, 128), jnp.float32)
    slot_ref[0:3, 0:S] = observed_ref[...]
    slot_ref[3:4, 0:S] = gain_ref[...]
    slot_ref[4:5, 0:S] = cell_ref[...].astype(jnp.float32)
    cell = slot_ref[4:5, :].astype(jnp.int32)
    cell_x, cell_y = cell // CY, cell % CY
    pick_y = (lax.broadcasted_iota(jnp.int32, (CY, 128), 0) == cell_y).astype(jnp.float32)
    pick_x = lax.broadcasted_iota(jnp.int32, (CX, 128), 0) == cell_x
    live = lanes(1) < count_ref[0]
    gain = slot_ref[3:4, :]
    region, tile = place_ref[0], place_ref[1]
    for c in range(3):
        surface = jnp.concatenate([x_ref[c, r + LOW, 8:9, :] for r in range(CX)], axis=0)
        rows = jnp.dot(surface, pick_y, precision=lax.Precision.HIGHEST,
                       preferred_element_type=jnp.float32)
        sample = jnp.sum(jnp.where(pick_x, rows, 0.0), axis=0, keepdims=True)
        slot_ref[8 + c:9 + c, :] = jnp.where(live, gain * (slot_ref[c:c + 1, :] - sample), 0.0)
    slot_ref[11:12, :] = (region * CX + cell_x).astype(jnp.float32)
    slot_ref[12:13, :] = (tile * CY + cell_y).astype(jnp.float32)
    own = jnp.where(lanes(8) < S, slot_ref[8:16, :], 0.0)
    packet_ref[...] = pltpu.roll(own, region * S, 1)


def last_kernel(place_ref, influence_ref, count_ref, profile_ref, main_ref, par_main, v_ref,
                before_ref, here_ref, after_ref, par_halo, out_ref, profile_rows):
    region, tile = place_ref[0], place_ref[1]
    lane = lanes(8)
    column = lax.broadcasted_iota(jnp.int32, (8, 128), 0) + tile - 1
    slot_id = (lane // S * 32 + column) * S + lane % S
    slot_id = jnp.where((column >= 0) & (column < 32), slot_id, -1)
    used = jnp.zeros((8, 128), jnp.int32)
    for k in range(LIST):
        hit = (slot_id == influence_ref[0, k]) & (k < count_ref[0])
        used = jnp.where(hit, 1, used)
    cell_x = (lax.broadcasted_iota(jnp.int32, (CX, 128), 0) + region * CX).astype(jnp.float32)
    cell_y = (lax.broadcasted_iota(jnp.int32, (CY, 128), 0) + tile * CY).astype(jnp.float32)
    increment = jnp.zeros((3 * CX, CY), jnp.float32)
    for d, ref in enumerate((before_ref, here_ref, after_ref)):
        packet = ref[0] + ref[1] + ref[2] + ref[3]
        dist_x = cell_x - packet[3:4]
        dist_y = cell_y - packet[4:5]
        along_x = jnp.exp(-(dist_x * dist_x) / (2.0 * (0.5 * CX) ** 2))
        along_y = jnp.exp(-(dist_y * dist_y) / (2.0 * (0.25 * CY) ** 2))
        keep = used[d:d + 1] > 0
        scaled = jnp.concatenate(
            [jnp.where(keep, packet[c:c + 1] * along_x, 0.0) for c in range(3)], axis=0)
        increment += lax.dot_general(
            scaled, along_y, (((1,), (1,)), ((), ())), precision=lax.Precision.HIGHEST,
            preferred_element_type=jnp.float32)
    for c in range(3):
        for z in range(NZ):
            profile_rows[c, z:z + 1, :] = jnp.full((1, 128), profile_ref[c, z], jnp.float32)
    for c in range(3):
        for r in range(CX):
            value = v_ref[c, r + LOW, 8:8 + NZ, :]
            value = value + profile_rows[c] * increment[c * CX + r:c * CX + r + 1, :]
            out_ref[pl.ds(c * NZ * CX + r, NZ, stride=CX), :] = value

    def body(r, _):
        lame, mu = param(par_main, par_halo, 1, r), param(par_main, par_halo, 2, r)
        for f, rate in stress_rates(v_ref, r + LOW, lame, mu).items():
            out_ref[pl.ds(f * NZ * CX + r, NZ, stride=CX), :] = main_ref[f, r] + DT * rate[:NZ]
        return 0

    lax.fori_loop(0, CX, body, 0)


def struct(*shape):
    return jax.ShapeDtypeStruct(shape, jnp.float32)


VM = pl.BlockSpec(memory_space=pltpu.VMEM)
SM = pl.BlockSpec(memory_space=pltpu.SMEM)


def call(kernel, out_shape, specs, scratch=()):
    many = isinstance(out_shape, (list, tuple))
    return pl.pallas_call(
        kernel, out_shape=out_shape, in_specs=specs,
        out_specs=[VM] * len(out_shape) if many else VM, scratch_shapes=list(scratch),
        compiler_params=pltpu.CompilerParams(vmem_limit_bytes=VMEM_BYTES))


def neighbours(up, down, axis):
    count = lax.axis_size(axis)
    forward = [(i, i + 1) for i in range(count - 1)]
    backward = [(b, a) for a, b in forward]
    return lax.ppermute(up, axis, forward), lax.ppermute(down, axis, backward)


def per_device(fields, buoyancy, lame_first, shear_modulus, observed, station_weight, depth_profile,
               station_cell, station_count, influence, influence_count):
    place = jnp.stack([lax.axis_index("region"), lax.axis_index("tile")]).astype(jnp.int32)
    main, right, left = call(
        pack_kernel,
        (struct(12, CX, NZ, 128), struct(12, CX // 2, PACK, 128), struct(12, CX // 2, PACK, 128)),
        [VM] * 4,
    )(fields.reshape(9 * NZ * CX, CY), buoyancy.reshape(NZ * CX, CY),
      lame_first.reshape(NZ * CX, CY), shear_modulus.reshape(NZ * CX, CY))
    from_left, from_right = neighbours(right, left, "tile")
    n_down, n_up = len(ABOVE), len(BELOW)
    halo, send_down, send_up = call(
        halo_kernel,
        (struct(12, CX, PACK, 128), struct(n_down + BUOY_ROWS, DEPTH, 128),
         struct(n_up + BUOY_ROWS, DEPTH, 128)),
        [VM] * 3,
    )(main, from_left, from_right)
    par_main, par_halo = main, halo
    below, above = neighbours(send_up, send_down, "region")
    below_first, above_first = below, above
    scratch = [pltpu.VMEM((9, PLANES, ZROWS, 128), jnp.float32),
               pltpu.VMEM((CX + 2 * BUOY_ROWS, DEPTH, 128), jnp.float32)]
    for _ in range(ITERS - 1):
        main, halo, send_down, send_up = call(
            step_kernel,
            (struct(9, CX, NZ, 128), struct(9, CX, PACK, 128), struct(n_down, DEPTH, 128),
             struct(n_up, DEPTH, 128)),
            [VM] * 8, scratch,
        )(main, halo, par_main, par_halo, below, above, below_first, above_first)
        below, above = neighbours(send_up, send_down, "region")
    v, packet = call(
        last_velocity_kernel, (struct(3, PLANES, ZROWS, 128), struct(8, 128)),
        [SM, SM] + [VM] * 11, scratch + [pltpu.VMEM((16, 128), jnp.float32)],
    )(place, station_count, main, halo, par_main, par_halo, below, above, below_first, above_first,
      observed, station_weight.reshape(1, S), station_cell.reshape(1, S))
    here = lax.all_gather(packet, "region")
    before, after = neighbours(here, here, "tile")
    out = call(
        last_kernel, struct(9 * NZ * CX, CY), [SM] * 4 + [VM] * 7,
        [pltpu.VMEM((3, NZ, 128), jnp.float32)],
    )(place, influence, influence_count, depth_profile, main, par_main, v, before, here, after,
      par_halo)
    return out.reshape(9, NZ, CX, CY)


def solution(mesh):
    in_specs = (
        P(None, None, "region", "tile"),
        P(None, "region", "tile"),
        P(None, "region", "tile"),
        P(None, "region", "tile"),
        P(None, ("region", "tile")),
        P(("region", "tile")),
        P(),
        P(("region", "tile")),
        P(("region", "tile")),
        P(("region", "tile"), None),
        P(("region", "tile")),
    )
    out_specs = P(None, None, "region", "tile")
    return jax.shard_map(
        per_device, mesh=mesh, in_specs=in_specs, out_specs=out_specs, check_vma=False
    )
```

```python
import jax
import jax.numpy as jnp
import numpy as np
from jax import lax
from jax.experimental import pallas as pl
from jax.experimental.pallas import tpu as pltpu
from jax.sharding import PartitionSpec as P

NEAR = 1.125
FAR = -1.0 / 24.0
DT = 0.15

CX, CY, NZ = 16, 128, 32
S, LIST = 32, 64
GROUPS = 4
HALF = 16
WIDE = 12
PACK = NZ // GROUPS
DEPTH = NZ + PACK
LOW = 6
PLANES = CX + 2 * LOW
ZROWS = 72

VX, VY, VZ = range(3)
SXX, SYY, SZZ, SXY, SXZ, SYZ = range(6)
Z_STRESS = (SZZ, SXZ, SYZ)

OUTER = [("t", f, 6) for f in (SXX, SXY, SXZ)] + [("t", f, 5) for f in (SYY, SYZ, SZZ)] + [
    ("v", f, 5) for f in range(3)]
OUTER_FIRST = OUTER + [("p", 0, 5), ("p", 1, 3), ("p", 2, 3)]
INNER = [("t", f, 3) for f in (SXX, SXY, SXZ)] + [("t", f, 2) for f in (SYY, SYZ, SZZ)] + [
    ("v", f, 2) for f in range(3)]
INNER_FIRST = INNER + [("p", 0, 2)]

VMEM_BYTES = 8 * 2 ** 20


def is_odd():
    return lax.rem(lax.axis_index("region"), 2) > 0


def plane_count(items):
    return sum(d for _, _, d in items)


def lanes(rows):
    return lax.broadcasted_iota(jnp.int32, (rows, 128), 1)


def band_matrices():
    taps = {0: ((-1, 1), (0, -27), (1, 27), (2, -1)), 1: ((-2, 1), (-1, -27), (0, 27), (1, -1))}
    own = np.zeros((2, GROUPS, 256, 128), np.float32)
    halo = np.zeros((2, 640, 128), np.float32)
    for k in range(2):
        for offset, coef in taps[k]:
            for g in range(GROUPS):
                for lane in range(128):
                    y = lane + offset
                    if 0 <= y < CY:
                        own[k, g, y, lane] += coef
                    else:
                        own[k, g, 128 + 32 * g + HALF + (y if y < 0 else y - CY), lane] += coef
                for spot in range(32):
                    to = spot + offset
                    out = 32 * g + spot
                    if not 0 <= to < 32:
                        continue
                    if (spot < HALF) == (to < HALF):
                        halo[k, 512 + 32 * g + to, out] += coef
                    elif spot < HALF:
                        halo[k, 128 * g + to - HALF, out] += coef
                    else:
                        halo[k, 128 * g + CY + to - HALF, out] += coef
    return own, halo


def two_terms(value):
    high = value.astype(jnp.bfloat16)
    return high, (value - high.astype(jnp.float32)).astype(jnp.bfloat16)


def y_differences(items, count, forward, own_ref, halo_ref, out_ref):
    k = 0 if forward else 1
    even = count + count % 2

    def rows(at):
        return jnp.concatenate(
            [ref[f, x + j, at:at + 8, :] for ref, f, x, _ in items for j in range(even)], axis=0)

    parts = [two_terms(rows(8 + 8 * g)) for g in range(GROUPS)] + [two_terms(rows(56))]

    def product(lhs, rhs):
        return jnp.dot(lhs, rhs, preferred_element_type=jnp.float32)

    for g in range(GROUPS + 1):
        total = 0.0
        for term in range(2):
            if g < GROUPS:
                lhs = jnp.concatenate([parts[g][term], parts[GROUPS][term]], axis=1)
                total += product(lhs, own_ref[k, g])
            else:
                lhs = jnp.concatenate([parts[n][term] for n in range(GROUPS + 1)], axis=1)
                total += product(lhs, halo_ref[k])
        total = total * (1.0 / 24.0)
        for n, (_, _, _, slot) in enumerate(items):
            for j in range(count):
                r = 8 * (n * even + j)
                out_ref[slot, j, 8 * g:8 * g + 8, :] = total[r:r + 8]


def load(ref, f, x, dz=0):
    return jnp.concatenate(
        [ref[f, x, 8 + dz:8 + NZ + dz, :], ref[f, x, 56 + dz:64 + dz, :]], axis=0)


def store(ref, f, x, value):
    ref[f, x, 8:8 + NZ, :] = value[:NZ]
    ref[f, x, 56:64, :] = value[NZ:]


def pad_halo(ref, f, x):
    lane = lanes(PACK)
    halo = ref[f, x, 56:64, :]
    ref[f, x, 48:56, :] = jnp.where(lane < 32, 0.0, pltpu.roll(halo, 32, 1))
    ref[f, x, 64:72, :] = jnp.where(lane >= 96, 0.0, pltpu.roll(halo, 96, 1))


def combine(m1, c0, p1, p2):
    return NEAR * (p1 - c0) + FAR * (p2 - m1)


def diff_x(ref, f, x, forward):
    first = -1 if forward else -2
    return combine(*[load(ref, f, x + first + k) for k in range(4)])


def diff_z(ref, f, x, forward):
    first = -1 if forward else -2
    return combine(*[load(ref, f, x, first + k) for k in range(4)])


def velocity_pass(v_ref, t_ref, p_ref, own_ref, halo_ref, d_ref, x_first, y_first, count):
    xa, ya = x_first + LOW, y_first + LOW
    y_differences([(t_ref, SXY, xa, 0), (t_ref, SYZ, ya, 2)], count, False, own_ref, halo_ref, d_ref)
    y_differences([(t_ref, SYY, ya, 1)], count, True, own_ref, halo_ref, d_ref)

    def body(j, _):
        x = xa + j
        force = diff_x(t_ref, SXX, x, True) + d_ref[0, j] + diff_z(t_ref, SXZ, x, False)
        store(v_ref, VX, x, load(v_ref, VX, x) + p_ref[0, x] * force)
        x = ya + j
        b = p_ref[0, x]
        force = diff_x(t_ref, SXY, x, False) + d_ref[1, j] + diff_z(t_ref, SYZ, x, False)
        store(v_ref, VY, x, load(v_ref, VY, x) + b * force)
        force = diff_x(t_ref, SXZ, x, False) + d_ref[2, j] + diff_z(t_ref, SZZ, x, True)
        store(v_ref, VZ, x, load(v_ref, VZ, x) + b * force)
        return 0

    lax.fori_loop(0, count, body, 0)
    for j in range(count):
        pad_halo(v_ref, VX, xa + j)
        pad_halo(v_ref, VY, ya + j)
        pad_halo(v_ref, VZ, ya + j)


def stress_pass(v_ref, t_ref, p_ref, own_ref, halo_ref, d_ref, first, count, pads=True):
    a = first + LOW
    y_differences([(v_ref, VX, a, 0), (v_ref, VZ, a, 2)], count, True, own_ref, halo_ref, d_ref)
    y_differences([(v_ref, VY, a, 1)], count, False, own_ref, halo_ref, d_ref)

    def body(j, _):
        x = a + j
        lame, mu = p_ref[1, x], p_ref[2, x]
        grad_x = diff_x(v_ref, VX, x, False)
        grad_y = d_ref[1, j]
        grad_z = diff_z(v_ref, VZ, x, False)
        modulus = lame + 2.0 * mu
        rates = (
            (SXX, modulus * grad_x + lame * (grad_y + grad_z)),
            (SYY, modulus * grad_y + lame * (grad_x + grad_z)),
            (SZZ, modulus * grad_z + lame * (grad_x + grad_y)),
            (SXY, mu * (d_ref[0, j] + diff_x(v_ref, VY, x, True))),
            (SXZ, mu * (diff_z(v_ref, VX, x, True) + diff_x(v_ref, VZ, x, True))),
            (SYZ, mu * (diff_z(v_ref, VY, x, True) + d_ref[2, j])),
        )
        for f, rate in rates:
            store(t_ref, f, x, load(t_ref, f, x) + rate)
        return 0

    lax.fori_loop(0, count, body, 0)
    if pads:
        for j in range(count):
            for f in Z_STRESS:
                pad_halo(t_ref, f, a + j)


def take_halo(items, odd, inner, got_ref, v_ref, t_ref, p_ref):
    n = 0
    padded = []
    for kind, f, depth in items:
        above, below = CX, -depth
        row = jnp.where(odd, below, above) if inner else jnp.where(odd, above, below)
        for k in range(depth):
            x = row + LOW + k
            if kind == "p":
                p_ref[f, x] = got_ref[n]
            else:
                store(v_ref if kind == "v" else t_ref, f, x, got_ref[n])
                if kind == "v" or f in Z_STRESS:
                    padded.append((v_ref if kind == "v" else t_ref, f, x))
            n += 1
    for ref, f, x in padded:
        pad_halo(ref, f, x)


def give_halo(items, odd, inner, send_ref, v_ref, t_ref, p_ref):
    n = 0
    for kind, f, depth in items:
        top, bottom = CX - depth, 0
        row = jnp.where(odd, bottom, top) if inner else jnp.where(odd, top, bottom)
        for k in range(depth):
            x = row + LOW + k
            if kind == "p":
                send_ref[n] = p_ref[f, x]
            else:
                send_ref[n] = load(v_ref if kind == "v" else t_ref, f, x)
            n += 1


def pieces():
    out = []
    for u in range(8):
        for v in range(3):
            start = WIDE * u - 32 * v
            a, b = max(0, start), min(32, start + WIDE)
            if a < b:
                out.append((u, v, start, a, b))
    return out


PIECES = pieces()


def edge_pack(main):
    lane = lanes(PACK)
    out = pltpu.roll(main[0:8], HALF, 1)
    for g in range(1, GROUPS):
        rolled = pltpu.roll(main[8 * g:8 * g + 8], (HALF + 32 * g) % 128, 1)
        out = jnp.where(lane >= 32 * g, rolled, out)
    return out


def fetch(refs, buf_ref, sems):
    size = NZ * CX
    waits = []
    for a in range(12):
        src = refs[0].at[pl.ds(a * size, size)] if a < 9 else refs[a - 8]
        waits.append(pltpu.make_async_copy(src, buf_ref.at[pl.ds(a * size, size)], sems.at[a]))
    for copy in waits:
        copy.start()
    return waits


def edge_kernel(fields_ref, buoy_ref, lame_ref, mu_ref, right_ref, left_ref, buf_ref, sems):
    size = NZ * CX
    spot = lanes(PACK) % 32
    for a, copy in enumerate(fetch((fields_ref, buoy_ref, lame_ref, mu_ref), buf_ref, sems)):
        copy.wait()
        for block in range(2):
            rights, lefts = [None] * 3, [None] * 3
            edges = [edge_pack(buf_ref[pl.ds(a * size + 8 * block + u, NZ, stride=CX), :])
                     for u in range(8)]
            for u, v, start, lo, hi in PIECES:
                keep = (spot >= lo) & (spot < hi)
                for parts, at in ((rights, HALF - WIDE), (lefts, HALF)):
                    moved = pltpu.roll(edges[u], (start - at) % 128, 1)
                    parts[v] = moved if parts[v] is None else jnp.where(keep, moved, parts[v])
            for v in range(3):
                right_ref[a, 3 * block + v] = rights[v]
                left_ref[a, 3 * block + v] = lefts[v]


def build_kernel(fields_ref, buoy_ref, lame_ref, mu_ref, v_ref, t_ref, p_ref):
    size = NZ * CX
    zero = jnp.zeros((8, 128), jnp.float32)

    def clear(x, _):
        for ref, f in [(v_ref, f) for f in range(3)] + [(t_ref, f) for f in Z_STRESS]:
            ref[f, x, 0:8, :] = zero
            ref[f, x, 40:48, :] = zero
        return 0

    lax.fori_loop(0, PLANES, clear, 0)
    for a in range(12):
        for x in range(CX):
            if a < 3:
                v_ref[a, x + LOW, 8:8 + NZ, :] = fields_ref[pl.ds(a * size + x, NZ, stride=CX), :]
            elif a < 9:
                t_ref[a - 3, x + LOW, 8:8 + NZ, :] = fields_ref[pl.ds(a * size + x, NZ, stride=CX), :]
            else:
                ref = (buoy_ref, lame_ref, mu_ref)[a - 9]
                p_ref[a - 9, x + LOW, 0:NZ, :] = DT * ref[pl.ds(x, NZ, stride=CX), :]


def halo_kernel(from_left, from_right, v_in, t_in, p_in, v_ref, t_ref, p_ref, outer_ref,
                inner_ref):
    odd = is_odd()
    spot = lanes(PACK) % 32

    def one(a, put):
        for block in range(2):
            for u in range(8):
                value = jnp.zeros((PACK, 128), jnp.float32)
                for w, v, start, lo, hi in PIECES:
                    if w != u:
                        continue
                    for ref, at in ((from_left, HALF - WIDE), (from_right, HALF)):
                        keep = (spot >= lo - start + at) & (spot < hi - start + at)
                        moved = pltpu.roll(ref[a, 3 * block + v], (at - start) % 128, 1)
                        value = jnp.where(keep, moved, value)
                put(8 * block + u + LOW, value)

    def to_v(f, _):
        def put(x, value):
            v_ref[f, x, 56:64, :] = value
        one(f, put)
        return 0

    def to_t(f, _):
        def put(x, value):
            t_ref[f, x, 56:64, :] = value
        one(f + 3, put)
        return 0

    def to_p(f, _):
        def put(x, value):
            p_ref[f, x, NZ:DEPTH, :] = DT * value
        one(f + 9, put)
        return 0

    lax.fori_loop(0, 3, to_v, 0)
    lax.fori_loop(0, 6, to_t, 0)
    lax.fori_loop(0, 3, to_p, 0)

    give_halo(OUTER_FIRST, odd, False, outer_ref, v_ref, t_ref, p_ref)
    give_halo(INNER_FIRST, odd, True, inner_ref, v_ref, t_ref, p_ref)


def pad_own(v_ref, t_ref):
    def pads(x, _):
        for f in range(3):
            pad_halo(v_ref, f, x)
        for f in Z_STRESS:
            pad_halo(t_ref, f, x)
        return 0

    lax.fori_loop(LOW, LOW + CX, pads, 0)


def near_kernel(items, back, sends, own_ref, halo_ref, got_ref, v_in, t_in, p_in, *refs):
    if sends:
        v_ref, t_ref, p_ref, inner_ref, d_ref = refs
    else:
        v_ref, t_ref, p_ref, d_ref = refs
    odd = is_odd()
    if items is INNER_FIRST:
        pad_own(v_ref, t_ref)
    take_halo(items, odd, True, got_ref, v_ref, t_ref, p_ref)
    mats = (v_ref, t_ref, p_ref, own_ref, halo_ref, d_ref)
    velocity_pass(*mats, jnp.where(odd, -2, back + 1), jnp.where(odd, -1, back + 2), CX - back)
    stress_pass(*mats, jnp.where(odd, 0, back + 3), CX - 3 - back)
    if sends:
        give_halo(INNER, odd, True, inner_ref, v_ref, t_ref, p_ref)


def far_steps(items, last, odd, got_ref, v_ref, t_ref, p_ref, own_ref, halo_ref, d_ref):
    take_halo(items, odd, False, got_ref, v_ref, t_ref, p_ref)
    mats = (v_ref, t_ref, p_ref, own_ref, halo_ref, d_ref)
    velocity_pass(*mats, jnp.where(odd, 14, -5), jnp.where(odd, 15, -4), 6)
    stress_pass(*mats, jnp.where(odd, 13, -3), 6)
    velocity_pass(*mats, jnp.where(odd, 11, -2), jnp.where(odd, 12, -1), 6)
    if not last:
        stress_pass(*mats, jnp.where(odd, 10, 0), 6)


def far_kernel(items, own_ref, halo_ref, got_ref, v_in, t_in, p_in, v_ref, t_ref, p_ref,
               outer_ref, d_ref):
    odd = is_odd()
    far_steps(items, False, odd, got_ref, v_ref, t_ref, p_ref, own_ref, halo_ref, d_ref)
    give_halo(OUTER, odd, False, outer_ref, v_ref, t_ref, p_ref)


def station_kernel(items, count_ref, observed_ref, gain_ref, cell_ref, own_ref, halo_ref,
                   got_ref, v_in, t_in, p_in, v_ref, t_ref, p_ref, packet_ref, d_ref, slot_ref):
    odd = is_odd()
    far_steps(items, True, odd, got_ref, v_ref, t_ref, p_ref, own_ref, halo_ref, d_ref)
    slot_ref[...] = jnp.zeros((16, 128), jnp.float32)
    slot_ref[0:3, 0:S] = observed_ref[...]
    slot_ref[3:4, 0:S] = gain_ref[...]
    slot_ref[4:5, 0:S] = cell_ref[...].astype(jnp.float32)
    cell = slot_ref[4:5, :].astype(jnp.int32)
    cell_x, cell_y = cell // CY, cell % CY
    pick_y = (lax.broadcasted_iota(jnp.int32, (CY, 128), 0) == cell_y).astype(jnp.float32)
    pick_x = lax.broadcasted_iota(jnp.int32, (CX, 128), 0) == cell_x
    live = lanes(1) < count_ref[0]
    gain = slot_ref[3:4, :]
    region, tile = lax.axis_index("region"), lax.axis_index("tile")
    surface = jnp.concatenate(
        [v_ref[c, r + LOW, 8:9, :] for c in range(3) for r in range(CX)], axis=0)
    rows = jnp.dot(surface, pick_y, precision=lax.Precision.HIGHEST,
                   preferred_element_type=jnp.float32)
    for c in range(3):
        picked = jnp.where(pick_x, rows[c * CX:(c + 1) * CX], 0.0)
        sample = jnp.sum(picked, axis=0, keepdims=True)
        slot_ref[8 + c:9 + c, :] = jnp.where(live, gain * (slot_ref[c:c + 1, :] - sample), 0.0)
    slot_ref[11:12, :] = (region * CX + cell_x).astype(jnp.float32)
    slot_ref[12:13, :] = (tile * CY + cell_y).astype(jnp.float32)
    own = jnp.where(lanes(8) < S, slot_ref[8:16, :], 0.0)
    packet_ref[...] = pltpu.roll(own, region * S, 1)


def stress_out_kernel(own_ref, halo_ref, v_ref, t_in, p_ref, t_ref, out_ref, d_ref,
                      rows_ref, sem):
    odd = is_odd()
    stress_pass(v_ref, t_ref, p_ref, own_ref, halo_ref, d_ref, jnp.where(odd, 10, 0), 6, pads=False)
    size = NZ * CX

    def body(r, _):
        for f in range(6):
            rows_ref[pl.ds(f * size + r, NZ, stride=CX), :] = t_ref[f, r + LOW, 8:8 + NZ, :]
        return 0

    lax.fori_loop(0, CX, body, 0)
    copy = pltpu.make_async_copy(rows_ref, out_ref.at[pl.ds(3 * size, 6 * size)], sem)
    copy.start()
    copy.wait()


def increment_kernel(influence_ref, count_ref, profile_ref, v_ref, before_ref, here_ref,
                     after_ref, out_in, out_ref, profile_rows, rows_ref, sem):
    region, tile = lax.axis_index("region"), lax.axis_index("tile")
    lane = lanes(8)
    column = lax.broadcasted_iota(jnp.int32, (8, 128), 0) + tile - 1
    slot_id = (lane // S * 32 + column) * S + lane % S
    slot_id = jnp.where((column >= 0) & (column < 32), slot_id, -1)
    used = jnp.zeros((8, 128), jnp.int32)
    for k in range(LIST):
        hit = (slot_id == influence_ref[0, k]) & (k < count_ref[0])
        used = jnp.where(hit, 1, used)
    cell_x = (lax.broadcasted_iota(jnp.int32, (CX, 128), 0) + region * CX).astype(jnp.float32)
    cell_y = (lax.broadcasted_iota(jnp.int32, (CY, 128), 0) + tile * CY).astype(jnp.float32)
    increment = jnp.zeros((3 * CX, CY), jnp.float32)
    for d, ref in enumerate((before_ref, here_ref, after_ref)):
        packet = ref[0] + ref[1] + ref[2] + ref[3]
        dist_x = cell_x - packet[3:4]
        dist_y = cell_y - packet[4:5]
        along_x = jnp.exp(-(dist_x * dist_x) / (2.0 * (0.5 * CX) ** 2))
        along_y = jnp.exp(-(dist_y * dist_y) / (2.0 * (0.25 * CY) ** 2))
        keep = used[d:d + 1] > 0
        scaled = jnp.concatenate(
            [jnp.where(keep, packet[c:c + 1] * along_x, 0.0) for c in range(3)], axis=0)
        increment += lax.dot_general(
            scaled, along_y, (((1,), (1,)), ((), ())), precision=lax.Precision.HIGHEST,
            preferred_element_type=jnp.float32)
    for c in range(3):
        for z in range(NZ):
            profile_rows[c, z:z + 1, :] = jnp.full((1, 128), profile_ref[c, z], jnp.float32)
    for c in range(3):
        for r in range(CX):
            value = v_ref[c, r + LOW, 8:8 + NZ, :]
            value = value + profile_rows[c] * increment[c * CX + r:c * CX + r + 1, :]
            rows_ref[pl.ds(c * NZ * CX + r, NZ, stride=CX), :] = value
    copy = pltpu.make_async_copy(rows_ref, out_ref.at[pl.ds(0, 3 * NZ * CX)], sem)
    copy.start()
    copy.wait()


def struct(*shape):
    return jax.ShapeDtypeStruct(shape, jnp.float32)


VM = pl.BlockSpec(memory_space=pltpu.VMEM)
SM = pl.BlockSpec(memory_space=pltpu.SMEM)
HB = pl.BlockSpec(memory_space=pltpu.HBM)


def call(kernel, outs, specs, scratch, out_specs=None, aliases=None, vmem=VMEM_BYTES):
    return pl.pallas_call(
        kernel, out_shape=outs, in_specs=specs, out_specs=out_specs or [VM] * len(outs),
        scratch_shapes=list(scratch), input_output_aliases=aliases or {},
        compiler_params=pltpu.CompilerParams(vmem_limit_bytes=vmem))


INNER_SWAP = [(0, 1), (1, 0), (2, 3), (3, 2)]
OUTER_SWAP = [(1, 2), (2, 1)]


def bind(kernel, *first):
    def bound(*refs):
        return kernel(*first, *refs)
    return bound


def per_device(fields, buoyancy, lame_first, shear_modulus, observed, station_weight, depth_profile,
               station_cell, station_count, influence, influence_count):
    own, edge = band_matrices()
    own, edge = jnp.asarray(own, jnp.bfloat16), jnp.asarray(edge, jnp.bfloat16)
    size = NZ * CX
    state = (struct(3, PLANES, ZROWS, 128), struct(6, PLANES, ZROWS, 128),
             struct(3, PLANES, DEPTH, 128))
    given = (fields.reshape(9 * size, CY), buoyancy.reshape(size, CY),
             lame_first.reshape(size, CY), shear_modulus.reshape(size, CY))
    fetched = [pltpu.VMEM((12 * size, 128), jnp.float32), pltpu.SemaphoreType.DMA((12,))]
    right, left = call(edge_kernel, (struct(12, 6, PACK, 128),) * 2, [HB] * 4, fetched,
                       vmem=60 * 2 ** 20)(*given)
    count = lax.axis_size("tile")
    forward = [(i, i + 1) for i in range(count - 1)]
    backward = [(b, a) for a, b in forward]
    from_left = lax.ppermute(right, "tile", forward)
    from_right = lax.ppermute(left, "tile", backward)
    v, t, p = call(build_kernel, state, [VM] * 4, [])(*given)
    v, t, p, outer, inner = call(
        halo_kernel, state + (struct(plane_count(OUTER_FIRST), DEPTH, 128),
                              struct(plane_count(INNER_FIRST), DEPTH, 128)),
        [VM] * 5, [], aliases={2: 0, 3: 1, 4: 2},
    )(from_left, from_right, v, t, p)
    inner_struct = struct(plane_count(INNER), DEPTH, 128)
    d_scratch = pltpu.VMEM((3, CX, DEPTH, 128), jnp.float32)
    alias = {3: 0, 4: 1, 5: 2}
    for block in range(2):
        got = lax.ppermute(inner, "region", INNER_SWAP)
        got_outer = lax.ppermute(outer, "region", OUTER_SWAP)
        v, t, p, inner = call(
            bind(near_kernel, INNER_FIRST if block == 0 else INNER, 0, True),
            state + (inner_struct,), [VM] * 6, [d_scratch], aliases=alias,
        )(own, edge, got, v, t, p)
        got = lax.ppermute(inner, "region", INNER_SWAP)
        if block == 0:
            v, t, p, inner = call(
                bind(near_kernel, INNER, 3, True), state + (inner_struct,), [VM] * 6,
                [d_scratch], aliases=alias,
            )(own, edge, got, v, t, p)
            v, t, p, outer = call(
                bind(far_kernel, OUTER_FIRST), state + (struct(plane_count(OUTER), DEPTH, 128),),
                [VM] * 6, [d_scratch], aliases=alias,
            )(own, edge, got_outer, v, t, p)
        else:
            v, t, p = call(
                bind(near_kernel, INNER, 3, False), state, [VM] * 6, [d_scratch],
                aliases=alias,
            )(own, edge, got, v, t, p)
    v, t, p, packet = call(
        bind(station_kernel, OUTER), state + (struct(8, 128),), [SM] + [VM] * 9,
        [d_scratch, pltpu.VMEM((16, 128), jnp.float32)], aliases={7: 0, 8: 1, 9: 2},
    )(station_count, observed, station_weight.reshape(1, S), station_cell.reshape(1, S),
      own, edge, got_outer, v, t, p)
    here = lax.all_gather(packet, "region")
    before = lax.ppermute(here, "tile", forward)
    after = lax.ppermute(here, "tile", backward)
    _, out = call(
        stress_out_kernel, (state[1], struct(9 * size, 128)), [VM] * 5,
        [d_scratch, pltpu.VMEM((6 * size, 128), jnp.float32), pltpu.SemaphoreType.DMA],
        out_specs=[VM, HB], aliases={3: 0},
    )(own, edge, v, t, p)
    out, = call(
        increment_kernel, (struct(9 * size, 128),), [SM] * 3 + [VM] * 4 + [HB],
        [pltpu.VMEM((3, NZ, 128), jnp.float32), pltpu.VMEM((3 * size, 128), jnp.float32),
         pltpu.SemaphoreType.DMA], out_specs=[HB], aliases={7: 0},
    )(influence, influence_count, depth_profile, v, before, here, after, out)
    return out.reshape(9, NZ, CX, CY)


def solution(mesh):
    in_specs = (
        P(None, None, "region", "tile"),
        P(None, "region", "tile"),
        P(None, "region", "tile"),
        P(None, "region", "tile"),
        P(None, ("region", "tile")),
        P(("region", "tile")),
        P(),
        P(("region", "tile")),
        P(("region", "tile")),
        P(("region", "tile"), None),
        P(("region", "tile")),
    )
    out_specs = P(None, None, "region", "tile")
    return jax.shard_map(
        per_device, mesh=mesh, in_specs=in_specs, out_specs=out_specs, check_vma=False
    )
```

```python
import jax
import jax.numpy as jnp
import numpy as np
from jax import lax
from jax.experimental import pallas as pl
from jax.experimental.pallas import tpu as pltpu
from jax.sharding import PartitionSpec as P

NEAR = 1.125
FAR = -1.0 / 24.0
DT = 0.15

CX, CY, NZ = 16, 128, 32
S, LIST = 32, 64
GROUPS = 4
HALF = 16
WIDE = 12
PACK = NZ // GROUPS
DEPTH = NZ + PACK
LOW = 6
PLANES = CX + 2 * LOW
ZROWS = 72

VX, VY, VZ = range(3)
SXX, SYY, SZZ, SXY, SXZ, SYZ = range(6)
Z_STRESS = (SZZ, SXZ, SYZ)

OUTER = [("t", f, 6) for f in (SXX, SXY, SXZ)] + [("t", f, 5) for f in (SYY, SYZ, SZZ)] + [
    ("v", f, 5) for f in range(3)]
OUTER_FIRST = OUTER + [("p", 0, 5), ("p", 1, 3), ("p", 2, 3)]
INNER = [("t", f, 3) for f in (SXX, SXY, SXZ)] + [("t", f, 2) for f in (SYY, SYZ, SZZ)] + [
    ("v", f, 2) for f in range(3)]
INNER_FIRST = INNER + [("p", 0, 2)]

VMEM_BYTES = 8 * 2 ** 20


def is_odd():
    return lax.rem(lax.axis_index("region"), 2) > 0


def plane_count(items):
    return sum(d for _, _, d in items)


def lanes(rows):
    return lax.broadcasted_iota(jnp.int32, (rows, 128), 1)


def band_matrices():
    taps = {0: ((-1, 1), (0, -27), (1, 27), (2, -1)), 1: ((-2, 1), (-1, -27), (0, 27), (1, -1))}
    own = np.zeros((2, GROUPS, 256, 128), np.float32)
    halo = np.zeros((2, 640, 128), np.float32)
    for k in range(2):
        for offset, coef in taps[k]:
            for g in range(GROUPS):
                for lane in range(128):
                    y = lane + offset
                    if 0 <= y < CY:
                        own[k, g, y, lane] += coef
                    else:
                        own[k, g, 128 + 32 * g + HALF + (y if y < 0 else y - CY), lane] += coef
                for spot in range(32):
                    to = spot + offset
                    out = 32 * g + spot
                    if not 0 <= to < 32:
                        continue
                    if (spot < HALF) == (to < HALF):
                        halo[k, 512 + 32 * g + to, out] += coef
                    elif spot < HALF:
                        halo[k, 128 * g + to - HALF, out] += coef
                    else:
                        halo[k, 128 * g + CY + to - HALF, out] += coef
    return own, halo


def two_terms(value):
    high = value.astype(jnp.bfloat16)
    return high, (value - high.astype(jnp.float32)).astype(jnp.bfloat16)


def y_differences(items, count, forward, own_ref, halo_ref, out_ref):
    k = 0 if forward else 1
    even = count + count % 2

    def rows(at):
        return jnp.concatenate(
            [ref[f, x + j, at:at + 8, :] for ref, f, x, _ in items for j in range(even)], axis=0)

    parts = [two_terms(rows(8 + 8 * g)) for g in range(GROUPS)] + [two_terms(rows(56))]

    def product(lhs, rhs):
        return jnp.dot(lhs, rhs, preferred_element_type=jnp.float32)

    for g in range(GROUPS + 1):
        total = 0.0
        for term in range(2):
            if g < GROUPS:
                lhs = jnp.concatenate([parts[g][term], parts[GROUPS][term]], axis=1)
                total += product(lhs, own_ref[k, g])
            else:
                lhs = jnp.concatenate([parts[n][term] for n in range(GROUPS + 1)], axis=1)
                total += product(lhs, halo_ref[k])
        total = total * (1.0 / 24.0)
        for n, (_, _, _, slot) in enumerate(items):
            for j in range(count):
                r = 8 * (n * even + j)
                out_ref[slot, j, 8 * g:8 * g + 8, :] = total[r:r + 8]


def load(ref, f, x, dz=0):
    return jnp.concatenate(
        [ref[f, x, 8 + dz:8 + NZ + dz, :], ref[f, x, 56 + dz:64 + dz, :]], axis=0)


def store(ref, f, x, value):
    ref[f, x, 8:8 + NZ, :] = value[:NZ]
    ref[f, x, 56:64, :] = value[NZ:]


def pad_halo(ref, f, x):
    lane = lanes(PACK)
    halo = ref[f, x, 56:64, :]
    ref[f, x, 48:56, :] = jnp.where(lane < 32, 0.0, pltpu.roll(halo, 32, 1))
    ref[f, x, 64:72, :] = jnp.where(lane >= 96, 0.0, pltpu.roll(halo, 96, 1))


def combine(m1, c0, p1, p2):
    return NEAR * (p1 - c0) + FAR * (p2 - m1)


def diff_x(ref, f, x, forward):
    first = -1 if forward else -2
    return combine(*[load(ref, f, x + first + k) for k in range(4)])


def diff_z(ref, f, x, forward):
    first = -1 if forward else -2
    return combine(*[load(ref, f, x, first + k) for k in range(4)])


def velocity_pass(v_ref, t_ref, p_ref, own_ref, halo_ref, d_ref, x_first, y_first, count):
    xa, ya = x_first + LOW, y_first + LOW
    y_differences([(t_ref, SXY, xa, 0), (t_ref, SYZ, ya, 2)], count, False, own_ref, halo_ref, d_ref)
    y_differences([(t_ref, SYY, ya, 1)], count, True, own_ref, halo_ref, d_ref)

    def body(j, _):
        x = xa + j
        force = diff_x(t_ref, SXX, x, True) + d_ref[0, j] + diff_z(t_ref, SXZ, x, False)
        store(v_ref, VX, x, load(v_ref, VX, x) + p_ref[0, x] * force)
        x = ya + j
        b = p_ref[0, x]
        force = diff_x(t_ref, SXY, x, False) + d_ref[1, j] + diff_z(t_ref, SYZ, x, False)
        store(v_ref, VY, x, load(v_ref, VY, x) + b * force)
        force = diff_x(t_ref, SXZ, x, False) + d_ref[2, j] + diff_z(t_ref, SZZ, x, True)
        store(v_ref, VZ, x, load(v_ref, VZ, x) + b * force)
        return 0

    lax.fori_loop(0, count, body, 0)
    for j in range(count):
        pad_halo(v_ref, VX, xa + j)
        pad_halo(v_ref, VY, ya + j)
        pad_halo(v_ref, VZ, ya + j)


def stress_pass(v_ref, t_ref, p_ref, own_ref, halo_ref, d_ref, first, count, pads=True):
    a = first + LOW
    y_differences([(v_ref, VX, a, 0), (v_ref, VZ, a, 2)], count, True, own_ref, halo_ref, d_ref)
    y_differences([(v_ref, VY, a, 1)], count, False, own_ref, halo_ref, d_ref)

    def body(j, _):
        x = a + j
        lame, mu = p_ref[1, x], p_ref[2, x]
        grad_x = diff_x(v_ref, VX, x, False)
        grad_y = d_ref[1, j]
        grad_z = diff_z(v_ref, VZ, x, False)
        modulus = lame + 2.0 * mu
        rates = (
            (SXX, modulus * grad_x + lame * (grad_y + grad_z)),
            (SYY, modulus * grad_y + lame * (grad_x + grad_z)),
            (SZZ, modulus * grad_z + lame * (grad_x + grad_y)),
            (SXY, mu * (d_ref[0, j] + diff_x(v_ref, VY, x, True))),
            (SXZ, mu * (diff_z(v_ref, VX, x, True) + diff_x(v_ref, VZ, x, True))),
            (SYZ, mu * (diff_z(v_ref, VY, x, True) + d_ref[2, j])),
        )
        for f, rate in rates:
            store(t_ref, f, x, load(t_ref, f, x) + rate)
        return 0

    lax.fori_loop(0, count, body, 0)
    if pads:
        for j in range(count):
            for f in Z_STRESS:
                pad_halo(t_ref, f, a + j)


def take_halo(items, odd, inner, got_ref, v_ref, t_ref, p_ref):
    n = 0
    padded = []
    for kind, f, depth in items:
        above, below = CX, -depth
        row = jnp.where(odd, below, above) if inner else jnp.where(odd, above, below)
        for k in range(depth):
            x = row + LOW + k
            if kind == "p":
                p_ref[f, x] = got_ref[n]
            else:
                store(v_ref if kind == "v" else t_ref, f, x, got_ref[n])
                if kind == "v" or f in Z_STRESS:
                    padded.append((v_ref if kind == "v" else t_ref, f, x))
            n += 1
    for ref, f, x in padded:
        pad_halo(ref, f, x)


def give_halo(items, odd, inner, send_ref, v_ref, t_ref, p_ref):
    n = 0
    for kind, f, depth in items:
        top, bottom = CX - depth, 0
        row = jnp.where(odd, bottom, top) if inner else jnp.where(odd, top, bottom)
        for k in range(depth):
            x = row + LOW + k
            if kind == "p":
                send_ref[n] = p_ref[f, x]
            else:
                send_ref[n] = load(v_ref if kind == "v" else t_ref, f, x)
            n += 1


def pieces():
    out = []
    for u in range(8):
        for v in range(3):
            start = WIDE * u - 32 * v
            a, b = max(0, start), min(32, start + WIDE)
            if a < b:
                out.append((u, v, start, a, b))
    return out


PIECES = pieces()


def fetch(refs, buf_ref, sems):
    size = NZ * CX
    waits = []
    for a in range(12):
        src = refs[0].at[pl.ds(a * size, size)] if a < 9 else refs[a - 8]
        waits.append(pltpu.make_async_copy(src, buf_ref.at[pl.ds(a * size, size)], sems.at[a]))
    for copy in waits:
        copy.start()
    return waits


def low_side(first):
    odd = lax.rem(lax.axis_index("tile"), 2) > 0
    return jnp.where(odd, HALF - WIDE, HALF) if first else jnp.where(odd, HALF, HALF - WIDE)


def pack_units(units, at, put):
    spot = lanes(PACK) % 32
    parts = [None] * 3
    for u, v, start, lo, hi in PIECES:
        keep = (spot >= lo) & (spot < hi)
        moved = pltpu.roll(units[u], lax.rem(start - at + 256, 128), 1)
        parts[v] = moved if parts[v] is None else jnp.where(keep, moved, parts[v])
    for v in range(3):
        put(v, parts[v])


def edge_kernel(fields_ref, buoy_ref, lame_ref, mu_ref, first_ref, second_ref, buf_ref, sems):
    size = NZ * CX
    lane = lanes(PACK)
    for a, copy in enumerate(fetch((fields_ref, buoy_ref, lame_ref, mu_ref), buf_ref, sems)):
        copy.wait()
        for block in range(2):
            units = []
            for u in range(8):
                out = None
                for g in range(GROUPS):
                    row = a * size + (8 * g + u) * CX + 8 * block
                    moved = pltpu.roll(buf_ref[row:row + 8, :], (HALF + 32 * g) % 128, 1)
                    out = moved if g == 0 else jnp.where(lane >= 32 * g, moved, out)
                units.append(out)
            for ref, is_first in ((first_ref, True), (second_ref, False)):
                def put(v, value):
                    ref[a, 3 * block + v] = value
                pack_units(units, 2 * HALF - WIDE - low_side(is_first), put)


def unpack_units(got_ref, a, block, at, under, put):
    spot = lanes(PACK) % 32
    for u in range(8):
        value = under(u)
        for w, v, start, lo, hi in PIECES:
            if w == u:
                keep = (spot >= lo - start + at) & (spot < hi - start + at)
                moved = pltpu.roll(got_ref[a, 3 * block + v], lax.rem(at - start + 256, 128), 1)
                value = jnp.where(keep, moved, value)
        put(u, value)


def first_halo_kernel(got_ref, half_ref):
    at = low_side(True)

    def body(a, _):
        for block in range(2):
            def put(u, value):
                half_ref[a, block, u] = value
            unpack_units(got_ref, a, block, at, lambda u: jnp.zeros((PACK, 128), jnp.float32), put)
        return 0

    lax.fori_loop(0, 12, body, 0)


def build_kernel(fields_ref, buoy_ref, lame_ref, mu_ref, v_ref, t_ref, p_ref):
    size = NZ * CX
    zero = jnp.zeros((8, 128), jnp.float32)

    def clear(x, _):
        for ref, f in [(v_ref, f) for f in range(3)] + [(t_ref, f) for f in Z_STRESS]:
            ref[f, x, 0:8, :] = zero
            ref[f, x, 40:48, :] = zero
        return 0

    lax.fori_loop(0, PLANES, clear, 0)
    for a in range(12):
        ref, first = (fields_ref, a * size) if a < 9 else ((buoy_ref, lame_ref, mu_ref)[a - 9], 0)
        for x in range(CX):
            value = ref[pl.ds(first + x, NZ, stride=CX), :]
            if a < 3:
                v_ref[a, x + LOW, 8:8 + NZ, :] = value
            elif a < 9:
                t_ref[a - 3, x + LOW, 8:8 + NZ, :] = value
            else:
                p_ref[a - 9, x + LOW, 0:NZ, :] = DT * value


def halo_kernel(got_ref, half_ref, v_in, t_in, p_in, v_ref, t_ref, p_ref, outer_ref, inner_ref):
    odd = is_odd()
    at = low_side(False)
    v_rows = v_ref.reshape(3 * PLANES * ZROWS, 128)
    t_rows = t_ref.reshape(6 * PLANES * ZROWS, 128)
    p_rows = p_ref.reshape(3 * PLANES * DEPTH, 128)

    def one(a, f, rows_ref, depth, begin, scale):
        for block in range(2):
            def put(u, value):
                row = (f * PLANES + LOW + 8 * block) * depth + begin + u
                rows_ref[pl.ds(row, 8, stride=depth), :] = scale * value if scale else value
            unpack_units(got_ref, a, block, at, lambda u: half_ref[a, block, u], put)

    for a in range(12):
        if a < 3:
            one(a, a, v_rows, ZROWS, 56, None)
        elif a < 9:
            one(a, a - 3, t_rows, ZROWS, 56, None)
        else:
            one(a, a - 9, p_rows, DEPTH, NZ, DT)
    give_halo(OUTER_FIRST, odd, False, outer_ref, v_ref, t_ref, p_ref)
    give_halo(INNER_FIRST, odd, True, inner_ref, v_ref, t_ref, p_ref)


def pad_own(v_ref, t_ref):
    def pads(x, _):
        for f in range(3):
            pad_halo(v_ref, f, x)
        for f in Z_STRESS:
            pad_halo(t_ref, f, x)
        return 0

    lax.fori_loop(LOW, LOW + CX, pads, 0)


def near_kernel(items, back, sends, own_ref, halo_ref, got_ref, v_in, t_in, p_in, *refs):
    if sends:
        v_ref, t_ref, p_ref, inner_ref, d_ref = refs
    else:
        v_ref, t_ref, p_ref, d_ref = refs
    odd = is_odd()
    if items is INNER_FIRST:
        pad_own(v_ref, t_ref)
    take_halo(items, odd, True, got_ref, v_ref, t_ref, p_ref)
    mats = (v_ref, t_ref, p_ref, own_ref, halo_ref, d_ref)
    velocity_pass(*mats, jnp.where(odd, -2, back + 1), jnp.where(odd, -1, back + 2), CX - back)
    stress_pass(*mats, jnp.where(odd, 0, back + 3), CX - 3 - back)
    if sends:
        give_halo(INNER, odd, True, inner_ref, v_ref, t_ref, p_ref)


def far_steps(items, last, odd, got_ref, v_ref, t_ref, p_ref, own_ref, halo_ref, d_ref):
    take_halo(items, odd, False, got_ref, v_ref, t_ref, p_ref)
    mats = (v_ref, t_ref, p_ref, own_ref, halo_ref, d_ref)
    velocity_pass(*mats, jnp.where(odd, 14, -5), jnp.where(odd, 15, -4), 6)
    stress_pass(*mats, jnp.where(odd, 13, -3), 6)
    velocity_pass(*mats, jnp.where(odd, 11, -2), jnp.where(odd, 12, -1), 6)
    if not last:
        stress_pass(*mats, jnp.where(odd, 10, 0), 6)


def far_kernel(items, own_ref, halo_ref, got_ref, v_in, t_in, p_in, v_ref, t_ref, p_ref,
               outer_ref, d_ref):
    odd = is_odd()
    far_steps(items, False, odd, got_ref, v_ref, t_ref, p_ref, own_ref, halo_ref, d_ref)
    give_halo(OUTER, odd, False, outer_ref, v_ref, t_ref, p_ref)


def station_kernel(items, count_ref, observed_ref, gain_ref, cell_ref, own_ref, halo_ref,
                   got_ref, v_in, t_in, p_in, v_ref, t_ref, p_ref, packet_ref, d_ref, slot_ref):
    odd = is_odd()
    far_steps(items, True, odd, got_ref, v_ref, t_ref, p_ref, own_ref, halo_ref, d_ref)
    slot_ref[...] = jnp.zeros((16, 128), jnp.float32)
    slot_ref[0:3, 0:S] = observed_ref[...]
    slot_ref[3:4, 0:S] = gain_ref[...]
    slot_ref[4:5, 0:S] = cell_ref[...].astype(jnp.float32)
    cell = slot_ref[4:5, :].astype(jnp.int32)
    cell_x, cell_y = cell // CY, cell % CY
    pick_y = (lax.broadcasted_iota(jnp.int32, (CY, 128), 0) == cell_y).astype(jnp.float32)
    pick_x = lax.broadcasted_iota(jnp.int32, (CX, 128), 0) == cell_x
    live = lanes(1) < count_ref[0]
    gain = slot_ref[3:4, :]
    region, tile = lax.axis_index("region"), lax.axis_index("tile")
    surface = jnp.concatenate(
        [v_ref[c, r + LOW, 8:9, :] for c in range(3) for r in range(CX)], axis=0)
    rows = jnp.dot(surface, pick_y, precision=lax.Precision.HIGHEST,
                   preferred_element_type=jnp.float32)
    for c in range(3):
        picked = jnp.where(pick_x, rows[c * CX:(c + 1) * CX], 0.0)
        sample = jnp.sum(picked, axis=0, keepdims=True)
        slot_ref[8 + c:9 + c, :] = jnp.where(live, gain * (slot_ref[c:c + 1, :] - sample), 0.0)
    slot_ref[11:12, :] = (region * CX + cell_x).astype(jnp.float32)
    slot_ref[12:13, :] = (tile * CY + cell_y).astype(jnp.float32)
    own = jnp.where(lanes(8) < S, slot_ref[8:16, :], 0.0)
    packet_ref[...] = pltpu.roll(own, region * S, 1)


def tile_column(packet_refs, used, cell_x, cell_y):
    packet = packet_refs[0] + packet_refs[1] + packet_refs[2] + packet_refs[3]
    dist_x = cell_x - packet[3:4]
    dist_y = cell_y - packet[4:5]
    along_x = jnp.exp(-(dist_x * dist_x) / (2.0 * (0.5 * CX) ** 2))
    along_y = jnp.exp(-(dist_y * dist_y) / (2.0 * (0.25 * CY) ** 2))
    scaled = jnp.concatenate(
        [jnp.where(used > 0, packet[c:c + 1] * along_x, 0.0) for c in range(3)], axis=0)
    return lax.dot_general(
        scaled, along_y, (((1,), (1,)), ((), ())), precision=lax.Precision.HIGHEST,
        preferred_element_type=jnp.float32)


def cell_places():
    region, tile = lax.axis_index("region"), lax.axis_index("tile")
    cell_x = (lax.broadcasted_iota(jnp.int32, (CX, 128), 0) + region * CX).astype(jnp.float32)
    cell_y = (lax.broadcasted_iota(jnp.int32, (CY, 128), 0) + tile * CY).astype(jnp.float32)
    return cell_x, cell_y


def stress_out_kernel(influence_ref, count_ref, profile_ref, own_ref, halo_ref, here_ref, v_ref,
                      t_in, p_ref, t_ref, out_ref, used_ref, profile_rows, own_part, d_ref, rows_ref,
                      sem):
    odd = is_odd()
    stress_pass(v_ref, t_ref, p_ref, own_ref, halo_ref, d_ref, jnp.where(odd, 10, 0), 6, pads=False)
    size = NZ * CX

    def body(r, _):
        for f in range(6):
            rows_ref[pl.ds(f * size + r, NZ, stride=CX), :] = t_ref[f, r + LOW, 8:8 + NZ, :]
        return 0

    lax.fori_loop(0, CX, body, 0)
    copy = pltpu.make_async_copy(rows_ref, out_ref.at[pl.ds(3 * size, 6 * size)], sem)
    copy.start()
    lane = lanes(8)
    column = lax.broadcasted_iota(jnp.int32, (8, 128), 0) + lax.axis_index("tile") - 1
    slot_id = (lane // S * 32 + column) * S + lane % S
    slot_id = jnp.where((column >= 0) & (column < 32), slot_id, -1)
    used = jnp.zeros((8, 128), jnp.int32)
    for k in range(LIST):
        hit = (slot_id == influence_ref[0, k]) & (k < count_ref[0])
        used = jnp.where(hit, 1, used)
    used_ref[...] = used
    for c in range(3):
        for z in range(NZ):
            profile_rows[c, z:z + 1, :] = jnp.full((1, 128), profile_ref[c, z], jnp.float32)
    own_part[...] = tile_column(here_ref, used[1:2], *cell_places())
    copy.wait()


def increment_kernel(v_ref, first_ref, second_ref, used_ref, profile_rows, own_part, out_in, out_ref,
                     rows_ref, sem):
    odd = lax.rem(lax.axis_index("tile"), 2) > 0
    before = [jnp.where(odd, first_ref[r], second_ref[r]) for r in range(4)]
    after = [jnp.where(odd, second_ref[r], first_ref[r]) for r in range(4)]
    places = cell_places()
    increment = (own_part[...] + tile_column(before, used_ref[0:1], *places)
                 + tile_column(after, used_ref[2:3], *places))
    for c in range(3):
        for r in range(CX):
            value = v_ref[c, r + LOW, 8:8 + NZ, :]
            value = value + profile_rows[c] * increment[c * CX + r:c * CX + r + 1, :]
            rows_ref[pl.ds(c * NZ * CX + r, NZ, stride=CX), :] = value
    copy = pltpu.make_async_copy(rows_ref, out_ref.at[pl.ds(0, 3 * NZ * CX)], sem)
    copy.start()
    copy.wait()


def struct(*shape):
    return jax.ShapeDtypeStruct(shape, jnp.float32)


VM = pl.BlockSpec(memory_space=pltpu.VMEM)
SM = pl.BlockSpec(memory_space=pltpu.SMEM)
HB = pl.BlockSpec(memory_space=pltpu.HBM)


def call(kernel, outs, specs, scratch, out_specs=None, aliases=None, vmem=VMEM_BYTES):
    return pl.pallas_call(
        kernel, out_shape=outs, in_specs=specs, out_specs=out_specs or [VM] * len(outs),
        scratch_shapes=list(scratch), input_output_aliases=aliases or {},
        compiler_params=pltpu.CompilerParams(vmem_limit_bytes=vmem))


def pairs(first):
    return [p for i in range(first, 31, 2) for p in ((i, i + 1), (i + 1, i))]


INNER_SWAP = [(0, 1), (1, 0), (2, 3), (3, 2)]
OUTER_SWAP = [(1, 2), (2, 1)]


def bind(kernel, *first):
    def bound(*refs):
        return kernel(*first, *refs)
    return bound


def per_device(fields, buoyancy, lame_first, shear_modulus, observed, station_weight, depth_profile,
               station_cell, station_count, influence, influence_count):
    own, edge = band_matrices()
    own, edge = jnp.asarray(own, jnp.bfloat16), jnp.asarray(edge, jnp.bfloat16)
    size = NZ * CX
    state = (struct(3, PLANES, ZROWS, 128), struct(6, PLANES, ZROWS, 128),
             struct(3, PLANES, DEPTH, 128))
    given = (fields.reshape(9 * size, CY), buoyancy.reshape(size, CY),
             lame_first.reshape(size, CY), shear_modulus.reshape(size, CY))
    fetched = [pltpu.VMEM((12 * size, 128), jnp.float32), pltpu.SemaphoreType.DMA((12,))]
    packed, edges = struct(12, 6, PACK, 128), struct(12, 2, 8, 8, 128)
    first, second = call(edge_kernel, (packed, packed), [HB] * 4, fetched,
                         vmem=62 * 2 ** 20)(*given)
    got_first = lax.ppermute(first, "tile", pairs(0))
    got_second = lax.ppermute(second, "tile", pairs(1))
    v, t, p = call(build_kernel, state, [VM] * 4, [])(*given)
    half, = call(first_halo_kernel, (edges,), [VM], [])(got_first)
    v, t, p, outer, inner = call(
        halo_kernel, state + (struct(plane_count(OUTER_FIRST), DEPTH, 128),
                              struct(plane_count(INNER_FIRST), DEPTH, 128)),
        [VM] * 5, [], aliases={2: 0, 3: 1, 4: 2},
    )(got_second, half, v, t, p)
    inner_struct = struct(plane_count(INNER), DEPTH, 128)
    d_scratch = pltpu.VMEM((3, CX, DEPTH, 128), jnp.float32)
    alias = {3: 0, 4: 1, 5: 2}
    for block in range(2):
        got = lax.ppermute(inner, "region", INNER_SWAP)
        got_outer = lax.ppermute(outer, "region", OUTER_SWAP)
        v, t, p, inner = call(
            bind(near_kernel, INNER_FIRST if block == 0 else INNER, 0, True),
            state + (inner_struct,), [VM] * 6, [d_scratch], aliases=alias,
        )(own, edge, got, v, t, p)
        got = lax.ppermute(inner, "region", INNER_SWAP)
        if block == 0:
            v, t, p, inner = call(
                bind(near_kernel, INNER, 3, True), state + (inner_struct,), [VM] * 6,
                [d_scratch], aliases=alias,
            )(own, edge, got, v, t, p)
            v, t, p, outer = call(
                bind(far_kernel, OUTER_FIRST), state + (struct(plane_count(OUTER), DEPTH, 128),),
                [VM] * 6, [d_scratch], aliases=alias,
            )(own, edge, got_outer, v, t, p)
        else:
            v, t, p = call(
                bind(near_kernel, INNER, 3, False), state, [VM] * 6, [d_scratch],
                aliases=alias,
            )(own, edge, got, v, t, p)
    v, t, p, packet = call(
        bind(station_kernel, OUTER), state + (struct(8, 128),), [SM] + [VM] * 9,
        [d_scratch, pltpu.VMEM((16, 128), jnp.float32)], aliases={7: 0, 8: 1, 9: 2},
    )(station_count, observed, station_weight.reshape(1, S), station_cell.reshape(1, S),
      own, edge, got_outer, v, t, p)
    here = lax.all_gather(packet, "region")
    got_first = lax.ppermute(here, "tile", pairs(0))
    got_second = lax.ppermute(here, "tile", pairs(1))
    _, out, used, profile_rows, own_part = call(
        stress_out_kernel,
        (state[1], struct(9 * size, 128), jax.ShapeDtypeStruct((8, 128), jnp.int32),
         struct(3, NZ, 128), struct(3 * CX, CY)), [SM] * 3 + [VM] * 6,
        [d_scratch, pltpu.VMEM((6 * size, 128), jnp.float32), pltpu.SemaphoreType.DMA],
        out_specs=[VM, HB, VM, VM, VM], aliases={7: 0},
    )(influence, influence_count, depth_profile, own, edge, here, v, t, p)
    out, = call(
        increment_kernel, (struct(9 * size, 128),), [VM] * 6 + [HB],
        [pltpu.VMEM((3 * size, 128), jnp.float32), pltpu.SemaphoreType.DMA], out_specs=[HB],
        aliases={6: 0},
    )(v, got_first, got_second, used, profile_rows, own_part, out)
    return out.reshape(9, NZ, CX, CY)


def solution(mesh):
    in_specs = (
        P(None, None, "region", "tile"),
        P(None, "region", "tile"),
        P(None, "region", "tile"),
        P(None, "region", "tile"),
        P(None, ("region", "tile")),
        P(("region", "tile")),
        P(),
        P(("region", "tile")),
        P(("region", "tile")),
        P(("region", "tile"), None),
        P(("region", "tile")),
    )
    out_specs = P(None, None, "region", "tile")
    return jax.shard_map(
        per_device, mesh=mesh, in_specs=in_specs, out_specs=out_specs, check_vma=False
    )
```

```python
import jax
import jax.numpy as jnp
import numpy as np
from jax import lax
from jax.experimental import pallas as pl
from jax.experimental.pallas import tpu as pltpu
from jax.sharding import PartitionSpec as P

DT = 0.15 / 24.0

CX, CY, NZ = 16, 128, 32
S, LIST = 32, 64
GROUPS = 4
HALF = 16
WIDE = 12
PACK = NZ // GROUPS
DEPTH = NZ + PACK
LOW = 6
PLANES = CX + 2 * LOW
ZROWS = 72

VX, VY, VZ = range(3)
SXX, SYY, SZZ, SXY, SXZ, SYZ = range(6)
Z_STRESS = (SZZ, SXZ, SYZ)

OUTER = [("t", f, 6) for f in (SXX, SXY, SXZ)] + [("t", f, 5) for f in (SYY, SYZ, SZZ)] + [
    ("v", f, 5) for f in range(3)]
OUTER_FIRST = OUTER + [("p", 0, 5), ("p", 1, 3), ("p", 2, 3)]
INNER = [("t", f, 3) for f in (SXX, SXY, SXZ)] + [("t", f, 2) for f in (SYY, SYZ, SZZ)] + [
    ("v", f, 2) for f in range(3)]
INNER_FIRST = INNER + [("p", 0, 2)]

VMEM_BYTES = 8 * 2 ** 20


def is_odd():
    return lax.rem(lax.axis_index("region"), 2) > 0


def plane_count(items):
    return sum(d for _, _, d in items)


def lanes(rows):
    return lax.broadcasted_iota(jnp.int32, (rows, 128), 1)


def band_matrices():
    taps = {0: ((-1, 1), (0, -27), (1, 27), (2, -1)), 1: ((-2, 1), (-1, -27), (0, 27), (1, -1))}
    own = np.zeros((2, GROUPS, 256, 128), np.float32)
    halo = np.zeros((2, 640, 128), np.float32)
    for k in range(2):
        for offset, coef in taps[k]:
            for g in range(GROUPS):
                for lane in range(128):
                    y = lane + offset
                    if 0 <= y < CY:
                        own[k, g, y, lane] += coef
                    else:
                        own[k, g, 128 + 32 * g + HALF + (y if y < 0 else y - CY), lane] += coef
                for spot in range(32):
                    to = spot + offset
                    out = 32 * g + spot
                    if not 0 <= to < 32:
                        continue
                    if (spot < HALF) == (to < HALF):
                        halo[k, 512 + 32 * g + to, out] += coef
                    elif spot < HALF:
                        halo[k, 128 * g + to - HALF, out] += coef
                    else:
                        halo[k, 128 * g + CY + to - HALF, out] += coef
    return own, halo


def two_terms(value):
    high = value.astype(jnp.bfloat16)
    return high, (value - high.astype(jnp.float32)).astype(jnp.bfloat16)


def y_differences(items, count, forward, own_ref, halo_ref, out_ref):
    k = 0 if forward else 1
    even = count + count % 2

    def rows(at):
        return jnp.concatenate(
            [ref[f, x + j, at:at + 8, :] for ref, f, x, _ in items for j in range(even)], axis=0)

    parts = [two_terms(rows(8 + 8 * g)) for g in range(GROUPS)] + [two_terms(rows(56))]

    def product(lhs, rhs):
        return jnp.dot(lhs, rhs, preferred_element_type=jnp.float32)

    for g in range(GROUPS + 1):
        total = 0.0
        for term in range(2):
            if g < GROUPS:
                lhs = jnp.concatenate([parts[g][term], parts[GROUPS][term]], axis=1)
                total += product(lhs, own_ref[k, g])
            else:
                lhs = jnp.concatenate([parts[n][term] for n in range(GROUPS + 1)], axis=1)
                total += product(lhs, halo_ref[k])
        for n, (_, _, _, slot) in enumerate(items):
            for j in range(count):
                r = 8 * (n * even + j)
                out_ref[slot, j, 8 * g:8 * g + 8, :] = total[r:r + 8]


def load(ref, f, x, dz=0):
    return jnp.concatenate(
        [ref[f, x, 8 + dz:8 + NZ + dz, :], ref[f, x, 56 + dz:64 + dz, :]], axis=0)


def store(ref, f, x, value):
    ref[f, x, 8:8 + NZ, :] = value[:NZ]
    ref[f, x, 56:64, :] = value[NZ:]


def pad_halo(ref, f, x):
    lane = lanes(PACK)
    halo = ref[f, x, 56:64, :]
    ref[f, x, 48:56, :] = jnp.where(lane < 32, 0.0, pltpu.roll(halo, 32, 1))
    ref[f, x, 64:72, :] = jnp.where(lane >= 96, 0.0, pltpu.roll(halo, 96, 1))


def combine(m1, c0, p1, p2):
    return 27.0 * (p1 - c0) - (p2 - m1)


def diff_x(ref, f, x, forward):
    first = -1 if forward else -2
    return combine(*[load(ref, f, x + first + k) for k in range(4)])


def diff_z(ref, f, x, forward):
    first = -1 if forward else -2
    return combine(*[load(ref, f, x, first + k) for k in range(4)])


def velocity_pass(v_ref, t_ref, p_ref, own_ref, halo_ref, d_ref, x_first, y_first, count):
    xa, ya = x_first + LOW, y_first + LOW
    y_differences([(t_ref, SXY, xa, 0), (t_ref, SYZ, ya, 2)], count, False, own_ref, halo_ref, d_ref)
    y_differences([(t_ref, SYY, ya, 1)], count, True, own_ref, halo_ref, d_ref)

    def body(j, _):
        x = xa + j
        force = diff_x(t_ref, SXX, x, True) + d_ref[0, j] + diff_z(t_ref, SXZ, x, False)
        store(v_ref, VX, x, load(v_ref, VX, x) + p_ref[0, x] * force)
        x = ya + j
        b = p_ref[0, x]
        force = diff_x(t_ref, SXY, x, False) + d_ref[1, j] + diff_z(t_ref, SYZ, x, False)
        store(v_ref, VY, x, load(v_ref, VY, x) + b * force)
        force = diff_x(t_ref, SXZ, x, False) + d_ref[2, j] + diff_z(t_ref, SZZ, x, True)
        store(v_ref, VZ, x, load(v_ref, VZ, x) + b * force)
        return 0

    lax.fori_loop(0, count, body, 0)
    for j in range(count):
        pad_halo(v_ref, VX, xa + j)
        pad_halo(v_ref, VY, ya + j)
        pad_halo(v_ref, VZ, ya + j)


def stress_pass(v_ref, t_ref, p_ref, own_ref, halo_ref, d_ref, first, count, pads=True):
    a = first + LOW
    y_differences([(v_ref, VX, a, 0), (v_ref, VZ, a, 2)], count, True, own_ref, halo_ref, d_ref)
    y_differences([(v_ref, VY, a, 1)], count, False, own_ref, halo_ref, d_ref)

    def body(j, _):
        x = a + j
        lame, mu = p_ref[1, x], p_ref[2, x]
        grad_x = diff_x(v_ref, VX, x, False)
        grad_y = d_ref[1, j]
        grad_z = diff_z(v_ref, VZ, x, False)
        spread = lame * (grad_x + grad_y + grad_z)
        double = mu + mu
        rates = (
            (SXX, double * grad_x + spread),
            (SYY, double * grad_y + spread),
            (SZZ, double * grad_z + spread),
            (SXY, mu * (d_ref[0, j] + diff_x(v_ref, VY, x, True))),
            (SXZ, mu * (diff_z(v_ref, VX, x, True) + diff_x(v_ref, VZ, x, True))),
            (SYZ, mu * (diff_z(v_ref, VY, x, True) + d_ref[2, j])),
        )
        for f, rate in rates:
            store(t_ref, f, x, load(t_ref, f, x) + rate)
        return 0

    lax.fori_loop(0, count, body, 0)
    if pads:
        for j in range(count):
            for f in Z_STRESS:
                pad_halo(t_ref, f, a + j)


def planes_of(items, odd, inner, out):
    for kind, f, depth in items:
        low, high = (0, CX - depth) if out else (-depth, CX)
        row = jnp.where(odd, low, high) if inner else jnp.where(odd, high, low)
        for k in range(depth):
            yield kind, f, row + LOW + k


def take_halo(items, odd, inner, read, v_ref, t_ref, p_ref):
    padded = []
    for n, (kind, f, x) in enumerate(planes_of(items, odd, inner, False)):
        if kind == "p":
            p_ref[f, x] = read(n)
        else:
            ref = v_ref if kind == "v" else t_ref
            store(ref, f, x, read(n))
            if kind == "v" or f in Z_STRESS:
                padded.append((ref, f, x))
    for ref, f, x in padded:
        pad_halo(ref, f, x)


def give_halo(items, odd, inner, send_ref, v_ref, t_ref, p_ref, own=True, halo=True):
    for n, (kind, f, x) in enumerate(planes_of(items, odd, inner, True)):
        ref = {"v": v_ref, "t": t_ref, "p": p_ref}[kind]
        a, b = (0, NZ) if kind == "p" else (8, 56)
        if own:
            send_ref[n, 0:NZ] = ref[f, x, a:a + NZ, :]
        if halo:
            at = NZ if own else 0
            send_ref[n, at:at + PACK] = ref[f, x, b:b + PACK, :]


def pieces():
    out = []
    for u in range(8):
        for v in range(3):
            start = WIDE * u - 32 * v
            a, b = max(0, start), min(32, start + WIDE)
            if a < b:
                out.append((u, v, start, a, b))
    return out


PIECES = pieces()


def fetch(refs, buf_ref, sems):
    size = NZ * CX
    waits = []
    for a in range(12):
        src = refs[0].at[pl.ds(a * size, size)] if a < 9 else refs[a - 8]
        waits.append(pltpu.make_async_copy(src, buf_ref.at[pl.ds(a * size, size)], sems.at[a]))
    for copy in waits:
        copy.start()
    return waits


def low_side(first):
    odd = lax.rem(lax.axis_index("tile"), 2) > 0
    return jnp.where(odd, HALF - WIDE, HALF) if first else jnp.where(odd, HALF, HALF - WIDE)


def pack_units(units, at, put):
    spot = lanes(PACK) % 32
    parts = [None] * 3
    for u, v, start, lo, hi in PIECES:
        keep = (spot >= lo) & (spot < hi)
        moved = pltpu.roll(units[u], lax.rem(start - at + 256, 128), 1)
        parts[v] = moved if parts[v] is None else jnp.where(keep, moved, parts[v])
    for v in range(3):
        put(v, parts[v])


def edge_kernel(fields_ref, buoy_ref, lame_ref, mu_ref, first_ref, second_ref, token_ref, buf_ref,
                sems):
    size = NZ * CX
    lane = lanes(PACK)
    token_ref[...] = jnp.zeros((8, 128), jnp.float32)
    for a, copy in enumerate(fetch((fields_ref, buoy_ref, lame_ref, mu_ref), buf_ref, sems)):
        copy.wait()
        for block in range(2):
            units = []
            for u in range(8):
                out = None
                for g in range(GROUPS):
                    row = a * size + (8 * g + u) * CX + 8 * block
                    moved = pltpu.roll(buf_ref[row:row + 8, :], (HALF + 32 * g) % 128, 1)
                    out = moved if g == 0 else jnp.where(lane >= 32 * g, moved, out)
                units.append(out)
            for ref, is_first in ((first_ref, True), (second_ref, False)):
                def put(v, value):
                    ref[a, 3 * block + v] = value
                pack_units(units, 2 * HALF - WIDE - low_side(is_first), put)


def unpack_units(got_ref, a, block, at, under, put):
    spot = lanes(PACK) % 32
    for u in range(8):
        value = under(u)
        for w, v, start, lo, hi in PIECES:
            if w == u:
                keep = (spot >= lo - start + at) & (spot < hi - start + at)
                moved = pltpu.roll(got_ref[a, 3 * block + v], lax.rem(at - start + 256, 128), 1)
                value = jnp.where(keep, moved, value)
        put(u, value)


def first_halo_kernel(got_ref, half_ref):
    at = low_side(True)

    def body(a, _):
        for block in range(2):
            def put(u, value):
                half_ref[a, block, u] = value
            unpack_units(got_ref, a, block, at, lambda u: jnp.zeros((PACK, 128), jnp.float32), put)
        return 0

    lax.fori_loop(0, 12, body, 0)


def build_kernel(fields_ref, buoy_ref, lame_ref, mu_ref, after_ref, v_ref, t_ref, p_ref, outer_ref):
    size = NZ * CX
    zero = jnp.zeros((8, 128), jnp.float32)

    def clear(x, _):
        for ref, f in [(v_ref, f) for f in range(3)] + [(t_ref, f) for f in Z_STRESS]:
            ref[f, x, 0:8, :] = zero
            ref[f, x, 40:48, :] = zero
        return 0

    lax.fori_loop(0, PLANES, clear, 0)
    for a in range(12):
        ref, first = (fields_ref, a * size) if a < 9 else ((buoy_ref, lame_ref, mu_ref)[a - 9], 0)
        for x in range(CX):
            value = ref[pl.ds(first + x, NZ, stride=CX), :]
            if a < 3:
                v_ref[a, x + LOW, 8:8 + NZ, :] = value
            elif a < 9:
                t_ref[a - 3, x + LOW, 8:8 + NZ, :] = value
            else:
                p_ref[a - 9, x + LOW, 0:NZ, :] = DT * value
    give_halo(OUTER_FIRST, is_odd(), False, outer_ref, v_ref, t_ref, p_ref, halo=False)


def halo_kernel(got_ref, half_ref, v_in, t_in, p_in, v_ref, t_ref, p_ref, outer_ref, inner_ref):
    odd = is_odd()
    at = low_side(False)
    v_rows = v_ref.reshape(3 * PLANES * ZROWS, 128)
    t_rows = t_ref.reshape(6 * PLANES * ZROWS, 128)
    p_rows = p_ref.reshape(3 * PLANES * DEPTH, 128)

    def one(a, f, rows_ref, depth, begin, scale):
        for block in range(2):
            def put(u, value):
                row = (f * PLANES + LOW + 8 * block) * depth + begin + u
                rows_ref[pl.ds(row, 8, stride=depth), :] = scale * value if scale else value
            unpack_units(got_ref, a, block, at, lambda u: half_ref[a, block, u], put)

    for a in range(12):
        if a < 3:
            one(a, a, v_rows, ZROWS, 56, None)
        elif a < 9:
            one(a, a - 3, t_rows, ZROWS, 56, None)
        else:
            one(a, a - 9, p_rows, DEPTH, NZ, DT)
    give_halo(OUTER_FIRST, odd, False, outer_ref, v_ref, t_ref, p_ref, own=False)
    give_halo(INNER_FIRST, odd, True, inner_ref, v_ref, t_ref, p_ref)


def pad_own(v_ref, t_ref):
    def pads(x, _):
        for f in range(3):
            pad_halo(v_ref, f, x)
        for f in Z_STRESS:
            pad_halo(t_ref, f, x)
        return 0

    lax.fori_loop(LOW, LOW + CX, pads, 0)


def near_kernel(items, back, sends, own_ref, halo_ref, got_ref, v_in, t_in, p_in, *refs):
    if sends:
        v_ref, t_ref, p_ref, inner_ref, d_ref = refs
    else:
        v_ref, t_ref, p_ref, d_ref = refs
    odd = is_odd()
    if items is INNER_FIRST:
        pad_own(v_ref, t_ref)
    take_halo(items, odd, True, lambda n: got_ref[n], v_ref, t_ref, p_ref)
    mats = (v_ref, t_ref, p_ref, own_ref, halo_ref, d_ref)
    velocity_pass(*mats, jnp.where(odd, -2, back + 1), jnp.where(odd, -1, back + 2), CX - back)
    stress_pass(*mats, jnp.where(odd, 0, back + 3), CX - 3 - back)
    if sends:
        give_halo(INNER, odd, True, inner_ref, v_ref, t_ref, p_ref)


def far_steps(items, last, odd, read, v_ref, t_ref, p_ref, own_ref, halo_ref, d_ref):
    take_halo(items, odd, False, read, v_ref, t_ref, p_ref)
    mats = (v_ref, t_ref, p_ref, own_ref, halo_ref, d_ref)
    velocity_pass(*mats, jnp.where(odd, 14, -5), jnp.where(odd, 15, -4), 6)
    stress_pass(*mats, jnp.where(odd, 13, -3), 6)
    velocity_pass(*mats, jnp.where(odd, 11, -2), jnp.where(odd, 12, -1), 6)
    if not last:
        stress_pass(*mats, jnp.where(odd, 10, 0), 6)


def far_kernel(own_ref, halo_ref, got_own, got_halo, v_in, t_in, p_in, v_ref, t_ref, p_ref,
               outer_ref, d_ref):
    odd = is_odd()
    far_steps(OUTER_FIRST, False, odd, lambda n: jnp.concatenate([got_own[n], got_halo[n]], axis=0),
              v_ref, t_ref, p_ref, own_ref, halo_ref, d_ref)
    give_halo(OUTER, odd, False, outer_ref, v_ref, t_ref, p_ref)


def station_kernel(count_ref, observed_ref, gain_ref, cell_ref, own_ref, halo_ref,
                   got_ref, v_in, t_in, p_in, v_ref, t_ref, p_ref, packet_ref, d_ref, slot_ref):
    odd = is_odd()
    far_steps(OUTER, True, odd, lambda n: got_ref[n], v_ref, t_ref, p_ref, own_ref, halo_ref, d_ref)
    slot_ref[...] = jnp.zeros((16, 128), jnp.float32)
    slot_ref[0:3, 0:S] = observed_ref[...]
    slot_ref[3:4, 0:S] = gain_ref[...]
    slot_ref[4:5, 0:S] = cell_ref[...].astype(jnp.float32)
    cell = slot_ref[4:5, :].astype(jnp.int32)
    cell_x, cell_y = cell // CY, cell % CY
    pick_y = (lax.broadcasted_iota(jnp.int32, (CY, 128), 0) == cell_y).astype(jnp.float32)
    pick_x = lax.broadcasted_iota(jnp.int32, (CX, 128), 0) == cell_x
    live = lanes(1) < count_ref[0]
    gain = slot_ref[3:4, :]
    region, tile = lax.axis_index("region"), lax.axis_index("tile")
    surface = jnp.concatenate(
        [v_ref[c, r + LOW, 8:9, :] for c in range(3) for r in range(CX)], axis=0)
    rows = jnp.dot(surface, pick_y, precision=lax.Precision.HIGHEST,
                   preferred_element_type=jnp.float32)
    for c in range(3):
        picked = jnp.where(pick_x, rows[c * CX:(c + 1) * CX], 0.0)
        sample = jnp.sum(picked, axis=0, keepdims=True)
        slot_ref[8 + c:9 + c, :] = jnp.where(live, gain * (slot_ref[c:c + 1, :] - sample), 0.0)
    slot_ref[11:12, :] = (region * CX + cell_x).astype(jnp.float32)
    slot_ref[12:13, :] = (tile * CY + cell_y).astype(jnp.float32)
    own = jnp.where(lanes(8) < S, slot_ref[8:16, :], 0.0)
    packet_ref[...] = pltpu.roll(own, region * S, 1)


def tile_column(packet_refs, used, cell_x, cell_y):
    packet = packet_refs[0] + packet_refs[1] + packet_refs[2] + packet_refs[3]
    dist_x = cell_x - packet[3:4]
    dist_y = cell_y - packet[4:5]
    along_x = jnp.exp(-(dist_x * dist_x) / (2.0 * (0.5 * CX) ** 2))
    along_y = jnp.exp(-(dist_y * dist_y) / (2.0 * (0.25 * CY) ** 2))
    scaled = jnp.concatenate(
        [jnp.where(used > 0, packet[c:c + 1] * along_x, 0.0) for c in range(3)], axis=0)
    return lax.dot_general(
        scaled, along_y, (((1,), (1,)), ((), ())), precision=lax.Precision.HIGHEST,
        preferred_element_type=jnp.float32)


def cell_places():
    region, tile = lax.axis_index("region"), lax.axis_index("tile")
    cell_x = (lax.broadcasted_iota(jnp.int32, (CX, 128), 0) + region * CX).astype(jnp.float32)
    cell_y = (lax.broadcasted_iota(jnp.int32, (CY, 128), 0) + tile * CY).astype(jnp.float32)
    return cell_x, cell_y


def stress_out_kernel(influence_ref, count_ref, profile_ref, own_ref, halo_ref, here_ref, v_ref,
                      t_in, p_ref, t_ref, out_ref, used_ref, profile_rows, own_part, d_ref, rows_ref,
                      sem):
    odd = is_odd()
    stress_pass(v_ref, t_ref, p_ref, own_ref, halo_ref, d_ref, jnp.where(odd, 10, 0), 6, pads=False)
    size = NZ * CX

    def body(r, _):
        for f in range(6):
            rows_ref[pl.ds(f * size + r, NZ, stride=CX), :] = t_ref[f, r + LOW, 8:8 + NZ, :]
        return 0

    lax.fori_loop(0, CX, body, 0)
    copy = pltpu.make_async_copy(rows_ref, out_ref.at[pl.ds(3 * size, 6 * size)], sem)
    copy.start()
    lane = lanes(8)
    column = lax.broadcasted_iota(jnp.int32, (8, 128), 0) + lax.axis_index("tile") - 1
    slot_id = (lane // S * 32 + column) * S + lane % S
    slot_id = jnp.where((column >= 0) & (column < 32), slot_id, -1)
    used = jnp.zeros((8, 128), jnp.int32)
    for k in range(LIST):
        hit = (slot_id == influence_ref[0, k]) & (k < count_ref[0])
        used = jnp.where(hit, 1, used)
    used_ref[...] = used
    for c in range(3):
        for z in range(NZ):
            profile_rows[c, z:z + 1, :] = jnp.full((1, 128), profile_ref[c, z], jnp.float32)
    own_part[...] = tile_column(here_ref, used[1:2], *cell_places())
    copy.wait()


def increment_kernel(v_ref, first_ref, second_ref, used_ref, profile_rows, own_part, out_in, out_ref,
                     rows_ref, sem):
    odd = lax.rem(lax.axis_index("tile"), 2) > 0
    before = [jnp.where(odd, first_ref[r], second_ref[r]) for r in range(4)]
    after = [jnp.where(odd, second_ref[r], first_ref[r]) for r in range(4)]
    places = cell_places()
    increment = (own_part[...] + tile_column(before, used_ref[0:1], *places)
                 + tile_column(after, used_ref[2:3], *places))
    for c in range(3):
        for r in range(CX):
            value = v_ref[c, r + LOW, 8:8 + NZ, :]
            value = value + profile_rows[c] * increment[c * CX + r:c * CX + r + 1, :]
            rows_ref[pl.ds(c * NZ * CX + r, NZ, stride=CX), :] = value
    copy = pltpu.make_async_copy(rows_ref, out_ref.at[pl.ds(0, 3 * NZ * CX)], sem)
    copy.start()
    copy.wait()


def struct(*shape):
    return jax.ShapeDtypeStruct(shape, jnp.float32)


VM = pl.BlockSpec(memory_space=pltpu.VMEM)
SM = pl.BlockSpec(memory_space=pltpu.SMEM)
HB = pl.BlockSpec(memory_space=pltpu.HBM)


def call(kernel, outs, specs, scratch, out_specs=None, aliases=None, vmem=VMEM_BYTES,
         cost=None):
    return pl.pallas_call(
        kernel, out_shape=outs, in_specs=specs, out_specs=out_specs or [VM] * len(outs),
        scratch_shapes=list(scratch), input_output_aliases=aliases or {}, cost_estimate=cost,
        compiler_params=pltpu.CompilerParams(vmem_limit_bytes=vmem))


def pairs(first):
    return [p for i in range(first, 31, 2) for p in ((i, i + 1), (i + 1, i))]


INNER_SWAP = [(0, 1), (1, 0), (2, 3), (3, 2)]
OUTER_SWAP = [(1, 2), (2, 1)]


def bind(kernel, *first):
    def bound(*refs):
        return kernel(*first, *refs)
    return bound


def per_device(fields, buoyancy, lame_first, shear_modulus, observed, station_weight, depth_profile,
               station_cell, station_count, influence, influence_count):
    own, edge = band_matrices()
    own, edge = jnp.asarray(own, jnp.bfloat16), jnp.asarray(edge, jnp.bfloat16)
    size = NZ * CX
    state = (struct(3, PLANES, ZROWS, 128), struct(6, PLANES, ZROWS, 128),
             struct(3, PLANES, DEPTH, 128))
    given = (fields.reshape(9 * size, CY), buoyancy.reshape(size, CY),
             lame_first.reshape(size, CY), shear_modulus.reshape(size, CY))
    fetched = [pltpu.VMEM((12 * size, 128), jnp.float32), pltpu.SemaphoreType.DMA((12,))]
    packed, edges = struct(12, 6, PACK, 128), struct(12, 2, 8, 8, 128)
    first, second, token = call(edge_kernel, (packed, packed, struct(8, 128)), [HB] * 4, fetched,
                         vmem=62 * 2 ** 20)(*given)
    got_first = lax.ppermute(first, "tile", pairs(0))
    got_second = lax.ppermute(second, "tile", pairs(1))
    planes = plane_count(OUTER_FIRST)
    v, t, p, outer = call(build_kernel, state + (struct(planes, NZ, 128),), [VM] * 5, [],
                          cost=pl.CostEstimate(flops=0, bytes_accessed=10 ** 8, transcendentals=0))(
        *given, token)
    got_own = lax.ppermute(outer, "region", OUTER_SWAP)
    half, = call(first_halo_kernel, (edges,), [VM], [])(got_first)
    v, t, p, outer, inner = call(
        halo_kernel, state + (struct(planes, PACK, 128),
                              struct(plane_count(INNER_FIRST), DEPTH, 128)),
        [VM] * 5, [], aliases={2: 0, 3: 1, 4: 2},
    )(got_second, half, v, t, p)
    inner_struct = struct(plane_count(INNER), DEPTH, 128)
    d_scratch = pltpu.VMEM((3, CX, DEPTH, 128), jnp.float32)
    alias = {3: 0, 4: 1, 5: 2}
    for block in range(2):
        got = lax.ppermute(inner, "region", INNER_SWAP)
        got_outer = lax.ppermute(outer, "region", OUTER_SWAP)
        v, t, p, inner = call(
            bind(near_kernel, INNER_FIRST if block == 0 else INNER, 0, True),
            state + (inner_struct,), [VM] * 6, [d_scratch], aliases=alias,
        )(own, edge, got, v, t, p)
        got = lax.ppermute(inner, "region", INNER_SWAP)
        if block == 0:
            v, t, p, inner = call(
                bind(near_kernel, INNER, 3, True), state + (inner_struct,), [VM] * 6,
                [d_scratch], aliases=alias,
            )(own, edge, got, v, t, p)
            v, t, p, outer = call(
                far_kernel, state + (struct(plane_count(OUTER), DEPTH, 128),),
                [VM] * 7, [d_scratch], aliases={4: 0, 5: 1, 6: 2},
            )(own, edge, got_own, got_outer, v, t, p)
        else:
            v, t, p = call(
                bind(near_kernel, INNER, 3, False), state, [VM] * 6, [d_scratch],
                aliases=alias,
            )(own, edge, got, v, t, p)
    v, t, p, packet = call(
        station_kernel, state + (struct(8, 128),), [SM] + [VM] * 9,
        [d_scratch, pltpu.VMEM((16, 128), jnp.float32)], aliases={7: 0, 8: 1, 9: 2},
    )(station_count, observed, station_weight.reshape(1, S), station_cell.reshape(1, S),
      own, edge, got_outer, v, t, p)
    here = lax.all_gather(packet, "region")
    got_first = lax.ppermute(here, "tile", pairs(0))
    got_second = lax.ppermute(here, "tile", pairs(1))
    _, out, used, profile_rows, own_part = call(
        stress_out_kernel,
        (state[1], struct(9 * size, 128), jax.ShapeDtypeStruct((8, 128), jnp.int32),
         struct(3, NZ, 128), struct(3 * CX, CY)), [SM] * 3 + [VM] * 6,
        [d_scratch, pltpu.VMEM((6 * size, 128), jnp.float32), pltpu.SemaphoreType.DMA],
        out_specs=[VM, HB, VM, VM, VM], aliases={7: 0},
    )(influence, influence_count, depth_profile, own, edge, here, v, t, p)
    out, = call(
        increment_kernel, (struct(9 * size, 128),), [VM] * 6 + [HB],
        [pltpu.VMEM((3 * size, 128), jnp.float32), pltpu.SemaphoreType.DMA], out_specs=[HB],
        aliases={6: 0},
    )(v, got_first, got_second, used, profile_rows, own_part, out)
    return out.reshape(9, NZ, CX, CY)


def solution(mesh):
    in_specs = (
        P(None, None, "region", "tile"),
        P(None, "region", "tile"),
        P(None, "region", "tile"),
        P(None, "region", "tile"),
        P(None, ("region", "tile")),
        P(("region", "tile")),
        P(),
        P(("region", "tile")),
        P(("region", "tile")),
        P(("region", "tile"), None),
        P(("region", "tile")),
    )
    out_specs = P(None, None, "region", "tile")
    return jax.shard_map(
        per_device, mesh=mesh, in_specs=in_specs, out_specs=out_specs, check_vma=False
    )
```

```python
import jax
import jax.numpy as jnp
import numpy as np
from jax import lax
from jax.experimental import pallas as pl
from jax.experimental.pallas import tpu as pltpu
from jax.sharding import PartitionSpec as P

DT = 0.15 / 24.0

CX, CY, NZ = 16, 128, 32
S, LIST = 32, 64
GROUPS = 4
HALF = 16
WIDE = 12
PACK = NZ // GROUPS
DEPTH = NZ + PACK
LOW = 6
PLANES = CX + 2 * LOW
ZROWS = 72

VX, VY, VZ = range(3)
SXX, SYY, SZZ, SXY, SXZ, SYZ = range(6)
Z_STRESS = (SZZ, SXZ, SYZ)

OUTER = [("t", f, 6) for f in (SXX, SXY, SXZ)] + [("t", f, 5) for f in (SYY, SYZ, SZZ)] + [
    ("v", f, 5) for f in range(3)]
OUTER_FIRST = OUTER + [("p", 0, 5), ("p", 1, 3), ("p", 2, 3)]
INNER = [("t", f, 3) for f in (SXX, SXY, SXZ)] + [("t", f, 2) for f in (SYY, SYZ, SZZ)] + [
    ("v", f, 2) for f in range(3)]
INNER_FIRST = INNER + [("p", 0, 2)]

EARLY_FIELDS = 12
SECOND_WIDE = 6

VMEM_BYTES = 8 * 2 ** 20


def is_odd():
    return lax.rem(lax.axis_index("region"), 2) > 0


def plane_count(items):
    return sum(d for _, _, d in items)


def lanes(rows):
    return lax.broadcasted_iota(jnp.int32, (rows, 128), 1)


def band_matrices():
    taps = {0: ((-1, 1), (0, -27), (1, 27), (2, -1)), 1: ((-2, 1), (-1, -27), (0, 27), (1, -1))}
    own = np.zeros((2, GROUPS, 256, 128), np.float32)
    halo = np.zeros((2, 640, 128), np.float32)
    for k in range(2):
        for offset, coef in taps[k]:
            for g in range(GROUPS):
                for lane in range(128):
                    y = lane + offset
                    if 0 <= y < CY:
                        own[k, g, y, lane] += coef
                    else:
                        own[k, g, 128 + 32 * g + HALF + (y if y < 0 else y - CY), lane] += coef
                for spot in range(32):
                    to = spot + offset
                    out = 32 * g + spot
                    if not 0 <= to < 32:
                        continue
                    if (spot < HALF) == (to < HALF):
                        halo[k, 512 + 32 * g + to, out] += coef
                    elif spot < HALF:
                        halo[k, 128 * g + to - HALF, out] += coef
                    else:
                        halo[k, 128 * g + CY + to - HALF, out] += coef
    return own, halo


def two_terms(value):
    high = value.astype(jnp.bfloat16)
    return high, (value - high.astype(jnp.float32)).astype(jnp.bfloat16)


def y_differences(items, count, forward, own_ref, halo_ref, out_ref):
    k = 0 if forward else 1
    even = count + count % 2

    def rows(at):
        return jnp.concatenate(
            [ref[f, x + j, at:at + 8, :] for ref, f, x, _ in items for j in range(even)], axis=0)

    parts = [two_terms(rows(8 + 8 * g)) for g in range(GROUPS)] + [two_terms(rows(56))]

    def product(lhs, rhs):
        return jnp.dot(lhs, rhs, preferred_element_type=jnp.float32)

    for g in range(GROUPS + 1):
        total = 0.0
        for term in range(2):
            if g < GROUPS:
                lhs = jnp.concatenate([parts[g][term], parts[GROUPS][term]], axis=1)
                total += product(lhs, own_ref[k, g])
            else:
                lhs = jnp.concatenate([parts[n][term] for n in range(GROUPS + 1)], axis=1)
                total += product(lhs, halo_ref[k])
        for n, (_, _, _, slot) in enumerate(items):
            for j in range(count):
                r = 8 * (n * even + j)
                out_ref[slot, j, 8 * g:8 * g + 8, :] = total[r:r + 8]


def load(ref, f, x, dz=0):
    return jnp.concatenate(
        [ref[f, x, 8 + dz:8 + NZ + dz, :], ref[f, x, 56 + dz:64 + dz, :]], axis=0)


def store(ref, f, x, value):
    ref[f, x, 8:8 + NZ, :] = value[:NZ]
    ref[f, x, 56:64, :] = value[NZ:]


def pad_halo(ref, f, x):
    lane = lanes(PACK)
    halo = ref[f, x, 56:64, :]
    ref[f, x, 48:56, :] = jnp.where(lane < 32, 0.0, pltpu.roll(halo, 32, 1))
    ref[f, x, 64:72, :] = jnp.where(lane >= 96, 0.0, pltpu.roll(halo, 96, 1))


def combine(m1, c0, p1, p2):
    return 27.0 * (p1 - c0) - (p2 - m1)


def diff_x(ref, f, x, forward):
    first = -1 if forward else -2
    return combine(*[load(ref, f, x + first + k) for k in range(4)])


def diff_z(ref, f, x, forward):
    first = -1 if forward else -2
    return combine(*[load(ref, f, x, first + k) for k in range(4)])


def velocity_pass(v_ref, t_ref, p_ref, own_ref, halo_ref, d_ref, x_first, y_first, count):
    xa, ya = x_first + LOW, y_first + LOW
    y_differences([(t_ref, SXY, xa, 0), (t_ref, SYZ, ya, 2)], count, False, own_ref, halo_ref, d_ref)
    y_differences([(t_ref, SYY, ya, 1)], count, True, own_ref, halo_ref, d_ref)

    def body(j, _):
        x = xa + j
        force = diff_x(t_ref, SXX, x, True) + d_ref[0, j] + diff_z(t_ref, SXZ, x, False)
        store(v_ref, VX, x, load(v_ref, VX, x) + p_ref[0, x] * force)
        x = ya + j
        b = p_ref[0, x]
        force = diff_x(t_ref, SXY, x, False) + d_ref[1, j] + diff_z(t_ref, SYZ, x, False)
        store(v_ref, VY, x, load(v_ref, VY, x) + b * force)
        force = diff_x(t_ref, SXZ, x, False) + d_ref[2, j] + diff_z(t_ref, SZZ, x, True)
        store(v_ref, VZ, x, load(v_ref, VZ, x) + b * force)
        return 0

    lax.fori_loop(0, count, body, 0, unroll=2)
    for j in range(count):
        pad_halo(v_ref, VX, xa + j)
        pad_halo(v_ref, VY, ya + j)
        pad_halo(v_ref, VZ, ya + j)


def stress_pass(v_ref, t_ref, p_ref, own_ref, halo_ref, d_ref, first, count, pads=True):
    a = first + LOW
    y_differences([(v_ref, VX, a, 0), (v_ref, VZ, a, 2)], count, True, own_ref, halo_ref, d_ref)
    y_differences([(v_ref, VY, a, 1)], count, False, own_ref, halo_ref, d_ref)

    def body(j, _):
        x = a + j
        lame, mu = p_ref[1, x], p_ref[2, x]
        grad_x = diff_x(v_ref, VX, x, False)
        grad_y = d_ref[1, j]
        grad_z = diff_z(v_ref, VZ, x, False)
        spread = lame * (grad_x + grad_y + grad_z)
        double = mu + mu
        rates = (
            (SXX, double * grad_x + spread),
            (SYY, double * grad_y + spread),
            (SZZ, double * grad_z + spread),
            (SXY, mu * (d_ref[0, j] + diff_x(v_ref, VY, x, True))),
            (SXZ, mu * (diff_z(v_ref, VX, x, True) + diff_x(v_ref, VZ, x, True))),
            (SYZ, mu * (diff_z(v_ref, VY, x, True) + d_ref[2, j])),
        )
        for f, rate in rates:
            store(t_ref, f, x, load(t_ref, f, x) + rate)
        return 0

    lax.fori_loop(0, count, body, 0, unroll=2)
    if pads:
        for j in range(count):
            for f in Z_STRESS:
                pad_halo(t_ref, f, a + j)


def planes_of(items, odd, inner, out):
    for kind, f, depth in items:
        low, high = (0, CX - depth) if out else (-depth, CX)
        row = jnp.where(odd, low, high) if inner else jnp.where(odd, high, low)
        for k in range(depth):
            yield kind, f, row + LOW + k


def take_halo(items, odd, inner, read, v_ref, t_ref, p_ref):
    padded = []
    for n, (kind, f, x) in enumerate(planes_of(items, odd, inner, False)):
        if kind == "p":
            p_ref[f, x] = read(n)
        else:
            ref = v_ref if kind == "v" else t_ref
            store(ref, f, x, read(n))
            if kind == "v" or f in Z_STRESS:
                padded.append((ref, f, x))
    for ref, f, x in padded:
        pad_halo(ref, f, x)


def give_halo(items, odd, inner, send_ref, v_ref, t_ref, p_ref):
    for n, (kind, f, x) in enumerate(planes_of(items, odd, inner, True)):
        ref = {"v": v_ref, "t": t_ref, "p": p_ref}[kind]
        send_ref[n] = p_ref[f, x] if kind == "p" else load(ref, f, x)


def own_rows(kind, f, x, v_ref, t_ref, p_ref):
    return p_ref[f, x, 0:NZ, :] if kind == "p" else {"v": v_ref, "t": t_ref}[kind][f, x, 8:8 + NZ, :]


def packed_rows(kind, f, x, v_ref, t_ref, p_ref):
    if kind == "p":
        return p_ref[f, x, NZ:DEPTH, :]
    return {"v": v_ref, "t": t_ref}[kind][f, x, 56:64, :]


def give_early(odd, send_ref, *state):
    for n, plane in enumerate(planes_of(OUTER_FIRST[:EARLY_FIELDS], odd, False, True)):
        send_ref[n] = own_rows(*plane, *state)


def give_late(odd, send_ref, *state):
    at = plane_count(OUTER_FIRST)
    for n, plane in enumerate(planes_of(OUTER_FIRST, odd, False, True)):
        send_ref[n] = packed_rows(*plane, *state)
    for plane in planes_of(OUTER_FIRST[EARLY_FIELDS:], odd, False, True):
        rows = own_rows(*plane, *state)
        for k in range(4):
            send_ref[at + k] = rows[8 * k:8 * k + 8]
        at += 4


def read_first(early_ref, late_ref):
    early, planes = plane_count(OUTER_FIRST[:EARLY_FIELDS]), plane_count(OUTER_FIRST)

    def read(n):
        if n < early:
            return jnp.concatenate([early_ref[n], late_ref[n]], axis=0)
        at = planes + 4 * (n - early)
        return jnp.concatenate([late_ref[at + k] for k in range(4)] + [late_ref[n]], axis=0)

    return read


def near_lanes():
    spot = lanes(PACK) % 32
    return (spot >= HALF - SECOND_WIDE) & (spot < HALF + SECOND_WIDE)


def give_second(odd, send_ref, *state):
    planes = list(planes_of(OUTER, odd, False, True))
    for n, plane in enumerate(planes):
        rows = own_rows(*plane, *state)
        for k in range(4):
            send_ref[4 * n + k] = rows[8 * k:8 * k + 8]
    keep = near_lanes()
    for n in range(0, len(planes), 2):
        one, two = (packed_rows(*plane, *state) for plane in planes[n:n + 2])
        send_ref[4 * len(planes) + n // 2] = jnp.where(keep, one, pltpu.roll(two, HALF, 1))


def read_second(got_ref):
    planes = plane_count(OUTER)

    def read(n):
        halo = got_ref[4 * planes + n // 2]
        halo = pltpu.roll(halo, 128 - HALF, 1) if n % 2 else halo
        halo = jnp.where(near_lanes(), halo, 0.0)
        return jnp.concatenate([got_ref[4 * n + k] for k in range(4)] + [halo], axis=0)

    return read


def pieces():
    out = []
    for u in range(8):
        for v in range(3):
            start = WIDE * u - 32 * v
            a, b = max(0, start), min(32, start + WIDE)
            if a < b:
                out.append((u, v, start, a, b))
    return out


PIECES = pieces()


def fetch(refs, buf_ref, sems):
    size = NZ * CX
    waits = []
    for a in range(12):
        src = refs[0].at[pl.ds(a * size, size)] if a < 9 else refs[a - 8]
        waits.append(pltpu.make_async_copy(src, buf_ref.at[pl.ds(a * size, size)], sems.at[a]))
    for copy in waits:
        copy.start()
    return waits


def low_side(first):
    odd = lax.rem(lax.axis_index("tile"), 2) > 0
    return jnp.where(odd, HALF - WIDE, HALF) if first else jnp.where(odd, HALF, HALF - WIDE)


def pack_units(units, at, put):
    spot = lanes(PACK) % 32
    parts = [None] * 3
    for u, v, start, lo, hi in PIECES:
        keep = (spot >= lo) & (spot < hi)
        moved = pltpu.roll(units[u], lax.rem(start - at + 256, 128), 1)
        parts[v] = moved if parts[v] is None else jnp.where(keep, moved, parts[v])
    for v in range(3):
        put(v, parts[v])


def edge_kernel(fields_ref, buoy_ref, lame_ref, mu_ref, first_ref, second_ref, token_ref, buf_ref,
                sems):
    size = NZ * CX
    lane = lanes(PACK)
    token_ref[...] = jnp.zeros((8, 128), jnp.float32)
    for a, copy in enumerate(fetch((fields_ref, buoy_ref, lame_ref, mu_ref), buf_ref, sems)):
        copy.wait()
        for block in range(2):
            units = []
            for u in range(8):
                out = None
                for g in range(GROUPS):
                    row = a * size + (8 * g + u) * CX + 8 * block
                    moved = pltpu.roll(buf_ref[row:row + 8, :], (HALF + 32 * g) % 128, 1)
                    out = moved if g == 0 else jnp.where(lane >= 32 * g, moved, out)
                units.append(out)
            for ref, is_first in ((first_ref, True), (second_ref, False)):
                def put(v, value):
                    ref[a, 3 * block + v] = value
                pack_units(units, 2 * HALF - WIDE - low_side(is_first), put)


def unpack_units(got_ref, a, block, at, under, put):
    spot = lanes(PACK) % 32
    for u in range(8):
        value = under(u)
        for w, v, start, lo, hi in PIECES:
            if w == u:
                keep = (spot >= lo - start + at) & (spot < hi - start + at)
                moved = pltpu.roll(got_ref[a, 3 * block + v], lax.rem(at - start + 256, 128), 1)
                value = jnp.where(keep, moved, value)
        put(u, value)


def first_halo_kernel(got_ref, half_ref):
    at = low_side(True)

    def body(a, _):
        for block in range(2):
            def put(u, value):
                half_ref[a, block, u] = value
            unpack_units(got_ref, a, block, at, lambda u: jnp.zeros((PACK, 128), jnp.float32), put)
        return 0

    lax.fori_loop(0, 12, body, 0)


def build_kernel(fields_ref, buoy_ref, lame_ref, mu_ref, after_ref, v_ref, t_ref, p_ref, outer_ref):
    size = NZ * CX
    zero = jnp.zeros((8, 128), jnp.float32)

    def clear(x, _):
        for ref, f in [(v_ref, f) for f in range(3)] + [(t_ref, f) for f in Z_STRESS]:
            ref[f, x, 0:8, :] = zero
            ref[f, x, 40:48, :] = zero
        return 0

    lax.fori_loop(0, PLANES, clear, 0)
    for a in range(12):
        ref, first = (fields_ref, a * size) if a < 9 else ((buoy_ref, lame_ref, mu_ref)[a - 9], 0)
        for x in range(CX):
            value = ref[pl.ds(first + x, NZ, stride=CX), :]
            if a < 3:
                v_ref[a, x + LOW, 8:8 + NZ, :] = value
            elif a < 9:
                t_ref[a - 3, x + LOW, 8:8 + NZ, :] = value
            else:
                p_ref[a - 9, x + LOW, 0:NZ, :] = DT * value
    give_early(is_odd(), outer_ref, v_ref, t_ref, p_ref)


def halo_kernel(got_ref, half_ref, v_in, t_in, p_in, v_ref, t_ref, p_ref, outer_ref, inner_ref):
    odd = is_odd()
    at = low_side(False)
    v_rows = v_ref.reshape(3 * PLANES * ZROWS, 128)
    t_rows = t_ref.reshape(6 * PLANES * ZROWS, 128)
    p_rows = p_ref.reshape(3 * PLANES * DEPTH, 128)

    def one(a, f, rows_ref, depth, begin, scale):
        for block in range(2):
            def put(u, value):
                row = (f * PLANES + LOW + 8 * block) * depth + begin + u
                rows_ref[pl.ds(row, 8, stride=depth), :] = scale * value if scale else value
            unpack_units(got_ref, a, block, at, lambda u: half_ref[a, block, u], put)

    for a in range(12):
        if a < 3:
            one(a, a, v_rows, ZROWS, 56, None)
        elif a < 9:
            one(a, a - 3, t_rows, ZROWS, 56, None)
        else:
            one(a, a - 9, p_rows, DEPTH, NZ, DT)
    give_late(odd, outer_ref, v_ref, t_ref, p_ref)
    give_halo(INNER_FIRST, odd, True, inner_ref, v_ref, t_ref, p_ref)


def pad_own(v_ref, t_ref):
    def pads(x, _):
        for f in range(3):
            pad_halo(v_ref, f, x)
        for f in Z_STRESS:
            pad_halo(t_ref, f, x)
        return 0

    lax.fori_loop(LOW, LOW + CX, pads, 0)


def near_step(items, back, odd, read, v_ref, t_ref, p_ref, own_ref, halo_ref, d_ref):
    take_halo(items, odd, True, read, v_ref, t_ref, p_ref)
    mats = (v_ref, t_ref, p_ref, own_ref, halo_ref, d_ref)
    velocity_pass(*mats, jnp.where(odd, -2, back + 1), jnp.where(odd, -1, back + 2), CX - back)
    stress_pass(*mats, jnp.where(odd, 0, back + 3), CX - 3 - back)


def near_kernel(items, back, gots, gives, own_ref, halo_ref, *refs):
    got_refs, refs = refs[:gots], refs[gots + 3:]
    v_ref, t_ref, p_ref = refs[:3]
    send_refs, d_ref = refs[3:3 + gives], refs[-1]
    odd = is_odd()
    if items is INNER_FIRST:
        pad_own(v_ref, t_ref)

    def read(n):
        part = plane_count(INNER[:4])
        return got_refs[0][n] if gots == 1 or n < part else got_refs[1][n - part]

    near_step(items, back, odd, read, v_ref, t_ref, p_ref, own_ref, halo_ref, d_ref)
    if gives == 1:
        give_halo(INNER, odd, True, send_refs[0], v_ref, t_ref, p_ref)
    else:
        give_halo(INNER[:4], odd, True, send_refs[0], v_ref, t_ref, p_ref)
        give_halo(INNER[4:], odd, True, send_refs[1], v_ref, t_ref, p_ref)


def stress_half(first, t_ref, out_ref, rows_ref, sem):
    flat = rows_ref.reshape(6 * NZ * 8, 128)

    def body(r, _):
        for f in range(6):
            flat[pl.ds(f * NZ * 8 + r, NZ, stride=8), :] = t_ref[f, first + r + LOW, 8:8 + NZ, :]
        return 0

    lax.fori_loop(0, 8, body, 0, unroll=2)
    copy = pltpu.make_async_copy(
        rows_ref, out_ref.at[pl.ds(3 * NZ, 6 * NZ), pl.ds(pl.multiple_of(first, 8), 8)], sem)
    copy.start()
    return copy


def last_near_kernel(influence_ref, count_ref, profile_ref, own_ref, halo_ref, got_ref, v_in, t_in,
                     p_in, v_ref, t_ref, p_ref, out_ref, used_ref, profile_rows, d_ref, rows_ref, sem):
    odd = is_odd()
    near_step(INNER, 3, odd, lambda n: got_ref[n], v_ref, t_ref, p_ref, own_ref, halo_ref, d_ref)
    copy = stress_half(jnp.where(odd, 0, 8), t_ref, out_ref, rows_ref, sem)
    lane = lanes(8)
    column = lax.broadcasted_iota(jnp.int32, (8, 128), 0) + lax.axis_index("tile") - 1
    slot_id = (lane // S * 32 + column) * S + lane % S
    slot_id = jnp.where((column >= 0) & (column < 32), slot_id, -1)
    used = jnp.zeros((8, 128), jnp.int32)
    for k in range(LIST):
        hit = (slot_id == influence_ref[0, k]) & (k < count_ref[0])
        used = jnp.where(hit, 1, used)
    used_ref[...] = used
    for c in range(3):
        for z in range(NZ):
            profile_rows[c, z:z + 1, :] = jnp.full((1, 128), profile_ref[c, z], jnp.float32)
    copy.wait()


def far_steps(items, last, odd, read, v_ref, t_ref, p_ref, own_ref, halo_ref, d_ref):
    take_halo(items, odd, False, read, v_ref, t_ref, p_ref)
    mats = (v_ref, t_ref, p_ref, own_ref, halo_ref, d_ref)
    velocity_pass(*mats, jnp.where(odd, 14, -5), jnp.where(odd, 15, -4), 6)
    stress_pass(*mats, jnp.where(odd, 13, -3), 6)
    velocity_pass(*mats, jnp.where(odd, 11, -2), jnp.where(odd, 12, -1), 6)
    if not last:
        stress_pass(*mats, jnp.where(odd, 10, 0), 6)


def far_kernel(own_ref, halo_ref, got_own, got_halo, v_in, t_in, p_in, v_ref, t_ref, p_ref,
               outer_ref, d_ref):
    odd = is_odd()
    far_steps(OUTER_FIRST, False, odd, read_first(got_own, got_halo), v_ref, t_ref, p_ref, own_ref, halo_ref, d_ref)
    give_second(odd, outer_ref, v_ref, t_ref, p_ref)


def station_kernel(count_ref, observed_ref, gain_ref, cell_ref, own_ref, halo_ref,
                   got_ref, v_in, t_in, p_in, v_ref, t_ref, p_ref, packet_ref, d_ref, slot_ref):
    odd = is_odd()
    far_steps(OUTER, True, odd, read_second(got_ref), v_ref, t_ref, p_ref, own_ref, halo_ref, d_ref)
    slot_ref[...] = jnp.zeros((16, 128), jnp.float32)
    slot_ref[0:3, 0:S] = observed_ref[...]
    slot_ref[3:4, 0:S] = gain_ref[...]
    slot_ref[4:5, 0:S] = cell_ref[...].astype(jnp.float32)
    cell = slot_ref[4:5, :].astype(jnp.int32)
    cell_x, cell_y = cell // CY, cell % CY
    pick_y = (lax.broadcasted_iota(jnp.int32, (CY, 128), 0) == cell_y).astype(jnp.float32)
    pick_x = lax.broadcasted_iota(jnp.int32, (CX, 128), 0) == cell_x
    live = lanes(1) < count_ref[0]
    gain = slot_ref[3:4, :]
    region, tile = lax.axis_index("region"), lax.axis_index("tile")
    surface = jnp.concatenate(
        [v_ref[c, r + LOW, 8:9, :] for c in range(3) for r in range(CX)], axis=0)
    rows = jnp.dot(surface, pick_y, precision=lax.Precision.HIGHEST,
                   preferred_element_type=jnp.float32)
    for c in range(3):
        picked = jnp.where(pick_x, rows[c * CX:(c + 1) * CX], 0.0)
        sample = jnp.sum(picked, axis=0, keepdims=True)
        slot_ref[8 + c:9 + c, :] = jnp.where(live, gain * (slot_ref[c:c + 1, :] - sample), 0.0)
    slot_ref[11:12, :] = (region * CX + cell_x).astype(jnp.float32)
    slot_ref[12:13, :] = (tile * CY + cell_y).astype(jnp.float32)
    own = jnp.where(lanes(8) < S, slot_ref[8:16, :], 0.0)
    packet_ref[...] = pltpu.roll(own, region * S, 1)


def tile_column(packet_refs, used, cell_x, cell_y):
    packet = packet_refs[0] + packet_refs[1] + packet_refs[2] + packet_refs[3]
    dist_x = cell_x - packet[3:4]
    dist_y = cell_y - packet[4:5]
    along_x = jnp.exp(-(dist_x * dist_x) / (2.0 * (0.5 * CX) ** 2))
    along_y = jnp.exp(-(dist_y * dist_y) / (2.0 * (0.25 * CY) ** 2))
    scaled = jnp.concatenate(
        [jnp.where(used > 0, packet[c:c + 1] * along_x, 0.0) for c in range(3)], axis=0)
    return lax.dot_general(
        scaled, along_y, (((1,), (1,)), ((), ())), precision=lax.Precision.HIGHEST,
        preferred_element_type=jnp.float32)


def cell_places():
    region, tile = lax.axis_index("region"), lax.axis_index("tile")
    cell_x = (lax.broadcasted_iota(jnp.int32, (CX, 128), 0) + region * CX).astype(jnp.float32)
    cell_y = (lax.broadcasted_iota(jnp.int32, (CY, 128), 0) + tile * CY).astype(jnp.float32)
    return cell_x, cell_y


def stress_out_kernel(own_ref, halo_ref, here_ref, used_ref, v_ref, t_in, p_ref, out_in, t_ref,
                      out_ref, own_part, d_ref, rows_ref, sem):
    odd = is_odd()
    stress_pass(v_ref, t_ref, p_ref, own_ref, halo_ref, d_ref, jnp.where(odd, 10, 0), 6, pads=False)
    copy = stress_half(jnp.where(odd, 8, 0), t_ref, out_ref, rows_ref, sem)
    own_part[...] = tile_column(here_ref, used_ref[1:2], *cell_places())
    copy.wait()


def increment_kernel(v_ref, first_ref, second_ref, used_ref, profile_rows, own_part, out_in, out_ref,
                     rows_ref, sems):
    odd = lax.rem(lax.axis_index("tile"), 2) > 0
    before = [jnp.where(odd, first_ref[r], second_ref[r]) for r in range(4)]
    after = [jnp.where(odd, second_ref[r], first_ref[r]) for r in range(4)]
    places = cell_places()
    increment = (own_part[...] + tile_column(before, used_ref[0:1], *places)
                 + tile_column(after, used_ref[2:3], *places))
    flat = rows_ref.reshape(3 * NZ * CX, 128)
    copies = []
    for c in range(3):
        for r in range(CX):
            value = v_ref[c, r + LOW, 8:8 + NZ, :]
            value = value + profile_rows[c] * increment[c * CX + r:c * CX + r + 1, :]
            flat[pl.ds(c * NZ * CX + r, NZ, stride=CX), :] = value
        part = pl.ds(c * NZ, NZ)
        copies.append(pltpu.make_async_copy(rows_ref.at[part], out_ref.at[part], sems.at[c]))
        copies[c].start()
    for copy in copies:
        copy.wait()


def struct(*shape):
    return jax.ShapeDtypeStruct(shape, jnp.float32)


VM = pl.BlockSpec(memory_space=pltpu.VMEM)
SM = pl.BlockSpec(memory_space=pltpu.SMEM)
HB = pl.BlockSpec(memory_space=pltpu.HBM)


def call(kernel, outs, specs, scratch, out_specs=None, aliases=None, vmem=VMEM_BYTES,
         cost=None):
    return pl.pallas_call(
        kernel, out_shape=outs, in_specs=specs, out_specs=out_specs or [VM] * len(outs),
        scratch_shapes=list(scratch), input_output_aliases=aliases or {}, cost_estimate=cost,
        compiler_params=pltpu.CompilerParams(vmem_limit_bytes=vmem))


def pairs(first):
    return [p for i in range(first, 31, 2) for p in ((i, i + 1), (i + 1, i))]


INNER_SWAP = [(0, 1), (1, 0), (2, 3), (3, 2)]
OUTER_SWAP = [(1, 2), (2, 1)]


FREE = pl.CostEstimate(flops=1024, bytes_accessed=1024, transcendentals=0)


def bind(kernel, *first):
    def bound(*refs):
        return kernel(*first, *refs)
    return bound


def per_device(fields, buoyancy, lame_first, shear_modulus, observed, station_weight, depth_profile,
               station_cell, station_count, influence, influence_count):
    own, edge = band_matrices()
    own, edge = jnp.asarray(own, jnp.bfloat16), jnp.asarray(edge, jnp.bfloat16)
    size = NZ * CX
    state = (struct(3, PLANES, ZROWS, 128), struct(6, PLANES, ZROWS, 128),
             struct(3, PLANES, DEPTH, 128))
    given = (fields.reshape(9 * size, CY), buoyancy.reshape(size, CY),
             lame_first.reshape(size, CY), shear_modulus.reshape(size, CY))
    fetched = [pltpu.VMEM((12 * size, 128), jnp.float32), pltpu.SemaphoreType.DMA((12,))]
    packed, edges = struct(12, 6, PACK, 128), struct(12, 2, 8, 8, 128)
    first, second, token = call(edge_kernel, (packed, packed, struct(8, 128)), [HB] * 4, fetched,
                         vmem=62 * 2 ** 20)(*given)
    got_first = lax.ppermute(first, "tile", pairs(0))
    got_second = lax.ppermute(second, "tile", pairs(1))
    early, planes = plane_count(OUTER_FIRST[:EARLY_FIELDS]), plane_count(OUTER_FIRST)
    v, t, p, outer = call(build_kernel, state + (struct(early, NZ, 128),), [VM] * 5, [],
                          cost=pl.CostEstimate(flops=0, bytes_accessed=10 ** 8, transcendentals=0))(
        *given, token)
    got_own = lax.ppermute(outer, "region", OUTER_SWAP)
    half, = call(first_halo_kernel, (edges,), [VM], [])(got_first)
    v, t, p, outer, inner = call(
        halo_kernel, state + (struct(planes + 4 * (planes - early), PACK, 128),
                              struct(plane_count(INNER_FIRST), DEPTH, 128)),
        [VM] * 5, [], aliases={2: 0, 3: 1, 4: 2},
    )(got_second, half, v, t, p)
    inner_struct = struct(plane_count(INNER), DEPTH, 128)
    d_scratch = pltpu.VMEM((3, CX, DEPTH, 128), jnp.float32)
    alias = {3: 0, 4: 1, 5: 2}
    result = struct(9 * NZ, CX, 128)
    for block in range(2):
        got = lax.ppermute(inner, "region", INNER_SWAP)
        got_outer = lax.ppermute(outer, "region", OUTER_SWAP)
        split = 2 if block == 0 else 1
        parts = (INNER[:4], INNER[4:]) if block == 0 else (INNER,)
        v, t, p, *inner = call(
            bind(near_kernel, INNER_FIRST if block == 0 else INNER, 0, 1, split),
            state + tuple(struct(plane_count(part), DEPTH, 128) for part in parts), [VM] * 6,
            [d_scratch], aliases=alias, cost=FREE,
        )(own, edge, got, v, t, p)
        got = [lax.ppermute(part, "region", INNER_SWAP) for part in inner]
        if block == 0:
            v, t, p, inner = call(
                bind(near_kernel, INNER, 3, 2, 1), state + (inner_struct,), [VM] * 7,
                [d_scratch], aliases={4: 0, 5: 1, 6: 2}, cost=FREE,
            )(own, edge, *got, v, t, p)
            v, t, p, outer = call(
                far_kernel, state + (struct(4 * plane_count(OUTER) + plane_count(OUTER) // 2, 8, 128),),
                [VM] * 7, [d_scratch], aliases={4: 0, 5: 1, 6: 2},
            )(own, edge, got_own, got_outer, v, t, p)
        else:
            v, t, p, out, used, profile_rows = call(
                last_near_kernel,
                state + (result, jax.ShapeDtypeStruct((8, 128), jnp.int32), struct(3, NZ, 128)),
                [SM] * 3 + [VM] * 6,
                [d_scratch, pltpu.VMEM((6 * NZ, 8, 128), jnp.float32), pltpu.SemaphoreType.DMA],
                out_specs=[VM] * 3 + [HB] + [VM] * 2, aliases={6: 0, 7: 1, 8: 2},
            )(influence, influence_count, depth_profile, own, edge, *got, v, t, p)
    v, t, p, packet = call(
        station_kernel, state + (struct(8, 128),), [SM] + [VM] * 9,
        [d_scratch, pltpu.VMEM((16, 128), jnp.float32)], aliases={7: 0, 8: 1, 9: 2},
    )(station_count, observed, station_weight.reshape(1, S), station_cell.reshape(1, S),
      own, edge, got_outer, v, t, p)
    here = lax.all_gather(packet, "region")
    got_first = lax.ppermute(here, "tile", pairs(0))
    got_second = lax.ppermute(here, "tile", pairs(1))
    _, out, own_part = call(
        stress_out_kernel, (state[1], result, struct(3 * CX, CY)), [VM] * 7 + [HB],
        [d_scratch, pltpu.VMEM((6 * NZ, 8, 128), jnp.float32), pltpu.SemaphoreType.DMA],
        out_specs=[VM, HB, VM], aliases={5: 0, 7: 1},
    )(own, edge, here, used, v, t, p, out)
    out, = call(
        increment_kernel, (result,), [VM] * 6 + [HB],
        [pltpu.VMEM((3 * NZ, CX, 128), jnp.float32), pltpu.SemaphoreType.DMA((3,))],
        out_specs=[HB], aliases={6: 0},
    )(v, got_first, got_second, used, profile_rows, own_part, out)
    return out.reshape(9, NZ, CX, CY)


def solution(mesh):
    in_specs = (
        P(None, None, "region", "tile"),
        P(None, "region", "tile"),
        P(None, "region", "tile"),
        P(None, "region", "tile"),
        P(None, ("region", "tile")),
        P(("region", "tile")),
        P(),
        P(("region", "tile")),
        P(("region", "tile")),
        P(("region", "tile"), None),
        P(("region", "tile")),
    )
    out_specs = P(None, None, "region", "tile")
    return jax.shard_map(
        per_device, mesh=mesh, in_specs=in_specs, out_specs=out_specs, check_vma=False
    )
```

```python
import jax
import jax.numpy as jnp
import numpy as np
from jax import lax
from jax.experimental import pallas as pl
from jax.experimental.pallas import tpu as pltpu
from jax.sharding import PartitionSpec as P

DT = 0.15 / 24.0

CX, CY, NZ = 16, 128, 32
S, LIST = 32, 64
GROUPS = 4
HALF = 16
WIDE = 12
PACK = NZ // GROUPS
DEPTH = NZ + PACK
LOW = 6
PLANES = CX + 2 * LOW
ZROWS = 72

VX, VY, VZ = range(3)
SXX, SYY, SZZ, SXY, SXZ, SYZ = range(6)
Z_STRESS = (SZZ, SXZ, SYZ)

OUTER = [("t", f, 6) for f in (SXX, SXY, SXZ)] + [("t", f, 5) for f in (SYY, SYZ, SZZ)] + [
    ("v", f, 5) for f in range(3)]
OUTER_FIRST = OUTER + [("p", 0, 5), ("p", 1, 3), ("p", 2, 3)]
INNER = [("t", f, 3) for f in (SXX, SXY, SXZ)] + [("t", f, 2) for f in (SYY, SYZ, SZZ)] + [
    ("v", f, 2) for f in range(3)]
INNER_FIRST = INNER + [("p", 0, 2)]

EARLY_FIELDS = 12
SECOND_WIDE = 6

VMEM_BYTES = 8 * 2 ** 20


def is_odd():
    return lax.rem(lax.axis_index("region"), 2) > 0


def plane_count(items):
    return sum(d for _, _, d in items)


def lanes(rows):
    return lax.broadcasted_iota(jnp.int32, (rows, 128), 1)


def band_matrices():
    taps = {0: ((-1, 1), (0, -27), (1, 27), (2, -1)), 1: ((-2, 1), (-1, -27), (0, 27), (1, -1))}
    band = np.zeros((2, GROUPS, 256, 256), np.float32)
    for k in range(2):
        for offset, coef in taps[k]:
            for g in range(GROUPS):
                for lane in range(128):
                    y = lane + offset
                    if 0 <= y < CY:
                        band[k, g, y, lane] += coef
                    else:
                        band[k, g, 128 + 32 * g + HALF + (y if y < 0 else y - CY), lane] += coef
                for spot in range(32):
                    to = spot + offset
                    out = 128 + 32 * g + spot
                    if not 0 <= to < 32:
                        continue
                    if (spot < HALF) == (to < HALF):
                        band[k, g, 128 + 32 * g + to, out] += coef
                    elif spot < HALF:
                        band[k, g, to - HALF, out] += coef
                    else:
                        band[k, g, CY + to - HALF, out] += coef
    return band


def two_terms(value):
    high = value.astype(jnp.bfloat16)
    return high, (value - high.astype(jnp.float32)).astype(jnp.bfloat16)


def y_differences(items, count, forward, band_ref, out_ref):
    even = count + count % 2
    size = 8 * even * len(items)

    def rows(at):
        value = jnp.concatenate(
            [ref[f, x + j, at:at + 8, :] for ref, f, x, _ in items for j in range(even)], axis=0)
        return jnp.concatenate(two_terms(value), axis=0)

    halo = rows(56)
    halo_out = None
    for g in range(GROUPS + 1):
        if g < GROUPS:
            both = jnp.dot(jnp.concatenate([rows(8 + 8 * g), halo], axis=1),
                           band_ref[0 if forward else 1, g], preferred_element_type=jnp.float32)
            total = both[:size, :128] + both[size:, :128]
            part = both[:size, 128:] + both[size:, 128:]
            halo_out = part if g == 0 else halo_out + part
        else:
            total = halo_out
        for n, (_, _, _, slot) in enumerate(items):
            for j in range(count):
                r = 8 * (n * even + j)
                out_ref[slot, j, 8 * g:8 * g + 8, :] = total[r:r + 8]


def load(ref, f, x, dz=0):
    return jnp.concatenate(
        [ref[f, x, 8 + dz:8 + NZ + dz, :], ref[f, x, 56 + dz:64 + dz, :]], axis=0)


def store(ref, f, x, value):
    ref[f, x, 8:8 + NZ, :] = value[:NZ]
    ref[f, x, 56:64, :] = value[NZ:]


def pad_halo(ref, f, x):
    lane = lanes(PACK)
    halo = ref[f, x, 56:64, :]
    ref[f, x, 48:56, :] = jnp.where(lane < 32, 0.0, pltpu.roll(halo, 32, 1))
    ref[f, x, 64:72, :] = jnp.where(lane >= 96, 0.0, pltpu.roll(halo, 96, 1))


def combine(m1, c0, p1, p2):
    return 27.0 * (p1 - c0) - (p2 - m1)


def diff_x(ref, f, x, forward):
    first = -1 if forward else -2
    return combine(*[load(ref, f, x + first + k) for k in range(4)])


def diff_z(ref, f, x, forward):
    first = -1 if forward else -2
    return combine(*[load(ref, f, x, first + k) for k in range(4)])


def velocity_pass(v_ref, t_ref, p_ref, band_ref, d_ref, x_first, y_first, count):
    xa, ya = x_first + LOW, y_first + LOW
    y_differences([(t_ref, SXY, xa, 0), (t_ref, SYZ, ya, 2)], count, False, band_ref, d_ref)
    y_differences([(t_ref, SYY, ya, 1)], count, True, band_ref, d_ref)

    def body(j, _):
        x = xa + j
        force = diff_x(t_ref, SXX, x, True) + d_ref[0, j] + diff_z(t_ref, SXZ, x, False)
        store(v_ref, VX, x, load(v_ref, VX, x) + p_ref[0, x] * force)
        x = ya + j
        b = p_ref[0, x]
        force = diff_x(t_ref, SXY, x, False) + d_ref[1, j] + diff_z(t_ref, SYZ, x, False)
        store(v_ref, VY, x, load(v_ref, VY, x) + b * force)
        force = diff_x(t_ref, SXZ, x, False) + d_ref[2, j] + diff_z(t_ref, SZZ, x, True)
        store(v_ref, VZ, x, load(v_ref, VZ, x) + b * force)
        return 0

    lax.fori_loop(0, count, body, 0, unroll=2)
    for j in range(count):
        pad_halo(v_ref, VX, xa + j)
        pad_halo(v_ref, VY, ya + j)
        pad_halo(v_ref, VZ, ya + j)


def stress_pass(v_ref, t_ref, p_ref, band_ref, d_ref, first, count, pads=True):
    a = first + LOW
    y_differences([(v_ref, VX, a, 0), (v_ref, VZ, a, 2)], count, True, band_ref, d_ref)
    y_differences([(v_ref, VY, a, 1)], count, False, band_ref, d_ref)

    def body(j, _):
        x = a + j
        lame, mu = p_ref[1, x], p_ref[2, x]
        grad_x = diff_x(v_ref, VX, x, False)
        grad_y = d_ref[1, j]
        grad_z = diff_z(v_ref, VZ, x, False)
        spread = lame * (grad_x + grad_y + grad_z)
        double = mu + mu
        rates = (
            (SXX, double * grad_x + spread),
            (SYY, double * grad_y + spread),
            (SZZ, double * grad_z + spread),
            (SXY, mu * (d_ref[0, j] + diff_x(v_ref, VY, x, True))),
            (SXZ, mu * (diff_z(v_ref, VX, x, True) + diff_x(v_ref, VZ, x, True))),
            (SYZ, mu * (diff_z(v_ref, VY, x, True) + d_ref[2, j])),
        )
        for f, rate in rates:
            store(t_ref, f, x, load(t_ref, f, x) + rate)
        return 0

    lax.fori_loop(0, count, body, 0, unroll=2)
    if pads:
        for j in range(count):
            for f in Z_STRESS:
                pad_halo(t_ref, f, a + j)


def planes_of(items, odd, inner, out):
    for kind, f, depth in items:
        low, high = (0, CX - depth) if out else (-depth, CX)
        row = jnp.where(odd, low, high) if inner else jnp.where(odd, high, low)
        for k in range(depth):
            yield kind, f, row + LOW + k


def take_halo(items, odd, inner, read, v_ref, t_ref, p_ref):
    padded = []
    for n, (kind, f, x) in enumerate(planes_of(items, odd, inner, False)):
        if kind == "p":
            p_ref[f, x] = read(n)
        else:
            ref = v_ref if kind == "v" else t_ref
            store(ref, f, x, read(n))
            if kind == "v" or f in Z_STRESS:
                padded.append((ref, f, x))
    for ref, f, x in padded:
        pad_halo(ref, f, x)


def give_halo(items, odd, inner, send_ref, v_ref, t_ref, p_ref):
    for n, (kind, f, x) in enumerate(planes_of(items, odd, inner, True)):
        ref = {"v": v_ref, "t": t_ref, "p": p_ref}[kind]
        send_ref[n] = p_ref[f, x] if kind == "p" else load(ref, f, x)


def own_rows(kind, f, x, v_ref, t_ref, p_ref):
    return p_ref[f, x, 0:NZ, :] if kind == "p" else {"v": v_ref, "t": t_ref}[kind][f, x, 8:8 + NZ, :]


def packed_rows(kind, f, x, v_ref, t_ref, p_ref):
    if kind == "p":
        return p_ref[f, x, NZ:DEPTH, :]
    return {"v": v_ref, "t": t_ref}[kind][f, x, 56:64, :]


def give_early(odd, send_ref, *state):
    for n, plane in enumerate(planes_of(OUTER_FIRST[:EARLY_FIELDS], odd, False, True)):
        send_ref[n] = own_rows(*plane, *state)


def give_late(odd, send_ref, *state):
    at = plane_count(OUTER_FIRST)
    for n, plane in enumerate(planes_of(OUTER_FIRST, odd, False, True)):
        send_ref[n] = packed_rows(*plane, *state)
    for plane in planes_of(OUTER_FIRST[EARLY_FIELDS:], odd, False, True):
        rows = own_rows(*plane, *state)
        for k in range(4):
            send_ref[at + k] = rows[8 * k:8 * k + 8]
        at += 4


def read_first(early_ref, late_ref):
    early, planes = plane_count(OUTER_FIRST[:EARLY_FIELDS]), plane_count(OUTER_FIRST)

    def read(n):
        if n < early:
            return jnp.concatenate([early_ref[n], late_ref[n]], axis=0)
        at = planes + 4 * (n - early)
        return jnp.concatenate([late_ref[at + k] for k in range(4)] + [late_ref[n]], axis=0)

    return read


def near_lanes():
    spot = lanes(PACK) % 32
    return (spot >= HALF - SECOND_WIDE) & (spot < HALF + SECOND_WIDE)


def give_second(odd, send_ref, *state):
    planes = list(planes_of(OUTER, odd, False, True))
    for n, plane in enumerate(planes):
        rows = own_rows(*plane, *state)
        for k in range(4):
            send_ref[4 * n + k] = rows[8 * k:8 * k + 8]
    keep = near_lanes()
    for n in range(0, len(planes), 2):
        one, two = (packed_rows(*plane, *state) for plane in planes[n:n + 2])
        send_ref[4 * len(planes) + n // 2] = jnp.where(keep, one, pltpu.roll(two, HALF, 1))


def read_second(got_ref):
    planes = plane_count(OUTER)

    def read(n):
        halo = got_ref[4 * planes + n // 2]
        halo = pltpu.roll(halo, 128 - HALF, 1) if n % 2 else halo
        halo = jnp.where(near_lanes(), halo, 0.0)
        return jnp.concatenate([got_ref[4 * n + k] for k in range(4)] + [halo], axis=0)

    return read


def pieces():
    out = []
    for u in range(8):
        for v in range(3):
            start = WIDE * u - 32 * v
            a, b = max(0, start), min(32, start + WIDE)
            if a < b:
                out.append((u, v, start, a, b))
    return out


PIECES = pieces()


def fetch(refs, buf_ref, sems):
    size = NZ * CX
    waits = []
    for a in range(12):
        src = refs[0].at[pl.ds(a * size, size)] if a < 9 else refs[a - 8]
        waits.append(pltpu.make_async_copy(src, buf_ref.at[pl.ds(a * size, size)], sems.at[a]))
    for copy in waits:
        copy.start()
    return waits


def low_side(first):
    odd = lax.rem(lax.axis_index("tile"), 2) > 0
    return jnp.where(odd, HALF - WIDE, HALF) if first else jnp.where(odd, HALF, HALF - WIDE)


def pack_units(units, at, put):
    spot = lanes(PACK) % 32
    parts = [None] * 3
    for u, v, start, lo, hi in PIECES:
        keep = (spot >= lo) & (spot < hi)
        moved = pltpu.roll(units[u], lax.rem(start - at + 256, 128), 1)
        parts[v] = moved if parts[v] is None else jnp.where(keep, moved, parts[v])
    for v in range(3):
        put(v, parts[v])


def edge_kernel(fields_ref, buoy_ref, lame_ref, mu_ref, first_ref, second_ref, token_ref, buf_ref,
                sems):
    size = NZ * CX
    lane = lanes(PACK)
    token_ref[...] = jnp.zeros((8, 128), jnp.float32)
    for a, copy in enumerate(fetch((fields_ref, buoy_ref, lame_ref, mu_ref), buf_ref, sems)):
        copy.wait()
        for block in range(2):
            units = []
            for u in range(8):
                out = None
                for g in range(GROUPS):
                    row = a * size + (8 * g + u) * CX + 8 * block
                    moved = pltpu.roll(buf_ref[row:row + 8, :], (HALF + 32 * g) % 128, 1)
                    out = moved if g == 0 else jnp.where(lane >= 32 * g, moved, out)
                units.append(out)
            for ref, is_first in ((first_ref, True), (second_ref, False)):
                def put(v, value):
                    ref[a, 3 * block + v] = value
                pack_units(units, 2 * HALF - WIDE - low_side(is_first), put)


def unpack_units(got_ref, a, block, at, under, put):
    spot = lanes(PACK) % 32
    for u in range(8):
        value = under(u)
        for w, v, start, lo, hi in PIECES:
            if w == u:
                keep = (spot >= lo - start + at) & (spot < hi - start + at)
                moved = pltpu.roll(got_ref[a, 3 * block + v], lax.rem(at - start + 256, 128), 1)
                value = jnp.where(keep, moved, value)
        put(u, value)


def first_halo_kernel(got_ref, half_ref):
    at = low_side(True)

    def body(a, _):
        for block in range(2):
            def put(u, value):
                half_ref[a, block, u] = value
            unpack_units(got_ref, a, block, at, lambda u: jnp.zeros((PACK, 128), jnp.float32), put)
        return 0

    lax.fori_loop(0, 12, body, 0)


def build_kernel(fields_ref, buoy_ref, lame_ref, mu_ref, after_ref, v_ref, t_ref, p_ref, outer_ref):
    size = NZ * CX
    zero = jnp.zeros((8, 128), jnp.float32)

    def clear(x, _):
        for ref, f in [(v_ref, f) for f in range(3)] + [(t_ref, f) for f in Z_STRESS]:
            ref[f, x, 0:8, :] = zero
            ref[f, x, 40:48, :] = zero
        return 0

    lax.fori_loop(0, PLANES, clear, 0)
    for a in range(12):
        ref, first = (fields_ref, a * size) if a < 9 else ((buoy_ref, lame_ref, mu_ref)[a - 9], 0)
        for x in range(CX):
            value = ref[pl.ds(first + x, NZ, stride=CX), :]
            if a < 3:
                v_ref[a, x + LOW, 8:8 + NZ, :] = value
            elif a < 9:
                t_ref[a - 3, x + LOW, 8:8 + NZ, :] = value
            else:
                p_ref[a - 9, x + LOW, 0:NZ, :] = DT * value
    give_early(is_odd(), outer_ref, v_ref, t_ref, p_ref)


def halo_kernel(got_ref, half_ref, v_in, t_in, p_in, v_ref, t_ref, p_ref, outer_ref, inner_ref):
    odd = is_odd()
    at = low_side(False)
    v_rows = v_ref.reshape(3 * PLANES * ZROWS, 128)
    t_rows = t_ref.reshape(6 * PLANES * ZROWS, 128)
    p_rows = p_ref.reshape(3 * PLANES * DEPTH, 128)

    def one(a, f, rows_ref, depth, begin, scale):
        for block in range(2):
            def put(u, value):
                row = (f * PLANES + LOW + 8 * block) * depth + begin + u
                rows_ref[pl.ds(row, 8, stride=depth), :] = scale * value if scale else value
            unpack_units(got_ref, a, block, at, lambda u: half_ref[a, block, u], put)

    for a in range(12):
        if a < 3:
            one(a, a, v_rows, ZROWS, 56, None)
        elif a < 9:
            one(a, a - 3, t_rows, ZROWS, 56, None)
        else:
            one(a, a - 9, p_rows, DEPTH, NZ, DT)
    give_late(odd, outer_ref, v_ref, t_ref, p_ref)
    give_halo(INNER_FIRST, odd, True, inner_ref, v_ref, t_ref, p_ref)


def pad_own(v_ref, t_ref):
    def pads(x, _):
        for f in range(3):
            pad_halo(v_ref, f, x)
        for f in Z_STRESS:
            pad_halo(t_ref, f, x)
        return 0

    lax.fori_loop(LOW, LOW + CX, pads, 0)


def near_step(items, back, odd, read, v_ref, t_ref, p_ref, band_ref, d_ref):
    take_halo(items, odd, True, read, v_ref, t_ref, p_ref)
    mats = (v_ref, t_ref, p_ref, band_ref, d_ref)
    velocity_pass(*mats, jnp.where(odd, -2, back + 1), jnp.where(odd, -1, back + 2), CX - back)
    stress_pass(*mats, jnp.where(odd, 0, back + 3), CX - 3 - back)


def near_kernel(items, back, gots, gives, band_ref, *refs):
    got_refs, refs = refs[:gots], refs[gots + 3:]
    v_ref, t_ref, p_ref = refs[:3]
    send_refs, d_ref = refs[3:3 + gives], refs[-1]
    odd = is_odd()
    if items is INNER_FIRST:
        pad_own(v_ref, t_ref)

    def read(n):
        part = plane_count(INNER[:4])
        return got_refs[0][n] if gots == 1 or n < part else got_refs[1][n - part]

    near_step(items, back, odd, read, v_ref, t_ref, p_ref, band_ref, d_ref)
    if gives == 1:
        give_halo(INNER, odd, True, send_refs[0], v_ref, t_ref, p_ref)
    else:
        give_halo(INNER[:4], odd, True, send_refs[0], v_ref, t_ref, p_ref)
        give_halo(INNER[4:], odd, True, send_refs[1], v_ref, t_ref, p_ref)


def stress_half(first, t_ref, out_ref, rows_ref, sem):
    flat = rows_ref.reshape(6 * NZ * 8, 128)

    def body(r, _):
        for f in range(6):
            flat[pl.ds(f * NZ * 8 + r, NZ, stride=8), :] = t_ref[f, first + r + LOW, 8:8 + NZ, :]
        return 0

    lax.fori_loop(0, 8, body, 0, unroll=2)
    copy = pltpu.make_async_copy(
        rows_ref, out_ref.at[pl.ds(3 * NZ, 6 * NZ), pl.ds(pl.multiple_of(first, 8), 8)], sem)
    copy.start()
    return copy


def last_near_kernel(influence_ref, count_ref, profile_ref, band_ref, got_ref, v_in, t_in,
                     p_in, v_ref, t_ref, p_ref, out_ref, used_ref, profile_rows, d_ref, rows_ref, sem):
    odd = is_odd()
    near_step(INNER, 3, odd, lambda n: got_ref[n], v_ref, t_ref, p_ref, band_ref, d_ref)
    copy = stress_half(jnp.where(odd, 0, 8), t_ref, out_ref, rows_ref, sem)
    lane = lanes(8)
    column = lax.broadcasted_iota(jnp.int32, (8, 128), 0) + lax.axis_index("tile") - 1
    slot_id = (lane // S * 32 + column) * S + lane % S
    slot_id = jnp.where((column >= 0) & (column < 32), slot_id, -1)
    used = jnp.zeros((8, 128), jnp.int32)
    for k in range(LIST):
        hit = (slot_id == influence_ref[0, k]) & (k < count_ref[0])
        used = jnp.where(hit, 1, used)
    used_ref[...] = used
    for c in range(3):
        for z in range(NZ):
            profile_rows[c, z:z + 1, :] = jnp.full((1, 128), profile_ref[c, z], jnp.float32)
    copy.wait()


def far_steps(items, last, odd, read, v_ref, t_ref, p_ref, band_ref, d_ref):
    take_halo(items, odd, False, read, v_ref, t_ref, p_ref)
    mats = (v_ref, t_ref, p_ref, band_ref, d_ref)
    velocity_pass(*mats, jnp.where(odd, 14, -5), jnp.where(odd, 15, -4), 6)
    stress_pass(*mats, jnp.where(odd, 13, -3), 6)
    velocity_pass(*mats, jnp.where(odd, 11, -2), jnp.where(odd, 12, -1), 6)
    if not last:
        stress_pass(*mats, jnp.where(odd, 10, 0), 6)


def far_kernel(band_ref, got_own, got_halo, v_in, t_in, p_in, v_ref, t_ref, p_ref,
               outer_ref, d_ref):
    odd = is_odd()
    far_steps(OUTER_FIRST, False, odd, read_first(got_own, got_halo), v_ref, t_ref, p_ref, band_ref, d_ref)
    give_second(odd, outer_ref, v_ref, t_ref, p_ref)


def station_kernel(count_ref, observed_ref, gain_ref, cell_ref, band_ref,
                   got_ref, v_in, t_in, p_in, v_ref, t_ref, p_ref, packet_ref, d_ref, slot_ref):
    odd = is_odd()
    far_steps(OUTER, True, odd, read_second(got_ref), v_ref, t_ref, p_ref, band_ref, d_ref)
    slot_ref[...] = jnp.zeros((16, 128), jnp.float32)
    slot_ref[0:3, 0:S] = observed_ref[...]
    slot_ref[3:4, 0:S] = gain_ref[...]
    slot_ref[4:5, 0:S] = cell_ref[...].astype(jnp.float32)
    cell = slot_ref[4:5, :].astype(jnp.int32)
    cell_x, cell_y = cell // CY, cell % CY
    pick_y = (lax.broadcasted_iota(jnp.int32, (CY, 128), 0) == cell_y).astype(jnp.float32)
    pick_x = lax.broadcasted_iota(jnp.int32, (CX, 128), 0) == cell_x
    live = lanes(1) < count_ref[0]
    gain = slot_ref[3:4, :]
    region, tile = lax.axis_index("region"), lax.axis_index("tile")
    surface = jnp.concatenate(
        [v_ref[c, r + LOW, 8:9, :] for c in range(3) for r in range(CX)], axis=0)
    rows = jnp.dot(surface, pick_y, precision=lax.Precision.HIGHEST,
                   preferred_element_type=jnp.float32)
    for c in range(3):
        picked = jnp.where(pick_x, rows[c * CX:(c + 1) * CX], 0.0)
        sample = jnp.sum(picked, axis=0, keepdims=True)
        slot_ref[8 + c:9 + c, :] = jnp.where(live, gain * (slot_ref[c:c + 1, :] - sample), 0.0)
    slot_ref[11:12, :] = (region * CX + cell_x).astype(jnp.float32)
    slot_ref[12:13, :] = (tile * CY + cell_y).astype(jnp.float32)
    own = jnp.where(lanes(8) < S, slot_ref[8:16, :], 0.0)
    packet_ref[...] = pltpu.roll(own, region * S, 1)


def tile_column(packet_refs, used, cell_x, cell_y):
    packet = packet_refs[0] + packet_refs[1] + packet_refs[2] + packet_refs[3]
    dist_x = cell_x - packet[3:4]
    dist_y = cell_y - packet[4:5]
    along_x = jnp.exp(-(dist_x * dist_x) / (2.0 * (0.5 * CX) ** 2))
    along_y = jnp.exp(-(dist_y * dist_y) / (2.0 * (0.25 * CY) ** 2))
    scaled = jnp.concatenate(
        [jnp.where(used > 0, packet[c:c + 1] * along_x, 0.0) for c in range(3)], axis=0)
    return lax.dot_general(
        scaled, along_y, (((1,), (1,)), ((), ())), precision=lax.Precision.HIGHEST,
        preferred_element_type=jnp.float32)


def cell_places():
    region, tile = lax.axis_index("region"), lax.axis_index("tile")
    cell_x = (lax.broadcasted_iota(jnp.int32, (CX, 128), 0) + region * CX).astype(jnp.float32)
    cell_y = (lax.broadcasted_iota(jnp.int32, (CY, 128), 0) + tile * CY).astype(jnp.float32)
    return cell_x, cell_y


def stress_out_kernel(band_ref, here_ref, used_ref, v_ref, t_in, p_ref, out_in, t_ref,
                      out_ref, own_part, d_ref, rows_ref, sem):
    odd = is_odd()
    stress_pass(v_ref, t_ref, p_ref, band_ref, d_ref, jnp.where(odd, 10, 0), 6, pads=False)
    copy = stress_half(jnp.where(odd, 8, 0), t_ref, out_ref, rows_ref, sem)
    own_part[...] = tile_column(here_ref, used_ref[1:2], *cell_places())
    copy.wait()


def increment_kernel(v_ref, first_ref, second_ref, used_ref, profile_rows, own_part, out_in, out_ref,
                     rows_ref, sems):
    odd = lax.rem(lax.axis_index("tile"), 2) > 0
    before = [jnp.where(odd, first_ref[r], second_ref[r]) for r in range(4)]
    after = [jnp.where(odd, second_ref[r], first_ref[r]) for r in range(4)]
    places = cell_places()
    increment = (own_part[...] + tile_column(before, used_ref[0:1], *places)
                 + tile_column(after, used_ref[2:3], *places))
    flat = rows_ref.reshape(3 * NZ * CX, 128)
    copies = []
    for c in range(3):
        for r in range(CX):
            value = v_ref[c, r + LOW, 8:8 + NZ, :]
            value = value + profile_rows[c] * increment[c * CX + r:c * CX + r + 1, :]
            flat[pl.ds(c * NZ * CX + r, NZ, stride=CX), :] = value
        part = pl.ds(c * NZ, NZ)
        copies.append(pltpu.make_async_copy(rows_ref.at[part], out_ref.at[part], sems.at[c]))
        copies[c].start()
    for copy in copies:
        copy.wait()


def struct(*shape):
    return jax.ShapeDtypeStruct(shape, jnp.float32)


VM = pl.BlockSpec(memory_space=pltpu.VMEM)
SM = pl.BlockSpec(memory_space=pltpu.SMEM)
HB = pl.BlockSpec(memory_space=pltpu.HBM)


def call(kernel, outs, specs, scratch, out_specs=None, aliases=None, vmem=VMEM_BYTES,
         cost=None):
    return pl.pallas_call(
        kernel, out_shape=outs, in_specs=specs, out_specs=out_specs or [VM] * len(outs),
        scratch_shapes=list(scratch), input_output_aliases=aliases or {}, cost_estimate=cost,
        compiler_params=pltpu.CompilerParams(vmem_limit_bytes=vmem))


def pairs(first):
    return [p for i in range(first, 31, 2) for p in ((i, i + 1), (i + 1, i))]


INNER_SWAP = [(0, 1), (1, 0), (2, 3), (3, 2)]
OUTER_SWAP = [(1, 2), (2, 1)]


FREE = pl.CostEstimate(flops=1024, bytes_accessed=1024, transcendentals=0)


def bind(kernel, *first):
    def bound(*refs):
        return kernel(*first, *refs)
    return bound


def per_device(fields, buoyancy, lame_first, shear_modulus, observed, station_weight, depth_profile,
               station_cell, station_count, influence, influence_count):
    band = jnp.asarray(band_matrices(), jnp.bfloat16)
    size = NZ * CX
    state = (struct(3, PLANES, ZROWS, 128), struct(6, PLANES, ZROWS, 128),
             struct(3, PLANES, DEPTH, 128))
    given = (fields.reshape(9 * size, CY), buoyancy.reshape(size, CY),
             lame_first.reshape(size, CY), shear_modulus.reshape(size, CY))
    fetched = [pltpu.VMEM((12 * size, 128), jnp.float32), pltpu.SemaphoreType.DMA((12,))]
    packed, edges = struct(12, 6, PACK, 128), struct(12, 2, 8, 8, 128)
    first, second, token = call(edge_kernel, (packed, packed, struct(8, 128)), [HB] * 4, fetched,
                         vmem=62 * 2 ** 20)(*given)
    got_first = lax.ppermute(first, "tile", pairs(0))
    got_second = lax.ppermute(second, "tile", pairs(1))
    early, planes = plane_count(OUTER_FIRST[:EARLY_FIELDS]), plane_count(OUTER_FIRST)
    v, t, p, outer = call(build_kernel, state + (struct(early, NZ, 128),), [VM] * 5, [],
                          cost=pl.CostEstimate(flops=0, bytes_accessed=10 ** 8, transcendentals=0))(
        *given, token)
    got_own = lax.ppermute(outer, "region", OUTER_SWAP)
    half, = call(first_halo_kernel, (edges,), [VM], [])(got_first)
    v, t, p, outer, inner = call(
        halo_kernel, state + (struct(planes + 4 * (planes - early), PACK, 128),
                              struct(plane_count(INNER_FIRST), DEPTH, 128)),
        [VM] * 5, [], aliases={2: 0, 3: 1, 4: 2},
    )(got_second, half, v, t, p)
    inner_struct = struct(plane_count(INNER), DEPTH, 128)
    d_scratch = pltpu.VMEM((3, CX, DEPTH, 128), jnp.float32)
    alias = {2: 0, 3: 1, 4: 2}
    result = struct(9 * NZ, CX, 128)
    for block in range(2):
        got = lax.ppermute(inner, "region", INNER_SWAP)
        got_outer = lax.ppermute(outer, "region", OUTER_SWAP)
        split = 2 if block == 0 else 1
        parts = (INNER[:4], INNER[4:]) if block == 0 else (INNER,)
        v, t, p, *inner = call(
            bind(near_kernel, INNER_FIRST if block == 0 else INNER, 0, 1, split),
            state + tuple(struct(plane_count(part), DEPTH, 128) for part in parts), [VM] * 5,
            [d_scratch], aliases=alias, cost=FREE,
        )(band, got, v, t, p)
        got = [lax.ppermute(part, "region", INNER_SWAP) for part in inner]
        if block == 0:
            v, t, p, inner = call(
                bind(near_kernel, INNER, 3, 2, 1), state + (inner_struct,), [VM] * 6,
                [d_scratch], aliases={3: 0, 4: 1, 5: 2}, cost=FREE,
            )(band, *got, v, t, p)
            v, t, p, outer = call(
                far_kernel, state + (struct(4 * plane_count(OUTER) + plane_count(OUTER) // 2, 8, 128),),
                [VM] * 6, [d_scratch], aliases={3: 0, 4: 1, 5: 2},
            )(band, got_own, got_outer, v, t, p)
        else:
            v, t, p, out, used, profile_rows = call(
                last_near_kernel,
                state + (result, jax.ShapeDtypeStruct((8, 128), jnp.int32), struct(3, NZ, 128)),
                [SM] * 3 + [VM] * 5,
                [d_scratch, pltpu.VMEM((6 * NZ, 8, 128), jnp.float32), pltpu.SemaphoreType.DMA],
                out_specs=[VM] * 3 + [HB] + [VM] * 2, aliases={5: 0, 6: 1, 7: 2},
            )(influence, influence_count, depth_profile, band, *got, v, t, p)
    v, t, p, packet = call(
        station_kernel, state + (struct(8, 128),), [SM] + [VM] * 8,
        [d_scratch, pltpu.VMEM((16, 128), jnp.float32)], aliases={6: 0, 7: 1, 8: 2},
    )(station_count, observed, station_weight.reshape(1, S), station_cell.reshape(1, S),
      band, got_outer, v, t, p)
    here = lax.all_gather(packet, "region")
    got_first = lax.ppermute(here, "tile", pairs(0))
    got_second = lax.ppermute(here, "tile", pairs(1))
    _, out, own_part = call(
        stress_out_kernel, (state[1], result, struct(3 * CX, CY)), [VM] * 6 + [HB],
        [d_scratch, pltpu.VMEM((6 * NZ, 8, 128), jnp.float32), pltpu.SemaphoreType.DMA],
        out_specs=[VM, HB, VM], aliases={4: 0, 6: 1},
    )(band, here, used, v, t, p, out)
    out, = call(
        increment_kernel, (result,), [VM] * 6 + [HB],
        [pltpu.VMEM((3 * NZ, CX, 128), jnp.float32), pltpu.SemaphoreType.DMA((3,))],
        out_specs=[HB], aliases={6: 0},
    )(v, got_first, got_second, used, profile_rows, own_part, out)
    return out.reshape(9, NZ, CX, CY)


def solution(mesh):
    in_specs = (
        P(None, None, "region", "tile"),
        P(None, "region", "tile"),
        P(None, "region", "tile"),
        P(None, "region", "tile"),
        P(None, ("region", "tile")),
        P(("region", "tile")),
        P(),
        P(("region", "tile")),
        P(("region", "tile")),
        P(("region", "tile"), None),
        P(("region", "tile")),
    )
    out_specs = P(None, None, "region", "tile")
    return jax.shard_map(
        per_device, mesh=mesh, in_specs=in_specs, out_specs=out_specs, check_vma=False
    )
```

```python
import jax
import jax.numpy as jnp
import numpy as np
from jax import lax
from jax.experimental import pallas as pl
from jax.experimental.pallas import tpu as pltpu
from jax.sharding import PartitionSpec as P

DT = 0.15 / 24.0

CX, CY, NZ = 16, 128, 32
S, LIST = 32, 64
GROUPS = 4
HALF = 16
WIDTHS = (11, 11, 11, 11, 12, 11, 12, 11, 12, 11, 9, 9)
PACK = NZ // GROUPS
DEPTH = NZ + PACK
LOW = 6
PLANES = CX + 2 * LOW
ZROWS = 72

VX, VY, VZ = range(3)
SXX, SYY, SZZ, SXY, SXZ, SYZ = range(6)
Z_STRESS = (SZZ, SXZ, SYZ)

OUTER = [("t", f, 6) for f in (SXX, SXY, SXZ)] + [("t", f, 5) for f in (SYY, SYZ, SZZ)] + [
    ("v", f, 5) for f in range(3)]
OUTER_FIRST = OUTER + [("p", 0, 5), ("p", 1, 3), ("p", 2, 3)]
INNER = [("t", f, 3) for f in (SXX, SXY, SXZ)] + [("t", f, 2) for f in (SYY, SYZ, SZZ)] + [
    ("v", f, 2) for f in range(3)]
INNER_FIRST = INNER + [("p", 0, 2)]

EARLY_FIELDS = 12
SECOND_WIDE = 6

VMEM_BYTES = 8 * 2 ** 20


def is_odd():
    return lax.rem(lax.axis_index("region"), 2) > 0


def plane_count(items):
    return sum(d for _, _, d in items)


def lanes(rows):
    return lax.broadcasted_iota(jnp.int32, (rows, 128), 1)


def band_matrices():
    taps = {0: ((-1, 1), (0, -27), (1, 27), (2, -1)), 1: ((-2, 1), (-1, -27), (0, 27), (1, -1))}
    band = np.zeros((2, GROUPS, 256, 256), np.float32)
    for k in range(2):
        for offset, coef in taps[k]:
            for g in range(GROUPS):
                for lane in range(128):
                    y = lane + offset
                    if 0 <= y < CY:
                        band[k, g, y, lane] += coef
                    else:
                        band[k, g, 128 + 32 * g + HALF + (y if y < 0 else y - CY), lane] += coef
                for spot in range(32):
                    to = spot + offset
                    out = 128 + 32 * g + spot
                    if not 0 <= to < 32:
                        continue
                    if (spot < HALF) == (to < HALF):
                        band[k, g, 128 + 32 * g + to, out] += coef
                    elif spot < HALF:
                        band[k, g, to - HALF, out] += coef
                    else:
                        band[k, g, CY + to - HALF, out] += coef
    return band


def two_terms(value):
    high = value.astype(jnp.bfloat16)
    return high, (value - high.astype(jnp.float32)).astype(jnp.bfloat16)


def y_differences(items, count, forward, band_ref, out_ref):
    even = count + count % 2
    size = 8 * even * len(items)

    def rows(at):
        value = jnp.concatenate(
            [ref[f, x + j, at:at + 8, :] for ref, f, x, _ in items for j in range(even)], axis=0)
        return jnp.concatenate(two_terms(value), axis=0)

    halo = rows(56)
    halo_out = None
    for g in range(GROUPS + 1):
        if g < GROUPS:
            both = jnp.dot(jnp.concatenate([rows(8 + 8 * g), halo], axis=1),
                           band_ref[0 if forward else 1, g], preferred_element_type=jnp.float32)
            total = both[:size, :128] + both[size:, :128]
            part = both[:size, 128:] + both[size:, 128:]
            halo_out = part if g == 0 else halo_out + part
        else:
            total = halo_out
        for n, (_, _, _, slot) in enumerate(items):
            for j in range(count):
                r = 8 * (n * even + j)
                out_ref[slot, j, 8 * g:8 * g + 8, :] = total[r:r + 8]


def load(ref, f, x, dz=0):
    return jnp.concatenate(
        [ref[f, x, 8 + dz:8 + NZ + dz, :], ref[f, x, 56 + dz:64 + dz, :]], axis=0)


def store(ref, f, x, value):
    ref[f, x, 8:8 + NZ, :] = value[:NZ]
    ref[f, x, 56:64, :] = value[NZ:]


def pad_halo(ref, f, x):
    lane = lanes(PACK)
    halo = ref[f, x, 56:64, :]
    ref[f, x, 48:56, :] = jnp.where(lane < 32, 0.0, pltpu.roll(halo, 32, 1))
    ref[f, x, 64:72, :] = jnp.where(lane >= 96, 0.0, pltpu.roll(halo, 96, 1))


def combine(m1, c0, p1, p2):
    return 27.0 * (p1 - c0) - (p2 - m1)


def diff_x(ref, f, x, forward):
    first = -1 if forward else -2
    return combine(*[load(ref, f, x + first + k) for k in range(4)])


def diff_z(ref, f, x, forward):
    first = -1 if forward else -2
    return combine(*[load(ref, f, x, first + k) for k in range(4)])


def velocity_pass(v_ref, t_ref, p_ref, band_ref, d_ref, x_first, y_first, count):
    xa, ya = x_first + LOW, y_first + LOW
    y_differences([(t_ref, SXY, xa, 0), (t_ref, SYZ, ya, 2)], count, False, band_ref, d_ref)
    y_differences([(t_ref, SYY, ya, 1)], count, True, band_ref, d_ref)

    def body(j, _):
        x = xa + j
        force = diff_x(t_ref, SXX, x, True) + d_ref[0, j] + diff_z(t_ref, SXZ, x, False)
        store(v_ref, VX, x, load(v_ref, VX, x) + p_ref[0, x] * force)
        x = ya + j
        b = p_ref[0, x]
        force = diff_x(t_ref, SXY, x, False) + d_ref[1, j] + diff_z(t_ref, SYZ, x, False)
        store(v_ref, VY, x, load(v_ref, VY, x) + b * force)
        force = diff_x(t_ref, SXZ, x, False) + d_ref[2, j] + diff_z(t_ref, SZZ, x, True)
        store(v_ref, VZ, x, load(v_ref, VZ, x) + b * force)
        return 0

    lax.fori_loop(0, count, body, 0, unroll=2)
    for j in range(count):
        pad_halo(v_ref, VX, xa + j)
        pad_halo(v_ref, VY, ya + j)
        pad_halo(v_ref, VZ, ya + j)


def stress_pass(v_ref, t_ref, p_ref, band_ref, d_ref, first, count, pads=True):
    a = first + LOW
    y_differences([(v_ref, VX, a, 0), (v_ref, VZ, a, 2)], count, True, band_ref, d_ref)
    y_differences([(v_ref, VY, a, 1)], count, False, band_ref, d_ref)

    def body(j, _):
        x = a + j
        lame, mu = p_ref[1, x], p_ref[2, x]
        grad_x = diff_x(v_ref, VX, x, False)
        grad_y = d_ref[1, j]
        grad_z = diff_z(v_ref, VZ, x, False)
        spread = lame * (grad_x + grad_y + grad_z)
        double = mu + mu
        rates = (
            (SXX, double * grad_x + spread),
            (SYY, double * grad_y + spread),
            (SZZ, double * grad_z + spread),
            (SXY, mu * (d_ref[0, j] + diff_x(v_ref, VY, x, True))),
            (SXZ, mu * (diff_z(v_ref, VX, x, True) + diff_x(v_ref, VZ, x, True))),
            (SYZ, mu * (diff_z(v_ref, VY, x, True) + d_ref[2, j])),
        )
        for f, rate in rates:
            store(t_ref, f, x, load(t_ref, f, x) + rate)
        return 0

    lax.fori_loop(0, count, body, 0, unroll=2)
    if pads:
        for j in range(count):
            for f in Z_STRESS:
                pad_halo(t_ref, f, a + j)


def planes_of(items, odd, inner, out):
    for kind, f, depth in items:
        low, high = (0, CX - depth) if out else (-depth, CX)
        row = jnp.where(odd, low, high) if inner else jnp.where(odd, high, low)
        for k in range(depth):
            yield kind, f, row + LOW + k


def take_halo(items, odd, inner, read, v_ref, t_ref, p_ref):
    padded = []
    for n, (kind, f, x) in enumerate(planes_of(items, odd, inner, False)):
        if kind == "p":
            p_ref[f, x] = read(n)
        else:
            ref = v_ref if kind == "v" else t_ref
            store(ref, f, x, read(n))
            if kind == "v" or f in Z_STRESS:
                padded.append((ref, f, x))
    for ref, f, x in padded:
        pad_halo(ref, f, x)


def give_halo(items, odd, inner, send_ref, v_ref, t_ref, p_ref):
    for n, (kind, f, x) in enumerate(planes_of(items, odd, inner, True)):
        ref = {"v": v_ref, "t": t_ref, "p": p_ref}[kind]
        send_ref[n] = p_ref[f, x] if kind == "p" else load(ref, f, x)


def own_rows(kind, f, x, v_ref, t_ref, p_ref):
    return p_ref[f, x, 0:NZ, :] if kind == "p" else {"v": v_ref, "t": t_ref}[kind][f, x, 8:8 + NZ, :]


def packed_rows(kind, f, x, v_ref, t_ref, p_ref):
    if kind == "p":
        return p_ref[f, x, NZ:DEPTH, :]
    return {"v": v_ref, "t": t_ref}[kind][f, x, 56:64, :]


def give_early(odd, send_ref, *state):
    for n, plane in enumerate(planes_of(OUTER_FIRST[:EARLY_FIELDS], odd, False, True)):
        send_ref[n] = own_rows(*plane, *state)


def give_late(odd, send_ref, *state):
    at = plane_count(OUTER_FIRST)
    for n, plane in enumerate(planes_of(OUTER_FIRST, odd, False, True)):
        send_ref[n] = packed_rows(*plane, *state)
    for plane in planes_of(OUTER_FIRST[EARLY_FIELDS:], odd, False, True):
        rows = own_rows(*plane, *state)
        for k in range(4):
            send_ref[at + k] = rows[8 * k:8 * k + 8]
        at += 4


def read_first(early_ref, late_ref):
    early, planes = plane_count(OUTER_FIRST[:EARLY_FIELDS]), plane_count(OUTER_FIRST)

    def read(n):
        if n < early:
            return jnp.concatenate([early_ref[n], late_ref[n]], axis=0)
        at = planes + 4 * (n - early)
        return jnp.concatenate([late_ref[at + k] for k in range(4)] + [late_ref[n]], axis=0)

    return read


def near_lanes():
    spot = lanes(PACK) % 32
    return (spot >= HALF - SECOND_WIDE) & (spot < HALF + SECOND_WIDE)


def give_second(odd, send_ref, *state):
    planes = list(planes_of(OUTER, odd, False, True))
    for n, plane in enumerate(planes):
        rows = own_rows(*plane, *state)
        for k in range(4):
            send_ref[4 * n + k] = rows[8 * k:8 * k + 8]
    keep = near_lanes()
    for n in range(0, len(planes), 2):
        one, two = (packed_rows(*plane, *state) for plane in planes[n:n + 2])
        send_ref[4 * len(planes) + n // 2] = jnp.where(keep, one, pltpu.roll(two, HALF, 1))


def read_second(got_ref):
    planes = plane_count(OUTER)

    def read(n):
        halo = got_ref[4 * planes + n // 2]
        halo = pltpu.roll(halo, 128 - HALF, 1) if n % 2 else halo
        halo = jnp.where(near_lanes(), halo, 0.0)
        return jnp.concatenate([got_ref[4 * n + k] for k in range(4)] + [halo], axis=0)

    return read


def pieces():
    out, at = {}, 0
    for a in range(12):
        for block in range(2):
            for u in range(8):
                unit = []
                for v in range(at // 32, (at + WIDTHS[a] - 1) // 32 + 1):
                    start = at - 32 * v
                    unit.append((v, start, max(0, start), min(32, start + WIDTHS[a])))
                out[a, block, u] = unit
                at += WIDTHS[a]
    return out, -(-at // 32)


PIECES, VECTORS = pieces()


def fetch(refs, buf_ref, sems):
    size = NZ * CX
    waits = []
    for a in range(12):
        src = refs[0].at[pl.ds(a * size, size)] if a < 9 else refs[a - 8]
        waits.append(pltpu.make_async_copy(src, buf_ref.at[pl.ds(a * size, size)], sems.at[a]))
    for copy in waits:
        copy.start()
    return waits


def odd_tile():
    return lax.rem(lax.axis_index("tile"), 2) > 0


def low_side(first, width):
    below, above = HALF - width, HALF
    return jnp.where(odd_tile(), below, above) if first else jnp.where(odd_tile(), above, below)


def edge_kernel(fields_ref, buoy_ref, lame_ref, mu_ref, first_ref, second_ref, buf_ref, sems):
    size = NZ * CX
    lane = lanes(PACK)
    spot = lane % 32
    open_parts = [{}, {}]
    for a, copy in enumerate(fetch((fields_ref, buoy_ref, lame_ref, mu_ref), buf_ref, sems)):
        copy.wait()
        last, zero = -WIDTHS[a], 0
        ats = (jnp.where(odd_tile(), zero, last), jnp.where(odd_tile(), last, zero))
        for block in range(2):
            for u in range(8):
                rows = [buf_ref[row:row + 8, :] for row in
                        [a * size + (8 * g + u) * CX + 8 * block for g in range(GROUPS)]]
                unit = rows[0]
                for g in range(1, GROUPS):
                    unit = jnp.where(lane >= 32 * g - 16, pltpu.roll(rows[g], 32 * g, 1), unit)
                unit = jnp.where(lane >= 112, rows[0], unit)
                for v, start, lo, hi in PIECES[a, block, u]:
                    keep = (spot >= lo) & (spot < hi)
                    for parts, at, ref in zip(open_parts, ats, (first_ref, second_ref)):
                        moved = pltpu.roll(unit, lax.rem(start - at + 256, 128), 1)
                        parts[v] = jnp.where(keep, moved, parts[v]) if v in parts else moved
                        if hi == 32:
                            ref[v] = parts.pop(v)
    for parts, ref in zip(open_parts, (first_ref, second_ref)):
        for v, value in parts.items():
            ref[v] = value


def unpack_units(got_ref, a, block, at, under, put):
    spot = lanes(PACK) % 32
    for u in range(8):
        value = under(u)
        for v, start, lo, hi in PIECES[a, block, u]:
            keep = (spot >= lo - start + at) & (spot < hi - start + at)
            moved = pltpu.roll(got_ref[v], lax.rem(at - start + 256, 128), 1)
            value = jnp.where(keep, moved, value)
        put(u, value)


def first_halo_kernel(got_ref, half_ref):
    for a in range(12):
        for block in range(2):
            def put(u, value):
                half_ref[a, block, u] = value
            unpack_units(got_ref, a, block, low_side(True, WIDTHS[a]),
                         lambda u: jnp.zeros((PACK, 128), jnp.float32), put)


def build_kernel(fields_ref, buoy_ref, lame_ref, mu_ref, v_ref, t_ref, p_ref, outer_ref):
    size = NZ * CX
    zero = jnp.zeros((8, 128), jnp.float32)

    def clear(x, _):
        for ref, f in [(v_ref, f) for f in range(3)] + [(t_ref, f) for f in Z_STRESS]:
            ref[f, x, 0:8, :] = zero
            ref[f, x, 40:48, :] = zero
        return 0

    lax.fori_loop(0, PLANES, clear, 0)
    for a in range(12):
        ref, first = (fields_ref, a * size) if a < 9 else ((buoy_ref, lame_ref, mu_ref)[a - 9], 0)
        for x in range(CX):
            value = ref[pl.ds(first + x, NZ, stride=CX), :]
            if a < 3:
                v_ref[a, x + LOW, 8:8 + NZ, :] = value
            elif a < 9:
                t_ref[a - 3, x + LOW, 8:8 + NZ, :] = value
            else:
                p_ref[a - 9, x + LOW, 0:NZ, :] = DT * value
    give_early(is_odd(), outer_ref, v_ref, t_ref, p_ref)


def halo_kernel(got_ref, half_ref, v_in, t_in, p_in, v_ref, t_ref, p_ref, outer_ref, inner_ref):
    odd = is_odd()
    v_rows = v_ref.reshape(3 * PLANES * ZROWS, 128)
    t_rows = t_ref.reshape(6 * PLANES * ZROWS, 128)
    p_rows = p_ref.reshape(3 * PLANES * DEPTH, 128)

    def one(a, f, rows_ref, depth, begin, scale):
        for block in range(2):
            def put(u, value):
                row = (f * PLANES + LOW + 8 * block) * depth + begin + u
                rows_ref[pl.ds(row, 8, stride=depth), :] = scale * value if scale else value
            unpack_units(got_ref, a, block, low_side(False, WIDTHS[a]),
                         lambda u: half_ref[a, block, u], put)

    for a in range(12):
        if a < 3:
            one(a, a, v_rows, ZROWS, 56, None)
        elif a < 9:
            one(a, a - 3, t_rows, ZROWS, 56, None)
        else:
            one(a, a - 9, p_rows, DEPTH, NZ, DT)
    give_late(odd, outer_ref, v_ref, t_ref, p_ref)
    give_halo(INNER_FIRST, odd, True, inner_ref, v_ref, t_ref, p_ref)


def pad_own(v_ref, t_ref):
    def pads(x, _):
        for f in range(3):
            pad_halo(v_ref, f, x)
        for f in Z_STRESS:
            pad_halo(t_ref, f, x)
        return 0

    lax.fori_loop(LOW, LOW + CX, pads, 0)


def near_step(items, back, odd, read, v_ref, t_ref, p_ref, band_ref, d_ref):
    take_halo(items, odd, True, read, v_ref, t_ref, p_ref)
    mats = (v_ref, t_ref, p_ref, band_ref, d_ref)
    velocity_pass(*mats, jnp.where(odd, -2, back + 1), jnp.where(odd, -1, back + 2), CX - back)
    stress_pass(*mats, jnp.where(odd, 0, back + 3), CX - 3 - back)


def near_kernel(items, back, gots, gives, band_ref, *refs):
    got_refs, refs = refs[:gots], refs[gots + 3:]
    v_ref, t_ref, p_ref = refs[:3]
    send_refs, d_ref = refs[3:3 + gives], refs[-1]
    odd = is_odd()
    if items is INNER_FIRST:
        pad_own(v_ref, t_ref)

    def read(n):
        part = plane_count(INNER[:4])
        return got_refs[0][n] if gots == 1 or n < part else got_refs[1][n - part]

    near_step(items, back, odd, read, v_ref, t_ref, p_ref, band_ref, d_ref)
    if gives == 1:
        give_halo(INNER, odd, True, send_refs[0], v_ref, t_ref, p_ref)
    else:
        give_halo(INNER[:4], odd, True, send_refs[0], v_ref, t_ref, p_ref)
        give_halo(INNER[4:], odd, True, send_refs[1], v_ref, t_ref, p_ref)


def stress_half(first, t_ref, out_ref, rows_ref, sem):
    flat = rows_ref.reshape(6 * NZ * 8, 128)

    def body(r, _):
        for f in range(6):
            flat[pl.ds(f * NZ * 8 + r, NZ, stride=8), :] = t_ref[f, first + r + LOW, 8:8 + NZ, :]
        return 0

    lax.fori_loop(0, 8, body, 0, unroll=2)
    copy = pltpu.make_async_copy(
        rows_ref, out_ref.at[pl.ds(3 * NZ, 6 * NZ), pl.ds(pl.multiple_of(first, 8), 8)], sem)
    copy.start()
    return copy


def last_near_kernel(influence_ref, count_ref, profile_ref, band_ref, got_ref, v_in, t_in,
                     p_in, v_ref, t_ref, p_ref, out_ref, used_ref, profile_rows, d_ref, rows_ref, sem):
    odd = is_odd()
    near_step(INNER, 3, odd, lambda n: got_ref[n], v_ref, t_ref, p_ref, band_ref, d_ref)
    copy = stress_half(jnp.where(odd, 0, 8), t_ref, out_ref, rows_ref, sem)
    lane = lanes(8)
    column = lax.broadcasted_iota(jnp.int32, (8, 128), 0) + lax.axis_index("tile") - 1
    slot_id = (lane // S * 32 + column) * S + lane % S
    slot_id = jnp.where((column >= 0) & (column < 32), slot_id, -1)
    used = jnp.zeros((8, 128), jnp.int32)
    for k in range(LIST):
        hit = (slot_id == influence_ref[0, k]) & (k < count_ref[0])
        used = jnp.where(hit, 1, used)
    used_ref[...] = used
    for c in range(3):
        for z in range(NZ):
            profile_rows[c, z:z + 1, :] = jnp.full((1, 128), profile_ref[c, z], jnp.float32)
    copy.wait()


def far_steps(items, last, odd, read, v_ref, t_ref, p_ref, band_ref, d_ref):
    take_halo(items, odd, False, read, v_ref, t_ref, p_ref)
    mats = (v_ref, t_ref, p_ref, band_ref, d_ref)
    velocity_pass(*mats, jnp.where(odd, 14, -5), jnp.where(odd, 15, -4), 6)
    stress_pass(*mats, jnp.where(odd, 13, -3), 6)
    velocity_pass(*mats, jnp.where(odd, 11, -2), jnp.where(odd, 12, -1), 6)
    if not last:
        stress_pass(*mats, jnp.where(odd, 10, 0), 6)


def far_kernel(band_ref, got_own, got_halo, v_in, t_in, p_in, v_ref, t_ref, p_ref,
               outer_ref, d_ref):
    odd = is_odd()
    far_steps(OUTER_FIRST, False, odd, read_first(got_own, got_halo), v_ref, t_ref, p_ref, band_ref, d_ref)
    give_second(odd, outer_ref, v_ref, t_ref, p_ref)


def station_kernel(count_ref, observed_ref, gain_ref, cell_ref, band_ref,
                   got_ref, v_in, t_in, p_in, v_ref, t_ref, p_ref, packet_ref, d_ref, slot_ref):
    odd = is_odd()
    far_steps(OUTER, True, odd, read_second(got_ref), v_ref, t_ref, p_ref, band_ref, d_ref)
    slot_ref[...] = jnp.zeros((16, 128), jnp.float32)
    slot_ref[0:3, 0:S] = observed_ref[...]
    slot_ref[3:4, 0:S] = gain_ref[...]
    slot_ref[4:5, 0:S] = cell_ref[...].astype(jnp.float32)
    cell = slot_ref[4:5, :].astype(jnp.int32)
    cell_x, cell_y = cell // CY, cell % CY
    pick_y = (lax.broadcasted_iota(jnp.int32, (CY, 128), 0) == cell_y).astype(jnp.float32)
    pick_x = lax.broadcasted_iota(jnp.int32, (CX, 128), 0) == cell_x
    live = lanes(1) < count_ref[0]
    gain = slot_ref[3:4, :]
    region, tile = lax.axis_index("region"), lax.axis_index("tile")
    surface = jnp.concatenate(
        [v_ref[c, r + LOW, 8:9, :] for c in range(3) for r in range(CX)], axis=0)
    rows = jnp.dot(surface, pick_y, precision=lax.Precision.HIGHEST,
                   preferred_element_type=jnp.float32)
    for c in range(3):
        picked = jnp.where(pick_x, rows[c * CX:(c + 1) * CX], 0.0)
        sample = jnp.sum(picked, axis=0, keepdims=True)
        slot_ref[8 + c:9 + c, :] = jnp.where(live, gain * (slot_ref[c:c + 1, :] - sample), 0.0)
    slot_ref[11:12, :] = (region * CX + cell_x).astype(jnp.float32)
    slot_ref[12:13, :] = (tile * CY + cell_y).astype(jnp.float32)
    own = jnp.where(lanes(8) < S, slot_ref[8:16, :], 0.0)
    packet_ref[...] = pltpu.roll(own, region * S, 1)


def tile_column(packet_refs, used, cell_x, cell_y):
    packet = packet_refs[0] + packet_refs[1] + packet_refs[2] + packet_refs[3]
    dist_x = cell_x - packet[3:4]
    dist_y = cell_y - packet[4:5]
    along_x = jnp.exp(-(dist_x * dist_x) / (2.0 * (0.5 * CX) ** 2))
    along_y = jnp.exp(-(dist_y * dist_y) / (2.0 * (0.25 * CY) ** 2))
    scaled = jnp.concatenate(
        [jnp.where(used > 0, packet[c:c + 1] * along_x, 0.0) for c in range(3)], axis=0)
    return lax.dot_general(
        scaled, along_y, (((1,), (1,)), ((), ())), precision=lax.Precision.HIGHEST,
        preferred_element_type=jnp.float32)


def cell_places():
    region, tile = lax.axis_index("region"), lax.axis_index("tile")
    cell_x = (lax.broadcasted_iota(jnp.int32, (CX, 128), 0) + region * CX).astype(jnp.float32)
    cell_y = (lax.broadcasted_iota(jnp.int32, (CY, 128), 0) + tile * CY).astype(jnp.float32)
    return cell_x, cell_y


def stress_out_kernel(band_ref, here_ref, used_ref, v_ref, t_in, p_ref, out_in, t_ref,
                      out_ref, own_part, d_ref, rows_ref, sem):
    odd = is_odd()
    stress_pass(v_ref, t_ref, p_ref, band_ref, d_ref, jnp.where(odd, 10, 0), 6, pads=False)
    copy = stress_half(jnp.where(odd, 8, 0), t_ref, out_ref, rows_ref, sem)
    own_part[...] = tile_column(here_ref, used_ref[1:2], *cell_places())
    copy.wait()


def increment_kernel(v_ref, first_ref, second_ref, used_ref, profile_rows, own_part, out_in, out_ref,
                     rows_ref, sems):
    odd = lax.rem(lax.axis_index("tile"), 2) > 0
    before = [jnp.where(odd, first_ref[r], second_ref[r]) for r in range(4)]
    after = [jnp.where(odd, second_ref[r], first_ref[r]) for r in range(4)]
    places = cell_places()
    increment = (own_part[...] + tile_column(before, used_ref[0:1], *places)
                 + tile_column(after, used_ref[2:3], *places))
    flat = rows_ref.reshape(3 * NZ * CX, 128)
    copies = []
    for c in range(3):
        for r in range(CX):
            value = v_ref[c, r + LOW, 8:8 + NZ, :]
            value = value + profile_rows[c] * increment[c * CX + r:c * CX + r + 1, :]
            flat[pl.ds(c * NZ * CX + r, NZ, stride=CX), :] = value
        part = pl.ds(c * NZ, NZ)
        copies.append(pltpu.make_async_copy(rows_ref.at[part], out_ref.at[part], sems.at[c]))
        copies[c].start()
    for copy in copies:
        copy.wait()


def struct(*shape):
    return jax.ShapeDtypeStruct(shape, jnp.float32)


VM = pl.BlockSpec(memory_space=pltpu.VMEM)
SM = pl.BlockSpec(memory_space=pltpu.SMEM)
HB = pl.BlockSpec(memory_space=pltpu.HBM)


def call(kernel, outs, specs, scratch, out_specs=None, aliases=None, vmem=VMEM_BYTES,
         cost=None):
    return pl.pallas_call(
        kernel, out_shape=outs, in_specs=specs, out_specs=out_specs or [VM] * len(outs),
        scratch_shapes=list(scratch), input_output_aliases=aliases or {}, cost_estimate=cost,
        compiler_params=pltpu.CompilerParams(vmem_limit_bytes=vmem))


def pairs(first):
    return [p for i in range(first, 31, 2) for p in ((i, i + 1), (i + 1, i))]


INNER_SWAP = [(0, 1), (1, 0), (2, 3), (3, 2)]
OUTER_SWAP = [(1, 2), (2, 1)]


FREE = pl.CostEstimate(flops=1024, bytes_accessed=1024, transcendentals=0)


def bind(kernel, *first):
    def bound(*refs):
        return kernel(*first, *refs)
    return bound


def per_device(fields, buoyancy, lame_first, shear_modulus, observed, station_weight, depth_profile,
               station_cell, station_count, influence, influence_count):
    band = jnp.asarray(band_matrices(), jnp.bfloat16)
    size = NZ * CX
    state = (struct(3, PLANES, ZROWS, 128), struct(6, PLANES, ZROWS, 128),
             struct(3, PLANES, DEPTH, 128))
    given = (fields.reshape(9 * size, CY), buoyancy.reshape(size, CY),
             lame_first.reshape(size, CY), shear_modulus.reshape(size, CY))
    fetched = [pltpu.VMEM((12 * size, 128), jnp.float32), pltpu.SemaphoreType.DMA((12,))]
    packed, edges = struct(VECTORS, PACK, 128), struct(12, 2, 8, 8, 128)
    first, second = call(edge_kernel, (packed, packed), [HB] * 4, fetched,
                         vmem=62 * 2 ** 20)(*given)
    got_first = lax.ppermute(first, "tile", pairs(0))
    got_second = lax.ppermute(second, "tile", pairs(1))
    early, planes = plane_count(OUTER_FIRST[:EARLY_FIELDS]), plane_count(OUTER_FIRST)
    v, t, p, outer = call(build_kernel, state + (struct(early, NZ, 128),), [VM] * 4, [],
                          cost=pl.CostEstimate(flops=0, bytes_accessed=10 ** 8, transcendentals=0))(
        *given)
    got_own = lax.ppermute(outer, "region", OUTER_SWAP)
    half, = call(first_halo_kernel, (edges,), [VM], [])(got_first)
    v, t, p, outer, inner = call(
        halo_kernel, state + (struct(planes + 4 * (planes - early), PACK, 128),
                              struct(plane_count(INNER_FIRST), DEPTH, 128)),
        [VM] * 5, [], aliases={2: 0, 3: 1, 4: 2},
    )(got_second, half, v, t, p)
    inner_struct = struct(plane_count(INNER), DEPTH, 128)
    d_scratch = pltpu.VMEM((3, CX, DEPTH, 128), jnp.float32)
    alias = {2: 0, 3: 1, 4: 2}
    result = struct(9 * NZ, CX, 128)
    for block in range(2):
        got = lax.ppermute(inner, "region", INNER_SWAP)
        got_outer = lax.ppermute(outer, "region", OUTER_SWAP)
        split = 2 if block == 0 else 1
        parts = (INNER[:4], INNER[4:]) if block == 0 else (INNER,)
        v, t, p, *inner = call(
            bind(near_kernel, INNER_FIRST if block == 0 else INNER, 0, 1, split),
            state + tuple(struct(plane_count(part), DEPTH, 128) for part in parts), [VM] * 5,
            [d_scratch], aliases=alias, cost=FREE,
        )(band, got, v, t, p)
        got = [lax.ppermute(part, "region", INNER_SWAP) for part in inner]
        if block == 0:
            v, t, p, inner = call(
                bind(near_kernel, INNER, 3, 2, 1), state + (inner_struct,), [VM] * 6,
                [d_scratch], aliases={3: 0, 4: 1, 5: 2}, cost=FREE,
            )(band, *got, v, t, p)
            v, t, p, outer = call(
                far_kernel, state + (struct(4 * plane_count(OUTER) + plane_count(OUTER) // 2, 8, 128),),
                [VM] * 6, [d_scratch], aliases={3: 0, 4: 1, 5: 2},
            )(band, got_own, got_outer, v, t, p)
        else:
            v, t, p, out, used, profile_rows = call(
                last_near_kernel,
                state + (result, jax.ShapeDtypeStruct((8, 128), jnp.int32), struct(3, NZ, 128)),
                [SM] * 3 + [VM] * 5,
                [d_scratch, pltpu.VMEM((6 * NZ, 8, 128), jnp.float32), pltpu.SemaphoreType.DMA],
                out_specs=[VM] * 3 + [HB] + [VM] * 2, aliases={5: 0, 6: 1, 7: 2},
            )(influence, influence_count, depth_profile, band, *got, v, t, p)
    v, t, p, packet = call(
        station_kernel, state + (struct(8, 128),), [SM] + [VM] * 8,
        [d_scratch, pltpu.VMEM((16, 128), jnp.float32)], aliases={6: 0, 7: 1, 8: 2},
    )(station_count, observed, station_weight.reshape(1, S), station_cell.reshape(1, S),
      band, got_outer, v, t, p)
    here = lax.all_gather(packet, "region")
    got_first = lax.ppermute(here, "tile", pairs(0))
    got_second = lax.ppermute(here, "tile", pairs(1))
    _, out, own_part = call(
        stress_out_kernel, (state[1], result, struct(3 * CX, CY)), [VM] * 6 + [HB],
        [d_scratch, pltpu.VMEM((6 * NZ, 8, 128), jnp.float32), pltpu.SemaphoreType.DMA],
        out_specs=[VM, HB, VM], aliases={4: 0, 6: 1},
    )(band, here, used, v, t, p, out)
    out, = call(
        increment_kernel, (result,), [VM] * 6 + [HB],
        [pltpu.VMEM((3 * NZ, CX, 128), jnp.float32), pltpu.SemaphoreType.DMA((3,))],
        out_specs=[HB], aliases={6: 0},
    )(v, got_first, got_second, used, profile_rows, own_part, out)
    return out.reshape(9, NZ, CX, CY)


def solution(mesh):
    in_specs = (
        P(None, None, "region", "tile"),
        P(None, "region", "tile"),
        P(None, "region", "tile"),
        P(None, "region", "tile"),
        P(None, ("region", "tile")),
        P(("region", "tile")),
        P(),
        P(("region", "tile")),
        P(("region", "tile")),
        P(("region", "tile"), None),
        P(("region", "tile")),
    )
    out_specs = P(None, None, "region", "tile")
    return jax.shard_map(
        per_device, mesh=mesh, in_specs=in_specs, out_specs=out_specs, check_vma=False
    )
```

```python
import jax
import jax.numpy as jnp
import numpy as np
from jax import lax
from jax.experimental import pallas as pl
from jax.experimental.pallas import tpu as pltpu
from jax.sharding import PartitionSpec as P

DT = 0.15 / 24.0

CX, CY, NZ = 16, 128, 32
S, LIST = 32, 64
GROUPS = 4
HALF = 16
WIDTHS = (11, 11, 11, 11, 12, 11, 12, 11, 12, 11, 9, 9)
PACK = NZ // GROUPS
DEPTH = NZ + PACK
LOW = 6
PLANES = CX + 2 * LOW
ZROWS = 72

VX, VY, VZ = range(3)
SXX, SYY, SZZ, SXY, SXZ, SYZ = range(6)
Z_STRESS = (SZZ, SXZ, SYZ)

OUTER = [("t", f, 6) for f in (SXX, SXY, SXZ)] + [("t", f, 5) for f in (SYY, SYZ, SZZ)] + [
    ("v", f, 5) for f in range(3)]
OUTER_FIRST = OUTER + [("p", 0, 5), ("p", 1, 3), ("p", 2, 3)]
INNER = [("t", f, 3) for f in (SXX, SXY, SXZ)] + [("t", f, 2) for f in (SYY, SYZ, SZZ)] + [
    ("v", f, 2) for f in range(3)]
INNER_FIRST = INNER + [("p", 0, 2)]

EARLY_FIELDS = 12
SECOND_WIDE = 6

VMEM_BYTES = 8 * 2 ** 20


def is_odd():
    return lax.rem(lax.axis_index("region"), 2) > 0


def plane_count(items):
    return sum(d for _, _, d in items)


def lanes(rows):
    return lax.broadcasted_iota(jnp.int32, (rows, 128), 1)


def band_matrices():
    taps = {0: ((-1, 1), (0, -27), (1, 27), (2, -1)), 1: ((-2, 1), (-1, -27), (0, 27), (1, -1))}
    band = np.zeros((2, GROUPS, 256, 256), np.float32)
    for k in range(2):
        for offset, coef in taps[k]:
            for g in range(GROUPS):
                for lane in range(128):
                    y = lane + offset
                    if 0 <= y < CY:
                        band[k, g, y, lane] += coef
                    else:
                        band[k, g, 128 + 32 * g + HALF + (y if y < 0 else y - CY), lane] += coef
                for spot in range(32):
                    to = spot + offset
                    out = 128 + 32 * g + spot
                    if not 0 <= to < 32:
                        continue
                    if (spot < HALF) == (to < HALF):
                        band[k, g, 128 + 32 * g + to, out] += coef
                    elif spot < HALF:
                        band[k, g, to - HALF, out] += coef
                    else:
                        band[k, g, CY + to - HALF, out] += coef
    return band


def two_terms(value):
    high = value.astype(jnp.bfloat16)
    return high, (value - high.astype(jnp.float32)).astype(jnp.bfloat16)


def y_differences(items, count, forward, band_ref, out_ref):
    even = count + count % 2
    size = 8 * even * len(items)

    def rows(at):
        value = jnp.concatenate(
            [ref[f, x + j, at:at + 8, :] for ref, f, x, _ in items for j in range(even)], axis=0)
        return jnp.concatenate(two_terms(value), axis=0)

    halo = rows(56)
    halo_out = None
    for g in range(GROUPS + 1):
        if g < GROUPS:
            both = jnp.dot(jnp.concatenate([rows(8 + 8 * g), halo], axis=1),
                           band_ref[0 if forward else 1, g], preferred_element_type=jnp.float32)
            total = both[:size, :128] + both[size:, :128]
            part = both[:size, 128:] + both[size:, 128:]
            halo_out = part if g == 0 else halo_out + part
        else:
            total = halo_out
        for n, (_, _, _, slot) in enumerate(items):
            for j in range(count):
                r = 8 * (n * even + j)
                out_ref[slot, j, 8 * g:8 * g + 8, :] = total[r:r + 8]


def load(ref, f, x, dz=0):
    return jnp.concatenate(
        [ref[f, x, 8 + dz:8 + NZ + dz, :], ref[f, x, 56 + dz:64 + dz, :]], axis=0)


def store(ref, f, x, value):
    ref[f, x, 8:8 + NZ, :] = value[:NZ]
    ref[f, x, 56:64, :] = value[NZ:]


def pad_halo(ref, f, x):
    lane = lanes(PACK)
    halo = ref[f, x, 56:64, :]
    ref[f, x, 48:56, :] = jnp.where(lane < 32, 0.0, pltpu.roll(halo, 32, 1))
    ref[f, x, 64:72, :] = jnp.where(lane >= 96, 0.0, pltpu.roll(halo, 96, 1))


def combine(m1, c0, p1, p2):
    return 27.0 * (p1 - c0) - (p2 - m1)


def diff_x(ref, f, x, forward):
    first = -1 if forward else -2
    return combine(*[load(ref, f, x + first + k) for k in range(4)])


def diff_z(ref, f, x, forward):
    first = -1 if forward else -2
    return combine(*[load(ref, f, x, first + k) for k in range(4)])


def velocity_pass(v_ref, t_ref, p_ref, band_ref, d_ref, x_first, y_first, count):
    xa, ya = x_first + LOW, y_first + LOW
    y_differences([(t_ref, SXY, xa, 0), (t_ref, SYZ, ya, 2)], count, False, band_ref, d_ref)
    y_differences([(t_ref, SYY, ya, 1)], count, True, band_ref, d_ref)

    def body(j, _):
        x = xa + j
        force = diff_x(t_ref, SXX, x, True) + d_ref[0, j] + diff_z(t_ref, SXZ, x, False)
        store(v_ref, VX, x, load(v_ref, VX, x) + p_ref[0, x] * force)
        x = ya + j
        b = p_ref[0, x]
        force = diff_x(t_ref, SXY, x, False) + d_ref[1, j] + diff_z(t_ref, SYZ, x, False)
        store(v_ref, VY, x, load(v_ref, VY, x) + b * force)
        force = diff_x(t_ref, SXZ, x, False) + d_ref[2, j] + diff_z(t_ref, SZZ, x, True)
        store(v_ref, VZ, x, load(v_ref, VZ, x) + b * force)
        return 0

    lax.fori_loop(0, count, body, 0, unroll=2)
    for j in range(count):
        pad_halo(v_ref, VX, xa + j)
        pad_halo(v_ref, VY, ya + j)
        pad_halo(v_ref, VZ, ya + j)


def stress_pass(v_ref, t_ref, p_ref, band_ref, d_ref, first, count, pads=True):
    a = first + LOW
    y_differences([(v_ref, VX, a, 0), (v_ref, VZ, a, 2)], count, True, band_ref, d_ref)
    y_differences([(v_ref, VY, a, 1)], count, False, band_ref, d_ref)

    def body(j, _):
        x = a + j
        lame, mu = p_ref[1, x], p_ref[2, x]
        grad_x = diff_x(v_ref, VX, x, False)
        grad_y = d_ref[1, j]
        grad_z = diff_z(v_ref, VZ, x, False)
        spread = lame * (grad_x + grad_y + grad_z)
        double = mu + mu
        rates = (
            (SXX, double * grad_x + spread),
            (SYY, double * grad_y + spread),
            (SZZ, double * grad_z + spread),
            (SXY, mu * (d_ref[0, j] + diff_x(v_ref, VY, x, True))),
            (SXZ, mu * (diff_z(v_ref, VX, x, True) + diff_x(v_ref, VZ, x, True))),
            (SYZ, mu * (diff_z(v_ref, VY, x, True) + d_ref[2, j])),
        )
        for f, rate in rates:
            store(t_ref, f, x, load(t_ref, f, x) + rate)
        return 0

    lax.fori_loop(0, count, body, 0, unroll=2)
    if pads:
        for j in range(count):
            for f in Z_STRESS:
                pad_halo(t_ref, f, a + j)


def planes_of(items, odd, inner, out):
    for kind, f, depth in items:
        low, high = (0, CX - depth) if out else (-depth, CX)
        row = jnp.where(odd, low, high) if inner else jnp.where(odd, high, low)
        for k in range(depth):
            yield kind, f, row + LOW + k


def take_halo(items, odd, inner, read, v_ref, t_ref, p_ref):
    padded = []
    for n, (kind, f, x) in enumerate(planes_of(items, odd, inner, False)):
        if kind == "p":
            p_ref[f, x] = read(n)
        else:
            ref = v_ref if kind == "v" else t_ref
            store(ref, f, x, read(n))
            if kind == "v" or f in Z_STRESS:
                padded.append((ref, f, x))
    for ref, f, x in padded:
        pad_halo(ref, f, x)


def give_halo(items, odd, inner, send_ref, v_ref, t_ref, p_ref):
    for n, (kind, f, x) in enumerate(planes_of(items, odd, inner, True)):
        ref = {"v": v_ref, "t": t_ref, "p": p_ref}[kind]
        send_ref[n] = p_ref[f, x] if kind == "p" else load(ref, f, x)


def own_rows(kind, f, x, v_ref, t_ref, p_ref):
    return p_ref[f, x, 0:NZ, :] if kind == "p" else {"v": v_ref, "t": t_ref}[kind][f, x, 8:8 + NZ, :]


def packed_rows(kind, f, x, v_ref, t_ref, p_ref):
    if kind == "p":
        return p_ref[f, x, NZ:DEPTH, :]
    return {"v": v_ref, "t": t_ref}[kind][f, x, 56:64, :]


def give_early(odd, send_ref, *state):
    for n, plane in enumerate(planes_of(OUTER_FIRST[:EARLY_FIELDS], odd, False, True)):
        send_ref[n] = own_rows(*plane, *state)


def give_late(odd, send_ref, *state):
    at = plane_count(OUTER_FIRST)
    for n, plane in enumerate(planes_of(OUTER_FIRST, odd, False, True)):
        send_ref[n] = packed_rows(*plane, *state)
    for plane in planes_of(OUTER_FIRST[EARLY_FIELDS:], odd, False, True):
        rows = own_rows(*plane, *state)
        for k in range(4):
            send_ref[at + k] = rows[8 * k:8 * k + 8]
        at += 4


def read_first(early_ref, late_ref):
    early, planes = plane_count(OUTER_FIRST[:EARLY_FIELDS]), plane_count(OUTER_FIRST)

    def read(n):
        if n < early:
            return jnp.concatenate([early_ref[n], late_ref[n]], axis=0)
        at = planes + 4 * (n - early)
        return jnp.concatenate([late_ref[at + k] for k in range(4)] + [late_ref[n]], axis=0)

    return read


def near_lanes():
    spot = lanes(PACK) % 32
    return (spot >= HALF - SECOND_WIDE) & (spot < HALF + SECOND_WIDE)


def give_second(odd, send_ref, *state):
    planes = list(planes_of(OUTER, odd, False, True))
    for n, plane in enumerate(planes):
        rows = own_rows(*plane, *state)
        for k in range(4):
            send_ref[4 * n + k] = rows[8 * k:8 * k + 8]
    keep = near_lanes()
    for n in range(0, len(planes), 2):
        one, two = (packed_rows(*plane, *state) for plane in planes[n:n + 2])
        send_ref[4 * len(planes) + n // 2] = jnp.where(keep, one, pltpu.roll(two, HALF, 1))


def read_second(got_ref):
    planes = plane_count(OUTER)

    def read(n):
        halo = got_ref[4 * planes + n // 2]
        halo = pltpu.roll(halo, 128 - HALF, 1) if n % 2 else halo
        halo = jnp.where(near_lanes(), halo, 0.0)
        return jnp.concatenate([got_ref[4 * n + k] for k in range(4)] + [halo], axis=0)

    return read


def pieces():
    out, at = {}, 0
    for a in range(12):
        for block in range(2):
            for u in range(8):
                unit = []
                for v in range(at // 32, (at + WIDTHS[a] - 1) // 32 + 1):
                    start = at - 32 * v
                    unit.append((v, start, max(0, start), min(32, start + WIDTHS[a])))
                out[a, block, u] = unit
                at += WIDTHS[a]
    return out, -(-at // 32)


PIECES, VECTORS = pieces()


def fetch(refs, buf_ref, sems):
    size = NZ * CX
    waits = []
    for a in range(12):
        src = refs[0].at[pl.ds(a * size, size)] if a < 9 else refs[a - 8]
        waits.append(pltpu.make_async_copy(src, buf_ref.at[pl.ds(a * size, size)], sems.at[a]))
    for copy in waits:
        copy.start()
    return waits


def odd_tile():
    return lax.rem(lax.axis_index("tile"), 2) > 0


def low_side(first, width):
    below, above = HALF - width, HALF
    return jnp.where(odd_tile(), below, above) if first else jnp.where(odd_tile(), above, below)


def edge_kernel(fields_ref, buoy_ref, lame_ref, mu_ref, first_ref, second_ref, buf_ref, sems):
    size = NZ * CX
    lane = lanes(PACK)
    spot = lane % 32
    open_parts = [{}, {}]
    for a, copy in enumerate(fetch((fields_ref, buoy_ref, lame_ref, mu_ref), buf_ref, sems)):
        copy.wait()
        last, zero = -WIDTHS[a], 0
        ats = (jnp.where(odd_tile(), zero, last), jnp.where(odd_tile(), last, zero))
        for block in range(2):
            for u in range(8):
                rows = [buf_ref[row:row + 8, :] for row in
                        [a * size + (8 * g + u) * CX + 8 * block for g in range(GROUPS)]]
                unit = rows[0]
                for g in range(1, GROUPS):
                    unit = jnp.where(lane >= 32 * g - 16, pltpu.roll(rows[g], 32 * g, 1), unit)
                unit = jnp.where(lane >= 112, rows[0], unit)
                for v, start, lo, hi in PIECES[a, block, u]:
                    keep = (spot >= lo) & (spot < hi)
                    for parts, at, ref in zip(open_parts, ats, (first_ref, second_ref)):
                        moved = pltpu.roll(unit, lax.rem(start - at + 256, 128), 1)
                        parts[v] = jnp.where(keep, moved, parts[v]) if v in parts else moved
                        if hi == 32:
                            ref[v] = parts.pop(v)
    for parts, ref in zip(open_parts, (first_ref, second_ref)):
        for v, value in parts.items():
            ref[v] = value


def unpack_units(got_ref, a, block, at, under, put):
    spot = lanes(PACK) % 32
    for u in range(8):
        value = under(u)
        for v, start, lo, hi in PIECES[a, block, u]:
            keep = (spot >= lo - start + at) & (spot < hi - start + at)
            moved = pltpu.roll(got_ref[v], lax.rem(at - start + 256, 128), 1)
            value = jnp.where(keep, moved, value)
        put(u, value)


def first_halo_kernel(got_ref, half_ref):
    for a in range(12):
        for block in range(2):
            def put(u, value):
                half_ref[a, block, u] = value
            unpack_units(got_ref, a, block, low_side(True, WIDTHS[a]),
                         lambda u: jnp.zeros((PACK, 128), jnp.float32), put)


def build_kernel(fields_ref, buoy_ref, lame_ref, mu_ref, v_ref, t_ref, p_ref, outer_ref):
    size = NZ * CX
    zero = jnp.zeros((8, 128), jnp.float32)

    def clear(x, _):
        for ref, f in [(v_ref, f) for f in range(3)] + [(t_ref, f) for f in Z_STRESS]:
            ref[f, x, 0:8, :] = zero
            ref[f, x, 40:48, :] = zero
        return 0

    lax.fori_loop(0, PLANES, clear, 0)
    for a in range(12):
        ref, first = (fields_ref, a * size) if a < 9 else ((buoy_ref, lame_ref, mu_ref)[a - 9], 0)
        for x in range(CX):
            value = ref[pl.ds(first + x, NZ, stride=CX), :]
            if a < 3:
                v_ref[a, x + LOW, 8:8 + NZ, :] = value
            elif a < 9:
                t_ref[a - 3, x + LOW, 8:8 + NZ, :] = value
            else:
                p_ref[a - 9, x + LOW, 0:NZ, :] = DT * value
    give_early(is_odd(), outer_ref, v_ref, t_ref, p_ref)


def halo_kernel(got_ref, half_ref, v_in, t_in, p_in, v_ref, t_ref, p_ref, outer_ref, inner_ref):
    odd = is_odd()
    v_rows = v_ref.reshape(3 * PLANES * ZROWS, 128)
    t_rows = t_ref.reshape(6 * PLANES * ZROWS, 128)
    p_rows = p_ref.reshape(3 * PLANES * DEPTH, 128)

    def one(a, f, rows_ref, depth, begin, scale):
        for block in range(2):
            def put(u, value):
                row = (f * PLANES + LOW + 8 * block) * depth + begin + u
                rows_ref[pl.ds(row, 8, stride=depth), :] = scale * value if scale else value
            unpack_units(got_ref, a, block, low_side(False, WIDTHS[a]),
                         lambda u: half_ref[a, block, u], put)

    for a in range(12):
        if a < 3:
            one(a, a, v_rows, ZROWS, 56, None)
        elif a < 9:
            one(a, a - 3, t_rows, ZROWS, 56, None)
        else:
            one(a, a - 9, p_rows, DEPTH, NZ, DT)
    give_late(odd, outer_ref, v_ref, t_ref, p_ref)
    give_halo(INNER_FIRST, odd, True, inner_ref, v_ref, t_ref, p_ref)


def pad_own(v_ref, t_ref):
    def pads(x, _):
        for f in range(3):
            pad_halo(v_ref, f, x)
        for f in Z_STRESS:
            pad_halo(t_ref, f, x)
        return 0

    lax.fori_loop(LOW, LOW + CX, pads, 0, unroll=4)


def near_step(items, back, odd, read, v_ref, t_ref, p_ref, band_ref, d_ref):
    take_halo(items, odd, True, read, v_ref, t_ref, p_ref)
    mats = (v_ref, t_ref, p_ref, band_ref, d_ref)
    velocity_pass(*mats, jnp.where(odd, -2, back + 1), jnp.where(odd, -1, back + 2), CX - back)
    stress_pass(*mats, jnp.where(odd, 0, back + 3), CX - 3 - back)


def near_kernel(items, back, gots, gives, band_ref, *refs):
    got_refs, refs = refs[:gots], refs[gots + 3:]
    v_ref, t_ref, p_ref = refs[:3]
    send_refs, d_ref = refs[3:3 + gives], refs[-1]
    odd = is_odd()
    if items is INNER_FIRST:
        pad_own(v_ref, t_ref)

    def read(n):
        part = plane_count(INNER[:4])
        return got_refs[0][n] if gots == 1 or n < part else got_refs[1][n - part]

    near_step(items, back, odd, read, v_ref, t_ref, p_ref, band_ref, d_ref)
    if gives == 1:
        give_halo(INNER, odd, True, send_refs[0], v_ref, t_ref, p_ref)
    else:
        give_halo(INNER[:4], odd, True, send_refs[0], v_ref, t_ref, p_ref)
        give_halo(INNER[4:], odd, True, send_refs[1], v_ref, t_ref, p_ref)


def stress_half(first, t_ref, out_ref, rows_ref, sem):
    flat = rows_ref.reshape(6 * NZ * 8, 128)

    def body(r, _):
        for f in range(6):
            flat[pl.ds(f * NZ * 8 + r, NZ, stride=8), :] = t_ref[f, first + r + LOW, 8:8 + NZ, :]
        return 0

    lax.fori_loop(0, 8, body, 0, unroll=2)
    copy = pltpu.make_async_copy(
        rows_ref, out_ref.at[pl.ds(3 * NZ, 6 * NZ), pl.ds(pl.multiple_of(first, 8), 8)], sem)
    copy.start()
    return copy


def last_near_kernel(influence_ref, count_ref, profile_ref, band_ref, got_ref, v_in, t_in,
                     p_in, v_ref, t_ref, p_ref, out_ref, used_ref, profile_rows, d_ref, rows_ref, sem):
    odd = is_odd()
    near_step(INNER, 3, odd, lambda n: got_ref[n], v_ref, t_ref, p_ref, band_ref, d_ref)
    copy = stress_half(jnp.where(odd, 0, 8), t_ref, out_ref, rows_ref, sem)
    lane = lanes(8)
    column = lax.broadcasted_iota(jnp.int32, (8, 128), 0) + lax.axis_index("tile") - 1
    slot_id = (lane // S * 32 + column) * S + lane % S
    slot_id = jnp.where((column >= 0) & (column < 32), slot_id, -1)
    used = jnp.zeros((8, 128), jnp.int32)
    for k in range(LIST):
        hit = (slot_id == influence_ref[0, k]) & (k < count_ref[0])
        used = jnp.where(hit, 1, used)
    used_ref[...] = used
    for c in range(3):
        for z in range(NZ):
            profile_rows[c, z:z + 1, :] = jnp.full((1, 128), profile_ref[c, z], jnp.float32)
    copy.wait()


def far_steps(items, last, odd, read, v_ref, t_ref, p_ref, band_ref, d_ref):
    take_halo(items, odd, False, read, v_ref, t_ref, p_ref)
    mats = (v_ref, t_ref, p_ref, band_ref, d_ref)
    velocity_pass(*mats, jnp.where(odd, 14, -5), jnp.where(odd, 15, -4), 6)
    stress_pass(*mats, jnp.where(odd, 13, -3), 6)
    velocity_pass(*mats, jnp.where(odd, 11, -2), jnp.where(odd, 12, -1), 6)
    if not last:
        stress_pass(*mats, jnp.where(odd, 10, 0), 6)


def far_kernel(band_ref, got_own, got_halo, v_in, t_in, p_in, v_ref, t_ref, p_ref,
               outer_ref, d_ref):
    odd = is_odd()
    far_steps(OUTER_FIRST, False, odd, read_first(got_own, got_halo), v_ref, t_ref, p_ref, band_ref, d_ref)
    give_second(odd, outer_ref, v_ref, t_ref, p_ref)


def station_kernel(count_ref, observed_ref, gain_ref, cell_ref, band_ref,
                   got_ref, v_in, t_in, p_in, v_ref, t_ref, p_ref, packet_ref, d_ref, slot_ref):
    odd = is_odd()
    far_steps(OUTER, True, odd, read_second(got_ref), v_ref, t_ref, p_ref, band_ref, d_ref)
    slot_ref[...] = jnp.zeros((16, 128), jnp.float32)
    slot_ref[0:3, 0:S] = observed_ref[...]
    slot_ref[3:4, 0:S] = gain_ref[...]
    slot_ref[4:5, 0:S] = cell_ref[...].astype(jnp.float32)
    cell = slot_ref[4:5, :].astype(jnp.int32)
    cell_x, cell_y = cell // CY, cell % CY
    pick_y = (lax.broadcasted_iota(jnp.int32, (CY, 128), 0) == cell_y).astype(jnp.float32)
    pick_x = lax.broadcasted_iota(jnp.int32, (CX, 128), 0) == cell_x
    live = lanes(1) < count_ref[0]
    gain = slot_ref[3:4, :]
    region, tile = lax.axis_index("region"), lax.axis_index("tile")
    surface = jnp.concatenate(
        [v_ref[c, r + LOW, 8:9, :] for c in range(3) for r in range(CX)], axis=0)
    rows = jnp.dot(surface, pick_y, precision=lax.Precision.HIGHEST,
                   preferred_element_type=jnp.float32)
    for c in range(3):
        picked = jnp.where(pick_x, rows[c * CX:(c + 1) * CX], 0.0)
        sample = jnp.sum(picked, axis=0, keepdims=True)
        slot_ref[8 + c:9 + c, :] = jnp.where(live, gain * (slot_ref[c:c + 1, :] - sample), 0.0)
    slot_ref[11:12, :] = (region * CX + cell_x).astype(jnp.float32)
    slot_ref[12:13, :] = (tile * CY + cell_y).astype(jnp.float32)
    own = jnp.where(lanes(8) < S, slot_ref[8:16, :], 0.0)
    packet_ref[...] = pltpu.roll(own, region * S, 1)


def tile_column(packet_refs, used, cell_x, cell_y):
    packet = packet_refs[0] + packet_refs[1] + packet_refs[2] + packet_refs[3]
    dist_x = cell_x - packet[3:4]
    dist_y = cell_y - packet[4:5]
    along_x = jnp.exp(-(dist_x * dist_x) / (2.0 * (0.5 * CX) ** 2))
    along_y = jnp.exp(-(dist_y * dist_y) / (2.0 * (0.25 * CY) ** 2))
    scaled = jnp.concatenate(
        [jnp.where(used > 0, packet[c:c + 1] * along_x, 0.0) for c in range(3)], axis=0)
    return lax.dot_general(
        scaled, along_y, (((1,), (1,)), ((), ())), precision=lax.Precision.HIGHEST,
        preferred_element_type=jnp.float32)


def cell_places():
    region, tile = lax.axis_index("region"), lax.axis_index("tile")
    cell_x = (lax.broadcasted_iota(jnp.int32, (CX, 128), 0) + region * CX).astype(jnp.float32)
    cell_y = (lax.broadcasted_iota(jnp.int32, (CY, 128), 0) + tile * CY).astype(jnp.float32)
    return cell_x, cell_y


def stress_out_kernel(band_ref, here_ref, used_ref, v_ref, t_in, p_ref, out_in, t_ref,
                      out_ref, own_part, d_ref, rows_ref, sem):
    odd = is_odd()
    stress_pass(v_ref, t_ref, p_ref, band_ref, d_ref, jnp.where(odd, 10, 0), 6, pads=False)
    copy = stress_half(jnp.where(odd, 8, 0), t_ref, out_ref, rows_ref, sem)
    own_part[...] = tile_column(here_ref, used_ref[1:2], *cell_places())
    copy.wait()


def increment_kernel(v_ref, first_ref, second_ref, used_ref, profile_rows, own_part, out_in, out_ref,
                     rows_ref, sems):
    odd = lax.rem(lax.axis_index("tile"), 2) > 0
    before = [jnp.where(odd, first_ref[r], second_ref[r]) for r in range(4)]
    after = [jnp.where(odd, second_ref[r], first_ref[r]) for r in range(4)]
    places = cell_places()
    increment = (own_part[...] + tile_column(before, used_ref[0:1], *places)
                 + tile_column(after, used_ref[2:3], *places))
    flat = rows_ref.reshape(3 * NZ * CX, 128)
    copies = []
    for c in range(3):
        for r in range(CX):
            value = v_ref[c, r + LOW, 8:8 + NZ, :]
            value = value + profile_rows[c] * increment[c * CX + r:c * CX + r + 1, :]
            flat[pl.ds(c * NZ * CX + r, NZ, stride=CX), :] = value
        part = pl.ds(c * NZ, NZ)
        copies.append(pltpu.make_async_copy(rows_ref.at[part], out_ref.at[part], sems.at[c]))
        copies[c].start()
    for copy in copies:
        copy.wait()


def struct(*shape):
    return jax.ShapeDtypeStruct(shape, jnp.float32)


VM = pl.BlockSpec(memory_space=pltpu.VMEM)
SM = pl.BlockSpec(memory_space=pltpu.SMEM)
HB = pl.BlockSpec(memory_space=pltpu.HBM)


def call(kernel, outs, specs, scratch, out_specs=None, aliases=None, vmem=VMEM_BYTES,
         cost=None):
    return pl.pallas_call(
        kernel, out_shape=outs, in_specs=specs, out_specs=out_specs or [VM] * len(outs),
        scratch_shapes=list(scratch), input_output_aliases=aliases or {}, cost_estimate=cost,
        compiler_params=pltpu.CompilerParams(vmem_limit_bytes=vmem))


def pairs(first):
    return [p for i in range(first, 31, 2) for p in ((i, i + 1), (i + 1, i))]


INNER_SWAP = [(0, 1), (1, 0), (2, 3), (3, 2)]
OUTER_SWAP = [(1, 2), (2, 1)]


FREE = pl.CostEstimate(flops=1024, bytes_accessed=1024, transcendentals=0)


def bind(kernel, *first):
    def bound(*refs):
        return kernel(*first, *refs)
    return bound


def per_device(fields, buoyancy, lame_first, shear_modulus, observed, station_weight, depth_profile,
               station_cell, station_count, influence, influence_count):
    band = jnp.asarray(band_matrices(), jnp.bfloat16)
    size = NZ * CX
    state = (struct(3, PLANES, ZROWS, 128), struct(6, PLANES, ZROWS, 128),
             struct(3, PLANES, DEPTH, 128))
    given = (fields.reshape(9 * size, CY), buoyancy.reshape(size, CY),
             lame_first.reshape(size, CY), shear_modulus.reshape(size, CY))
    fetched = [pltpu.VMEM((12 * size, 128), jnp.float32), pltpu.SemaphoreType.DMA((12,))]
    packed, edges = struct(VECTORS, PACK, 128), struct(12, 2, 8, 8, 128)
    first, second = call(edge_kernel, (packed, packed), [HB] * 4, fetched,
                         vmem=62 * 2 ** 20)(*given)
    got_first = lax.ppermute(first, "tile", pairs(0))
    got_second = lax.ppermute(second, "tile", pairs(1))
    early, planes = plane_count(OUTER_FIRST[:EARLY_FIELDS]), plane_count(OUTER_FIRST)
    v, t, p, outer = call(build_kernel, state + (struct(early, NZ, 128),), [VM] * 4, [],
                          cost=pl.CostEstimate(flops=0, bytes_accessed=10 ** 8, transcendentals=0))(
        *given)
    got_own = lax.ppermute(outer, "region", OUTER_SWAP)
    half, = call(first_halo_kernel, (edges,), [VM], [])(got_first)
    v, t, p, outer, inner = call(
        halo_kernel, state + (struct(planes + 4 * (planes - early), PACK, 128),
                              struct(plane_count(INNER_FIRST), DEPTH, 128)),
        [VM] * 5, [], aliases={2: 0, 3: 1, 4: 2},
    )(got_second, half, v, t, p)
    inner_struct = struct(plane_count(INNER), DEPTH, 128)
    d_scratch = pltpu.VMEM((3, CX, DEPTH, 128), jnp.float32)
    alias = {2: 0, 3: 1, 4: 2}
    result = struct(9 * NZ, CX, 128)
    for block in range(2):
        got = lax.ppermute(inner, "region", INNER_SWAP)
        got_outer = lax.ppermute(outer, "region", OUTER_SWAP)
        split = 2 if block == 0 else 1
        parts = (INNER[:4], INNER[4:]) if block == 0 else (INNER,)
        v, t, p, *inner = call(
            bind(near_kernel, INNER_FIRST if block == 0 else INNER, 0, 1, split),
            state + tuple(struct(plane_count(part), DEPTH, 128) for part in parts), [VM] * 5,
            [d_scratch], aliases=alias, cost=FREE,
        )(band, got, v, t, p)
        got = [lax.ppermute(part, "region", INNER_SWAP) for part in inner]
        if block == 0:
            v, t, p, inner = call(
                bind(near_kernel, INNER, 3, 2, 1), state + (inner_struct,), [VM] * 6,
                [d_scratch], aliases={3: 0, 4: 1, 5: 2}, cost=FREE,
            )(band, *got, v, t, p)
            v, t, p, outer = call(
                far_kernel, state + (struct(4 * plane_count(OUTER) + plane_count(OUTER) // 2, 8, 128),),
                [VM] * 6, [d_scratch], aliases={3: 0, 4: 1, 5: 2},
            )(band, got_own, got_outer, v, t, p)
        else:
            v, t, p, out, used, profile_rows = call(
                last_near_kernel,
                state + (result, jax.ShapeDtypeStruct((8, 128), jnp.int32), struct(3, NZ, 128)),
                [SM] * 3 + [VM] * 5,
                [d_scratch, pltpu.VMEM((6 * NZ, 8, 128), jnp.float32), pltpu.SemaphoreType.DMA],
                out_specs=[VM] * 3 + [HB] + [VM] * 2, aliases={5: 0, 6: 1, 7: 2},
            )(influence, influence_count, depth_profile, band, *got, v, t, p)
    v, t, p, packet = call(
        station_kernel, state + (struct(8, 128),), [SM] + [VM] * 8,
        [d_scratch, pltpu.VMEM((16, 128), jnp.float32)], aliases={6: 0, 7: 1, 8: 2},
    )(station_count, observed, station_weight.reshape(1, S), station_cell.reshape(1, S),
      band, got_outer, v, t, p)
    here = lax.all_gather(packet, "region")
    got_first = lax.ppermute(here, "tile", pairs(0))
    got_second = lax.ppermute(here, "tile", pairs(1))
    _, out, own_part = call(
        stress_out_kernel, (state[1], result, struct(3 * CX, CY)), [VM] * 6 + [HB],
        [d_scratch, pltpu.VMEM((6 * NZ, 8, 128), jnp.float32), pltpu.SemaphoreType.DMA],
        out_specs=[VM, HB, VM], aliases={4: 0, 6: 1},
    )(band, here, used, v, t, p, out)
    out, = call(
        increment_kernel, (result,), [VM] * 6 + [HB],
        [pltpu.VMEM((3 * NZ, CX, 128), jnp.float32), pltpu.SemaphoreType.DMA((3,))],
        out_specs=[HB], aliases={6: 0},
    )(v, got_first, got_second, used, profile_rows, own_part, out)
    return out.reshape(9, NZ, CX, CY)


def solution(mesh):
    in_specs = (
        P(None, None, "region", "tile"),
        P(None, "region", "tile"),
        P(None, "region", "tile"),
        P(None, "region", "tile"),
        P(None, ("region", "tile")),
        P(("region", "tile")),
        P(),
        P(("region", "tile")),
        P(("region", "tile")),
        P(("region", "tile"), None),
        P(("region", "tile")),
    )
    out_specs = P(None, None, "region", "tile")
    return jax.shard_map(
        per_device, mesh=mesh, in_specs=in_specs, out_specs=out_specs, check_vma=False
    )
```
